32 devices in a mesh: gx: 4 (over y, x), gy: 8 (over z, core).
Axes of the slice: x: 2, y: 2, z: 4, core: 2. Of those that a mesh axis runs over, the one named last changes fastest.
Arguments:
- right_side: float32 [32, 64, 256], P('gx', 'gy'), may hold values from -6 to 6
- coefficient: float32 [32, 64, 256], P('gx', 'gy'), may hold values from 0.5 to 4
Outputs:
- solution_field: float32 [32, 64, 256], P('gx', 'gy')
The draws below stay inside these ranges and needn't reach their ends.
All inputs are finite; a program needn't handle non-finite values.
Results may differ from the reference program's by a relative error of at most 0.000078.
Values sent between devices are 32-bit elements; how exact they have to be, the bound alone decides.
No kernel may reach another device: no remote copies, remote signals or barrier semaphores. Data moves between devices by JAX's collectives and lax.ppermute only.
A program may use at most 64 MiB of HBM per device.

```python
import math
import jax
import jax.numpy as jnp
from jax import lax

NZ = 256
LEVELS = 3
SMOOTH = 2
COARSE_STEPS = 6
NX = 32
NY = 64


def draw_right_side(key, part):
    rough_part = jax.random.normal(key, (NX, NY, NZ), jnp.float32)
    return jnp.clip(rough_part, -6.0, 6.0)


def level_of(rng, shape, pieces, smallest, top_value):
    def one(position, blocks):
        steps = jax.random.uniform(jax.random.fold_in(jax.random.fold_in(rng, 6), position), (blocks,), jnp.float32, smallest / len(pieces), top_value / len(pieces))
        return jnp.repeat(jnp.exp(steps), shape[position] // blocks).reshape((-1,) + (1,) * (len(shape) - position - 1))

    loudness = one(*pieces[0])
    for cut in pieces[1:]:
        loudness = loudness * one(*cut)
    return loudness


def setup_inputs(seed: int = 0) -> dict:
    seeds = jax.random.split(jax.random.key(seed), 3)
    return {
        "right_side": draw_right_side(jax.random.fold_in(seeds[2], 71), 0),
        "coefficient": jnp.clip(jnp.exp(math.log(4.0) - 2.0794415 * jax.random.uniform(seeds[1], (NX, NY, NZ), jnp.float32) ** level_of(seeds[1], (NX, NY, NZ), ((0, 4), (1, 8)), -0.2, 0.2)), 0.5, 4.0),
    }


SMOOTH_LOW = 0.5
SMOOTH_HIGH = 2.0
COARSE_LOW = 0.05
COARSE_HIGH = 2.0


def chebyshev(low_end, high_end, sweeps):
    middle = 0.5 * (high_end + low_end)
    half_span = 0.5 * (high_end - low_end)
    sig_ratio = middle / half_span
    rho_now = 1.0 / sig_ratio
    coeff_pairs = []
    for sweep_num in range(1, sweeps):
        rho_next = 1.0 / (2.0 * sig_ratio - rho_now)
        coeff_pairs.append((rho_next * rho_now, 2.0 * rho_next / half_span))
        rho_now = rho_next
    return 1.0 / middle, coeff_pairs


def neighbours(padded):
    return [padded[2:, 1:-1, 1:-1], padded[:-2, 1:-1, 1:-1], padded[1:-1, 2:, 1:-1],
            padded[1:-1, :-2, 1:-1], padded[1:-1, 1:-1, 2:], padded[1:-1, 1:-1, :-2]]


def face_weights(padded):
    centre = padded[1:-1, 1:-1, 1:-1]
    weights = [0.5 * (centre + beside_cell) for beside_cell in neighbours(padded)]
    diagonal = weights[0] + weights[1] + weights[2] + weights[3] + weights[4] + weights[5]
    return weights, diagonal


def apply_operator(padded, weights, diagonal):
    beside_list = neighbours(padded)
    summed = weights[0] * beside_list[0]
    for face_num in range(1, 6):
        summed = summed + weights[face_num] * beside_list[face_num]
    return diagonal * padded[1:-1, 1:-1, 1:-1] - summed


def restrict_sum(field):
    field = field[0::2] + field[1::2]
    field = field[:, 0::2] + field[:, 1::2]
    return field[:, :, 0::2] + field[:, :, 1::2]


def prolong_axis(padded, axis_num):
    length = padded.shape[axis_num] - 2
    centre = lax.slice_in_dim(padded, 1, length + 1, axis=axis_num)
    before = lax.slice_in_dim(padded, 0, length, axis=axis_num)
    following = lax.slice_in_dim(padded, 2, length + 2, axis=axis_num)
    even_part = 0.75 * centre + 0.25 * before
    odd_part = 0.75 * centre + 0.25 * following
    joined = jnp.stack([even_part, odd_part], axis=axis_num + 1)
    new_shape = list(centre.shape)
    new_shape[axis_num] = 2 * length
    return joined.reshape(new_shape)


def prolong_whole(coarse):
    padded = jnp.pad(coarse, 1)
    for axis_num in range(3):
        padded = prolong_axis(padded, axis_num)
    return padded


def residual_whole(iterate, source, weights, diagonal):
    return source - apply_operator(jnp.pad(iterate, 1), weights, diagonal)


def smooth_whole(iterate, source, weights, diagonal, low_end, high_end, sweeps):
    inverse = 1.0 / diagonal
    inv_mid, coeff_pairs = chebyshev(low_end, high_end, sweeps)
    residue = source if iterate is None else residual_whole(iterate, source, weights, diagonal)
    step_dir = residue * inverse * inv_mid
    iterate = step_dir if iterate is None else iterate + step_dir
    for keep_part, push_part in coeff_pairs:
        residue = residual_whole(iterate, source, weights, diagonal)
        step_dir = keep_part * step_dir + push_part * (residue * inverse)
        iterate = iterate + step_dir
    return iterate


def reference(right_side, coefficient):
    source = right_side
    coeffs = coefficient
    stored = []
    for level_num in range(LEVELS - 1):
        weights, diagonal = face_weights(jnp.pad(coeffs, 1))
        iterate = smooth_whole(None, source, weights, diagonal, SMOOTH_LOW, SMOOTH_HIGH, SMOOTH)
        residue = residual_whole(iterate, source, weights, diagonal)
        stored.append((iterate, source, weights, diagonal))
        source = 0.5 * restrict_sum(residue)
        coeffs = 0.125 * restrict_sum(coeffs)
    weights, diagonal = face_weights(jnp.pad(coeffs, 1))
    coarse = smooth_whole(None, source, weights, diagonal, COARSE_LOW, COARSE_HIGH, COARSE_STEPS)
    residue = residual_whole(coarse, source, weights, diagonal)
    ones_image = apply_operator(jnp.pad(jnp.ones_like(source), 1), weights, diagonal)
    coarse = coarse + jnp.sum(residue) / jnp.sum(ones_image)
    for iterate, source, weights, diagonal in reversed(stored):
        iterate = iterate + prolong_whole(coarse)
        coarse = smooth_whole(iterate, source, weights, diagonal, SMOOTH_LOW, SMOOTH_HIGH, SMOOTH)
    return coarse
```

```python
import functools

import jax
import jax.numpy as jnp
from jax import lax
from jax.experimental import pallas as pl
from jax.experimental.pallas import tpu as pltpu
from jax.sharding import PartitionSpec as P

SMOOTH = 2
COARSE_STEPS = 6
SMOOTH_LOW = 0.5
SMOOTH_HIGH = 2.0
COARSE_LOW = 0.05
COARSE_HIGH = 2.0

DEEP_F = 2 * SMOOTH - 1
DEEP_C = 2 * SMOOTH
SUB = 8
PAD = 4
WRITTEN_OUT = 512

VMEM = pl.BlockSpec(memory_space=pltpu.VMEM)
F32 = jnp.float32


def chebyshev(low_end, high_end, sweeps):
    middle = 0.5 * (high_end + low_end)
    half_span = 0.5 * (high_end - low_end)
    sig_ratio = middle / half_span
    rho_now = 1.0 / sig_ratio
    coeff_pairs = []
    for sweep_num in range(1, sweeps):
        rho_next = 1.0 / (2.0 * sig_ratio - rho_now)
        coeff_pairs.append((rho_next * rho_now, 2.0 * rho_next / half_span))
        rho_now = rho_next
    return (1.0 / middle, coeff_pairs)


def each(count, registers, step):
    if count * registers <= WRITTEN_OUT:
        for i in range(count):
            step(i)
    else:

        def one(i, carry):
            step(i)
            return carry

        lax.fori_loop(0, count, one, 0)


def turn(value, amount, axis):
    return pltpu.roll(value, amount % value.shape[axis], axis)


def iota(shape, axis):
    return lax.broadcasted_iota(jnp.int32, shape, axis)


def beside(v, below, above, w_below, w_above, w_cols, w_depth, stride=1):
    out = w_above * above + w_below * below
    out = out + w_cols * turn(v, -1, 0)
    out = out + w_depth * turn(v, -stride, 1)
    return out + turn(w_cols * v, 1, 0) + turn(w_depth * v, stride, 1)


def exact_dot(a, b):
    return jnp.dot(a, b, precision=lax.Precision.HIGHEST, preferred_element_type=F32)


def call(kernel, out_shapes, scratch, args, limit):
    return pl.pallas_call(
        kernel,
        out_shape=[jax.ShapeDtypeStruct(s, F32) for s in out_shapes],
        in_specs=[VMEM] * len(args),
        out_specs=[VMEM] * len(out_shapes),
        scratch_shapes=[pltpu.VMEM(s, F32) for s in scratch],
        compiler_params=pltpu.CompilerParams(vmem_limit_bytes=limit),
    )(*args)


def pack_rows(f_ref, c_ref, a_ref, b_ref):
    rows = f_ref.shape[0]
    odd = lax.rem(lax.axis_index("gx"), 2)
    for ref, at_end in ((a_ref, 1 - odd), (b_ref, odd)):
        ref[0:DEEP_F] = f_ref[pl.ds(at_end * (rows - DEEP_F), DEEP_F)]
        ref[DEEP_F:] = c_ref[pl.ds(at_end * (rows - DEEP_C), DEEP_C)]


def row_sources(along_x, rows, f_ref, c_ref, a_ref, b_ref):
    gx = lax.axis_index("gx")
    odd = lax.rem(gx, 2) == 1
    has_before = (gx > 0).astype(F32)
    has_after = (gx < along_x - 1).astype(F32)

    def before(i):
        return jnp.where(odd, a_ref[i], b_ref[i]) * has_before

    def after(i):
        return jnp.where(odd, b_ref[i], a_ref[i]) * has_after

    def f_row(i):
        if i < 0:
            return before(DEEP_F + i)
        return f_ref[i] if i < rows else after(i - rows)

    def c_row(i):
        if i < 0:
            return before(DEEP_F + DEEP_C + i)
        return c_ref[i] if i < rows else after(DEEP_F + i - rows)

    return f_row, c_row


def pack_cols(along_x, f_ref, c_ref, a_ref, b_ref, z_ref, k_ref):
    rows = f_ref.shape[0]
    f_row, c_row = row_sources(along_x, rows, f_ref, c_ref, a_ref, b_ref)
    odd = lax.rem(lax.axis_index("gy"), 2) == 1
    low_half = iota(f_ref.shape[1:], 0) < DEEP_C
    for t in range(rows + 2 * DEEP_F):
        f, c = f_row(t - DEEP_F), c_row(t - DEEP_F)
        first = jnp.where(low_half, c, turn(f, DEEP_C, 0))
        last = jnp.where(low_half, turn(c, DEEP_C, 0), f)
        z_ref[t] = jnp.where(odd, last, first)
        k_ref[t] = jnp.where(odd, first, last)


def fine_down(
    along_x, along_y, copies,
    f_ref, c_ref, a_ref, b_ref, z_ref, k_ref,
    send_ref, u_ref, fx_ref, wx_ref, wy_ref, wz_ref, diag_ref, inv_ref,
    cx_ref, v_ref, r_ref,
):
    rows, cols, depth = f_ref.shape
    f_row, c_row = row_sources(along_x, rows, f_ref, c_ref, a_ref, b_ref)
    gx, gy = lax.axis_index("gx"), lax.axis_index("gy")
    odd = lax.rem(gy, 2) == 1
    has_left = (gy > 0).astype(F32)
    has_right = (gy < along_y - 1).astype(F32)
    low_half = iota((cols, depth), 0) < DEEP_C
    wide = (cols + 2 * DEEP_C, depth)
    lane = iota(wide, 1)
    col = iota(wide, 0)
    col_inside = ((col >= DEEP_C) | (gy > 0)) & (
        (col < DEEP_C + cols) | (gy < along_y - 1)
    )
    inv_mid, ((keep, push),) = chebyshev(SMOOTH_LOW, SMOOTH_HIGH, SMOOTH)

    for t in range(rows + 2 * DEEP_C):
        row = t - DEEP_C
        c = c_row(row)
        turned = turn(c, DEEP_C, 0)
        s = row + DEEP_F
        if 0 <= s < rows + 2 * DEEP_F:
            left = jnp.where(odd, k_ref[s], z_ref[s]) * has_left
            right = jnp.where(odd, z_ref[s], k_ref[s]) * has_right
            f = f_row(row)
            fx_ref[s, 0:cols] = turn(jnp.where(low_half, f, left), DEEP_C, 0)
            fx_ref[s, cols:] = jnp.where(low_half, turn(f, DEEP_C, 0), right)
        else:
            left = right = jnp.zeros_like(c)
        cx_ref[t, 0:cols] = jnp.where(low_half, left, turned)
        cx_ref[t, cols:] = jnp.where(low_half, turned, turn(right, DEEP_C, 0))

    tall = rows + 2 * DEEP_F
    wx_ref[0] = 0.5 * (cx_ref[0] + cx_ref[1])
    for s in range(tall):
        c = cx_ref[s + 1]
        half = 0.5 * c
        above = half + 0.5 * cx_ref[s + 2]
        wx_ref[s + 1] = above
        w_cols = half + turn(half, -1, 0)
        w_depth = jnp.where(lane == depth - 1, 0.0, half + turn(half, -1, 1))
        edge = jnp.where((lane == 0) | (lane == depth - 1), half, 0.0)
        diag = wx_ref[s] + above + w_cols + turn(w_cols, 1, 0)
        diag = diag + w_depth + turn(w_depth, 1, 1) + edge
        inside = col_inside
        if s < DEEP_F:
            inside = inside & (gx > 0)
        if s >= rows + DEEP_F:
            inside = inside & (gx < along_x - 1)
        inv = jnp.where(inside, 1.0 / diag, 0.0)
        wy_ref[s] = w_cols
        wz_ref[s] = w_depth
        diag_ref[s] = diag
        inv_ref[s] = inv
        v_ref[s] = fx_ref[s] * inv * inv_mid

    def residual(x_ref, shift, s):
        x = x_ref[s - shift]
        total = beside(
            x, x_ref[s - shift - 1], x_ref[s - shift + 1],
            wx_ref[s], wx_ref[s + 1], wy_ref[s], wz_ref[s],
        )
        return x, fx_ref[s] - (diag_ref[s] * x - total)

    for s in range(1, tall - 1):
        v, r = residual(v_ref, 0, s)
        u_ref[s - 1] = v + (keep * v + push * (r * inv_ref[s]))
    for i in range(rows):
        _, r_ref[i] = residual(u_ref, 1, i + DEEP_F)

    half_rows = rows // 2
    summed = [r_ref[2 * i] + r_ref[2 * i + 1] for i in range(half_rows)]
    summed += [c_ref[2 * i] + c_ref[2 * i + 1] for i in range(half_rows)]
    summed = jnp.concatenate(summed, axis=0)
    pairs = (depth, depth // 2)
    thin = exact_dot(summed, (iota(pairs, 0) // 2 == iota(pairs, 1)).astype(F32))
    choice = (SUB * half_rows, summed.shape[0])
    line, source = iota(choice, 0), iota(choice, 1)
    block, place = line // SUB, line % SUB
    half_cols = cols // 2
    f_half = (place >= half_cols) == odd
    place = place % half_cols
    f_from = wide[0] * block + DEEP_C + 2 * place
    c_from = wide[0] * half_rows + cols * block + 2 * place
    from_f = (source == f_from) | (source == f_from + 1)
    from_c = (source == c_from) | (source == c_from + 1)
    picker = jnp.where(f_half, jnp.where(from_f, 0.5, 0.0), jnp.where(from_c, 0.125, 0.0))
    tile = exact_dot(picker, thin).reshape(half_rows, SUB, depth // 2)

    def put(i):
        send_ref[pl.ds(i * half_rows, half_rows)] = tile

    each(copies, half_rows, put)


def coarse_and_up(
    along_x, along_y,
    own_ref, other_ref, u0_ref, fx_ref, wx0_ref, wy0_ref, wz0_ref, diag0_ref, inv0_ref,
    out_ref,
    f_ref, c_ref, wx_ref, wy_ref, wz_ref, diag_ref, inv_ref, v_ref,
    f2_ref, c2_ref, wx2_ref, wy2_ref, wz2_ref, diag2_ref, inv2_ref, d2_ref, e2_ref, e3_ref,
    py_ref, vw_ref, dw_ref, vx_ref, e1_ref, yy_ref, v0_ref, d0_ref, x0_ref, o_ref,
):
    gx, gy = lax.axis_index("gx"), lax.axis_index("gy")
    odd = lax.rem(gy, 2) == 1
    brick1 = own_ref.shape[0] // (along_x * (along_y // 2))
    rows1, cols1, depth1 = f_ref.shape[0] - 2 * PAD, f_ref.shape[1], f_ref.shape[2]
    across = cols1 // SUB
    registers1 = across * (depth1 // 128)
    shape1 = (cols1, depth1)
    zero1 = jnp.zeros(shape1, F32)
    inv_mid, ((keep, push),) = chebyshev(SMOOTH_LOW, SMOOTH_HIGH, SMOOTH)

    mine = (iota((SUB, depth1), 0) < SUB // 2) != odd
    c_ref[PAD - 1] = zero1
    c_ref[PAD + rows1] = zero1

    def place(k):
        x, z = k // across, k % across
        for i in range(brick1):
            own, other = own_ref[k * brick1 + i], other_ref[k * brick1 + i]
            row = PAD + x * brick1 + i
            at = z * SUB if isinstance(z, int) else pl.multiple_of(z * SUB, SUB)
            f_ref[row, pl.ds(at, SUB)] = jnp.where(mine, own, other)
            c_ref[row, pl.ds(at, SUB)] = turn(jnp.where(mine, other, own), SUB // 2, 0)

    each(along_x * across, brick1, place)

    wx_ref[PAD] = 0.5 * c_ref[PAD]

    def weigh(c, below, above, shape, stride):
        col, lane = iota(shape, 0), iota(shape, 1)
        half = 0.5 * c
        w_above = half + 0.5 * above
        w_cols = jnp.where(col == shape[0] - 1, 0.0, half + turn(half, -1, 0))
        w_depth = jnp.where(lane >= shape[1] - stride, 0.0, half + turn(half, -stride, 1))
        edge = jnp.where((col == 0) | (col == shape[0] - 1), half, 0.0)
        edge = edge + jnp.where((lane < stride) | (lane >= shape[1] - stride), half, 0.0)
        diag = half + 0.5 * below + w_above + w_cols + turn(w_cols, 1, 0)
        diag = diag + w_depth + turn(w_depth, stride, 1) + edge
        return w_above, w_cols, w_depth, diag

    def weigh1(i):
        row = PAD + i
        w_above, w_cols, w_depth, diag = weigh(
            c_ref[row], c_ref[row - 1], c_ref[row + 1], shape1, 1
        )
        inv = 1.0 / diag
        wx_ref[row + 1] = w_above
        wy_ref[row] = w_cols
        wz_ref[row] = w_depth
        diag_ref[row] = diag
        inv_ref[row] = inv
        v_ref[row] = f_ref[row] * inv * inv_mid

    v_ref[PAD - 1] = zero1
    v_ref[PAD + rows1] = zero1
    each(rows1, registers1, weigh1)

    rows2, cols2 = rows1 // 2, cols1 // 2
    shape2 = (cols2, depth1)
    registers2 = max(registers1 // 2, 1)
    zero2 = jnp.zeros(shape2, F32)
    lane2, col2 = iota(shape2, 1), iota(shape2, 0)
    even2 = lane2 % 2 == 0

    def fold(ref, row):
        half = ref[row, pl.ds(0, cols2, stride=2), :] + ref[row, pl.ds(1, cols2, stride=2), :]
        return half + jnp.where(even2, turn(half, -1, 1), turn(half, 1, 1))

    def restrict_c(k):
        row = PAD + 2 * k
        c2_ref[k + 1] = 0.125 * (fold(c_ref, row) + fold(c_ref, row + 1))

    each(rows2, 2 * registers1, restrict_c)
    u_ref = c_ref

    def residual1(x_ref, at, row):
        x = x_ref[at]
        total = beside(
            x, x_ref[at - 1], x_ref[at + 1],
            wx_ref[row], wx_ref[row + 1], wy_ref[row], wz_ref[row],
        )
        return x, f_ref[row] - (diag_ref[row] * x - total)

    def second1(i):
        row = PAD + i
        v, r = residual1(v_ref, row, row)
        u_ref[row] = v + (keep * v + push * (r * inv_ref[row]))

    each(rows1, registers1, second1)

    def restrict(k):
        row = PAD + 2 * k
        _, first = residual1(u_ref, row, row)
        _, second = residual1(u_ref, row + 1, row + 1)
        v_ref[k] = first + second
        f2_ref[k] = 0.5 * fold(v_ref, k)

    each(rows2, 2 * registers1, restrict)
    c2_ref[0] = zero2
    c2_ref[rows2 + 1] = zero2
    wx2_ref[0] = 0.5 * c2_ref[1]
    for ref in (e2_ref, e3_ref):
        ref[0] = zero2
        ref[rows2 + 1] = zero2
    inv_mid2, pairs2 = chebyshev(COARSE_LOW, COARSE_HIGH, COARSE_STEPS)

    def weigh2(k):
        w_above, w_cols, w_depth, diag = weigh(
            c2_ref[k + 1], c2_ref[k], c2_ref[k + 2], shape2, 2
        )
        inv = 1.0 / diag
        wx2_ref[k + 1] = w_above
        wy2_ref[k] = w_cols
        wz2_ref[k] = w_depth
        diag2_ref[k] = diag
        inv2_ref[k] = inv
        d = f2_ref[k] * inv * inv_mid2
        d2_ref[k] = d
        e2_ref[k + 1] = d

    each(rows2, registers2, weigh2)

    def residual2(e_ref, k):
        e = e_ref[k + 1]
        total = beside(
            e, e_ref[k], e_ref[k + 2], wx2_ref[k], wx2_ref[k + 1], wy2_ref[k], wz2_ref[k], 2
        )
        return e, f2_ref[k] - (diag2_ref[k] * e - total)

    now_ref, next_ref = e2_ref, e3_ref
    for keep2, push2 in pairs2:

        def step2(k):
            e, r = residual2(now_ref, k)
            d = keep2 * d2_ref[k] + push2 * (r * inv2_ref[k])
            d2_ref[k] = d
            next_ref[k + 1] = e + d

        each(rows2, registers2, step2)
        now_ref, next_ref = next_ref, now_ref

    def gather_sums(k, sums):
        _, r = residual2(now_ref, k)
        total = wx2_ref[k] * (k > 0) + wx2_ref[k + 1] * (k < rows2 - 1)
        total = total + wy2_ref[k] + turn(wy2_ref[k], 1, 0)
        total = total + wz2_ref[k] + turn(wz2_ref[k], 2, 1)
        return sums[0] + r, sums[1] + (diag2_ref[k] - total)

    sums = (zero2, zero2)
    if rows2 * registers2 <= WRITTEN_OUT:
        for k in range(rows2):
            sums = gather_sums(k, sums)
    else:
        sums = lax.fori_loop(0, rows2, gather_sums, sums)
    top = jnp.sum(sums[0], axis=(0, 1), keepdims=True)
    bottom = jnp.sum(sums[1], axis=(0, 1), keepdims=True)
    mean = top / bottom

    span = brick1 + 2 * PAD
    start = gx * brick1 - PAD
    coarse_span = span // 2 + 2
    for k in range(coarse_span):
        row = lax.div(gx * brick1, 2) - PAD // 2 - 1 + k
        good = (row >= 0) & (row < rows2)
        e = now_ref[jnp.clip(row, 0, rows2 - 1) + 1] + mean
        e = jnp.where(good, e, 0.0)
        back = jnp.where(lane2 < 2, 0.0, turn(e, 2, 1))
        ahead = jnp.where(lane2 >= depth1 - 2, 0.0, turn(e, -2, 1))
        e = 0.75 * e + 0.25 * jnp.where(even2, back, ahead)
        back = jnp.where(col2 == 0, 0.0, turn(e, 1, 0))
        ahead = jnp.where(col2 == cols2 - 1, 0.0, turn(e, -1, 0))
        py_ref[k, pl.ds(0, cols2, stride=2), :] = 0.75 * e + 0.25 * back
        py_ref[k, pl.ds(1, cols2, stride=2), :] = 0.75 * e + 0.25 * ahead

    def inside1(m):
        return (start + m >= 0) & (start + m < rows1)

    for m in range(span):
        near = m // 2 + 1
        far = near - 1 if m % 2 == 0 else near + 1
        total = u_ref[PAD + start + m] + (0.75 * py_ref[near] + 0.25 * py_ref[far])
        vw_ref[m] = jnp.where(inside1(m), total, 0.0)
    for m in range(1, span - 1):
        row = PAD + start + m
        v, r = residual1(vw_ref, m, row)
        d = r * inv_ref[row] * inv_mid
        dw_ref[m] = d
        vx_ref[m] = jnp.where(inside1(m), v + d, 0.0)
    margin = SUB
    e1_ref[:, 0:margin, :] = jnp.zeros((span - 4, margin, depth1), F32)
    e1_ref[:, margin + cols1 :, :] = jnp.zeros((span - 4, margin, depth1), F32)
    for m in range(2, span - 2):
        row = PAD + start + m
        v, r = residual1(vx_ref, m, row)
        e = v + (keep * dw_ref[m] + push * (r * inv_ref[row]))
        e1_ref[m - 2, margin : margin + cols1, :] = jnp.where(inside1(m), e, 0.0)

    rows, cols, depth = out_ref.shape
    wide = (cols + 2 * DEEP_C, depth)
    half_wide = wide[0] // 2
    first_col = margin + gy * (cols // 2) - DEEP_C // 2
    for k in range(span - 4):
        e = e1_ref[k, pl.ds(first_col, half_wide), :]
        at = k * wide[0]
        yy_ref[pl.ds(at, half_wide, stride=2), :] = 0.75 * e + 0.25 * turn(e, 1, 0)
        yy_ref[pl.ds(at + 1, half_wide, stride=2), :] = 0.75 * e + 0.25 * turn(e, -1, 0)
    spread = (depth1, depth)
    from_cell, to_cell = iota(spread, 0), iota(spread, 1)
    home = to_cell // 2
    near_cell = jnp.where(to_cell % 2 == 0, home - 1, home + 1)
    weights = jnp.where(from_cell == home, 0.75, 0.0) + jnp.where(from_cell == near_cell, 0.25, 0.0)
    carried = exact_dot(yy_ref[...], weights).reshape(span - 4, wide[0], depth)
    col = iota(wide, 0)
    col_inside = ((col >= DEEP_C) | (gy > 0)) & (
        (col < DEEP_C + cols) | (gy < along_y - 1)
    )
    for s in range(1, rows + 2 * DEEP_F - 1):
        row = s - DEEP_F
        near = row // 2 + 2
        far = near - 1 if row % 2 == 0 else near + 1
        inside = col_inside
        if row < 0:
            inside = inside & (gx > 0)
        if row >= rows:
            inside = inside & (gx < along_x - 1)
        total = u0_ref[s - 1] + (0.75 * carried[near] + 0.25 * carried[far])
        v0_ref[s] = jnp.where(inside, total, 0.0)

    def residual0(x_ref, s):
        x = x_ref[s]
        total = beside(
            x, x_ref[s - 1], x_ref[s + 1],
            wx0_ref[s], wx0_ref[s + 1], wy0_ref[s], wz0_ref[s],
        )
        return x, fx_ref[s] - (diag0_ref[s] * x - total)

    for s in range(2, rows + 2 * DEEP_F - 2):
        v, r = residual0(v0_ref, s)
        d = r * inv0_ref[s] * inv_mid
        d0_ref[s] = d
        x0_ref[s] = v + d
    for i in range(rows):
        s = i + DEEP_F
        v, r = residual0(x0_ref, s)
        o_ref[i] = v + (keep * d0_ref[s] + push * (r * inv0_ref[s]))
    for i in range(rows):
        out_ref[i] = o_ref[i, DEEP_C : DEEP_C + cols, :]


def pairs_from(first, count):
    swaps = []
    for i in range(first, first + count, 2):
        a, b = i % count, (i + 1) % count
        swaps += [(a, b), (b, a)]
    return swaps


def body(right_side, coefficient):
    along_x, along_y = lax.axis_size("gx"), lax.axis_size("gy")
    rows, cols, depth = right_side.shape
    assert cols == 2 * DEEP_C and rows % 4 == 0 and depth % 256 == 0
    assert along_x % 2 == 0 and along_y % 2 == 0
    small = 16 << 20
    strip = (DEEP_F + DEEP_C, cols, depth)
    a, b = call(pack_rows, [strip] * 2, [], (right_side, coefficient), small)
    a = lax.ppermute(a, "gx", pairs_from(0, along_x))
    b = lax.ppermute(b, "gx", pairs_from(1, along_x))

    tall = rows + 2 * DEEP_F
    z, k = call(
        functools.partial(pack_cols, along_x),
        [(tall, cols, depth)] * 2,
        [],
        (right_side, coefficient, a, b),
        small,
    )
    z = lax.ppermute(z, "gy", pairs_from(1, along_y))
    k = lax.ppermute(k, "gy", pairs_from(0, along_y))

    wide = (cols + 2 * DEEP_C, depth)
    half = (rows // 2, SUB, depth // 2)
    copies = along_x * along_y // 2
    send, *state = call(
        functools.partial(fine_down, along_x, along_y, copies),
        [(copies * half[0],) + half[1:], (tall - 2,) + wide, (tall,) + wide, (tall + 1,) + wide]
        + [(tall,) + wide] * 4,
        [(tall + 2,) + wide, (tall,) + wide, (rows,) + wide],
        (right_side, coefficient, a, b, z, k),
        small + 2 * 4 * copies * half[0] * half[1] * half[2],
    )
    flat = along_x * along_y
    groups = [[i for i in range(flat) if i % 2 == core] for core in range(2)]
    own = lax.all_to_all(send, ("gx", "gy"), 0, 0, axis_index_groups=groups, tiled=True)
    other = lax.ppermute(own, "gy", pairs_from(0, along_y))

    rows1, cols1, depth1 = along_x * half[0], along_y * (cols // 2), half[2]
    whole1 = (rows1 + 2 * PAD + 1, cols1, depth1)
    rows2, cols2 = rows1 // 2, cols1 // 2
    whole2 = (rows2 + 2, cols2, depth1)
    span = half[0] + 2 * PAD
    line = (cols1, depth1)
    scratch = [(rows1 + 2 * PAD,) + line] + [whole1] * 7 + [whole2] * 10
    scratch += [(span // 2 + 2,) + line] + [(span,) + line] * 3
    scratch += [(span - 4, cols1 + 2 * SUB, depth1), ((span - 4) * wide[0], depth1)]
    scratch += [(tall,) + wide] * 3 + [(rows,) + wide]
    size = sum(4 * s[0] * s[1] * (s[2] if len(s) == 3 else 1) for s in scratch)
    size += 2 * 4 * own.size + 4 * 8 * tall * wide[0] * wide[1]
    (out,) = call(
        functools.partial(coarse_and_up, along_x, along_y),
        [right_side.shape],
        scratch,
        (own, other, *state),
        size + (12 << 20),
    )
    return out


def solution(mesh):
    placed = (P("gx", "gy", None), P("gx", "gy", None))
    return jax.shard_map(
        body, mesh=mesh, in_specs=placed, out_specs=P("gx", "gy", None), check_vma=False
    )
```

```python
import functools

import jax
import jax.numpy as jnp
from jax import lax
from jax.experimental import pallas as pl
from jax.experimental.pallas import tpu as pltpu
from jax.sharding import PartitionSpec as P

SMOOTH = 2
COARSE_STEPS = 6
SMOOTH_LOW = 0.5
SMOOTH_HIGH = 2.0
COARSE_LOW = 0.05
COARSE_HIGH = 2.0

DEEP_F = 2 * SMOOTH - 1
DEEP_C = 2 * SMOOTH
SUB = 8
PAD = 4
WRITTEN_OUT = 512

VMEM = pl.BlockSpec(memory_space=pltpu.VMEM)
F32 = jnp.float32


def chebyshev(low_end, high_end, sweeps):
    middle = 0.5 * (high_end + low_end)
    half_span = 0.5 * (high_end - low_end)
    sig_ratio = middle / half_span
    rho_now = 1.0 / sig_ratio
    coeff_pairs = []
    for sweep_num in range(1, sweeps):
        rho_next = 1.0 / (2.0 * sig_ratio - rho_now)
        coeff_pairs.append((rho_next * rho_now, 2.0 * rho_next / half_span))
        rho_now = rho_next
    return (1.0 / middle, coeff_pairs)


def each(count, registers, step):
    if count * registers <= WRITTEN_OUT:
        for i in range(count):
            step(i)
    else:

        def one(i, carry):
            step(i)
            return carry

        lax.fori_loop(0, count, one, 0)


def turn(value, amount, axis):
    return pltpu.roll(value, amount % value.shape[axis], axis)


def iota(shape, axis):
    return lax.broadcasted_iota(jnp.int32, shape, axis)


def beside(v, below, above, w_below, w_above, w_cols, w_depth, stride=1):
    out = w_above * above + w_below * below
    out = out + w_cols * turn(v, -1, 0)
    out = out + w_depth * turn(v, -stride, 1)
    return out + turn(w_cols * v, 1, 0) + turn(w_depth * v, stride, 1)


def exact_dot(a, b):
    return jnp.dot(a, b, precision=lax.Precision.HIGHEST, preferred_element_type=F32)


def call(kernel, out_shapes, scratch, args, limit):
    return pl.pallas_call(
        kernel,
        out_shape=[jax.ShapeDtypeStruct(s, F32) for s in out_shapes],
        in_specs=[VMEM] * len(args),
        out_specs=[VMEM] * len(out_shapes),
        scratch_shapes=[pltpu.VMEM(s, F32) for s in scratch],
        compiler_params=pltpu.CompilerParams(vmem_limit_bytes=limit),
    )(*args)


def pack_rows(f_ref, c_ref, a_ref, b_ref, sems):
    rows = f_ref.shape[0]
    odd = lax.rem(lax.axis_index("gx"), 2)
    copies = []
    for ref, at_end in ((a_ref, 1 - odd), (b_ref, odd)):
        for whole_ref, first, count in ((f_ref, 0, DEEP_F), (c_ref, DEEP_F, DEEP_C)):
            copies.append(
                pltpu.make_async_copy(
                    whole_ref.at[pl.ds(at_end * (rows - count), count)],
                    ref.at[pl.ds(first, count)],
                    sems.at[len(copies)],
                )
            )
    for copy in copies:
        copy.start()
    for copy in copies:
        copy.wait()


def row_sources(along_x, rows, f_ref, c_ref, a_ref, b_ref):
    gx = lax.axis_index("gx")
    odd = lax.rem(gx, 2) == 1
    has_before = (gx > 0).astype(F32)
    has_after = (gx < along_x - 1).astype(F32)

    def before(i):
        return jnp.where(odd, a_ref[i], b_ref[i]) * has_before

    def after(i):
        return jnp.where(odd, b_ref[i], a_ref[i]) * has_after

    def f_row(i):
        if i < 0:
            return before(DEEP_F + i)
        return f_ref[i] if i < rows else after(i - rows)

    def c_row(i):
        if i < 0:
            return before(DEEP_F + DEEP_C + i)
        return c_ref[i] if i < rows else after(DEEP_F + i - rows)

    return f_row, c_row


def pack_cols(along_x, f_ref, c_ref, a_ref, b_ref, z_ref, k_ref):
    rows = f_ref.shape[0]
    f_row, c_row = row_sources(along_x, rows, f_ref, c_ref, a_ref, b_ref)
    odd = lax.rem(lax.axis_index("gy"), 2) == 1
    low_half = iota(f_ref.shape[1:], 0) < DEEP_C
    for t in range(rows + 2 * DEEP_F):
        f, c = f_row(t - DEEP_F), c_row(t - DEEP_F)
        first = jnp.where(low_half, c, turn(f, DEEP_C, 0))
        last = jnp.where(low_half, turn(c, DEEP_C, 0), f)
        z_ref[t] = jnp.where(odd, last, first)
        k_ref[t] = jnp.where(odd, first, last)


def fine_down(
    along_x, along_y, copies,
    f_ref, c_ref, a_ref, b_ref, z_ref, k_ref,
    send_ref, u_ref, fx_ref, wx_ref, wy_ref, wz_ref, diag_ref, inv_ref,
    cx_ref, v_ref, r_ref,
):
    rows, cols, depth = f_ref.shape
    f_row, c_row = row_sources(along_x, rows, f_ref, c_ref, a_ref, b_ref)
    gx, gy = lax.axis_index("gx"), lax.axis_index("gy")
    odd = lax.rem(gy, 2) == 1
    has_left = (gy > 0).astype(F32)
    has_right = (gy < along_y - 1).astype(F32)
    low_half = iota((cols, depth), 0) < DEEP_C
    wide = (cols + 2 * DEEP_C, depth)
    lane = iota(wide, 1)
    col = iota(wide, 0)
    col_inside = ((col >= DEEP_C) | (gy > 0)) & (
        (col < DEEP_C + cols) | (gy < along_y - 1)
    )
    inv_mid, ((keep, push),) = chebyshev(SMOOTH_LOW, SMOOTH_HIGH, SMOOTH)

    for t in range(rows + 2 * DEEP_C):
        row = t - DEEP_C
        c = c_row(row)
        turned = turn(c, DEEP_C, 0)
        s = row + DEEP_F
        if 0 <= s < rows + 2 * DEEP_F:
            left = jnp.where(odd, k_ref[s], z_ref[s]) * has_left
            right = jnp.where(odd, z_ref[s], k_ref[s]) * has_right
            f = f_row(row)
            fx_ref[s, 0:cols] = turn(jnp.where(low_half, f, left), DEEP_C, 0)
            fx_ref[s, cols:] = jnp.where(low_half, turn(f, DEEP_C, 0), right)
        else:
            left = right = jnp.zeros_like(c)
        cx_ref[t, 0:cols] = jnp.where(low_half, left, turned)
        cx_ref[t, cols:] = jnp.where(low_half, turned, turn(right, DEEP_C, 0))

    tall = rows + 2 * DEEP_F
    wx_ref[0] = 0.5 * (cx_ref[0] + cx_ref[1])
    for s in range(tall):
        c = cx_ref[s + 1]
        half = 0.5 * c
        above = half + 0.5 * cx_ref[s + 2]
        wx_ref[s + 1] = above
        w_cols = half + turn(half, -1, 0)
        w_depth = jnp.where(lane == depth - 1, 0.0, half + turn(half, -1, 1))
        edge = jnp.where((lane == 0) | (lane == depth - 1), half, 0.0)
        diag = wx_ref[s] + above + w_cols + turn(w_cols, 1, 0)
        diag = diag + w_depth + turn(w_depth, 1, 1) + edge
        inside = col_inside
        if s < DEEP_F:
            inside = inside & (gx > 0)
        if s >= rows + DEEP_F:
            inside = inside & (gx < along_x - 1)
        inv = jnp.where(inside, 1.0 / diag, 0.0)
        wy_ref[s] = w_cols
        wz_ref[s] = w_depth
        diag_ref[s] = diag
        inv_ref[s] = inv
        v_ref[s] = fx_ref[s] * inv * inv_mid

    def residual(x_ref, shift, s):
        x = x_ref[s - shift]
        total = beside(
            x, x_ref[s - shift - 1], x_ref[s - shift + 1],
            wx_ref[s], wx_ref[s + 1], wy_ref[s], wz_ref[s],
        )
        return x, fx_ref[s] - (diag_ref[s] * x - total)

    for s in range(1, tall - 1):
        v, r = residual(v_ref, 0, s)
        u_ref[s - 1] = v + (keep * v + push * (r * inv_ref[s]))
    for i in range(rows):
        _, r_ref[i] = residual(u_ref, 1, i + DEEP_F)

    half_rows = rows // 2
    summed = [r_ref[2 * i] + r_ref[2 * i + 1] for i in range(half_rows)]
    summed += [c_ref[2 * i] + c_ref[2 * i + 1] for i in range(half_rows)]
    summed = jnp.concatenate(summed, axis=0)
    pairs = (depth, depth // 2)
    thin = exact_dot(summed, (iota(pairs, 0) // 2 == iota(pairs, 1)).astype(F32))
    choice = (SUB * half_rows, summed.shape[0])
    line, source = iota(choice, 0), iota(choice, 1)
    block, place = line // SUB, line % SUB
    half_cols = cols // 2
    f_half = (place >= half_cols) == odd
    place = place % half_cols
    f_from = wide[0] * block + DEEP_C + 2 * place
    c_from = wide[0] * half_rows + cols * block + 2 * place
    from_f = (source == f_from) | (source == f_from + 1)
    from_c = (source == c_from) | (source == c_from + 1)
    picker = jnp.where(f_half, jnp.where(from_f, 0.5, 0.0), jnp.where(from_c, 0.125, 0.0))
    tile = exact_dot(picker, thin).reshape(half_rows, SUB, depth // 2)

    def put(i):
        send_ref[pl.ds(i * half_rows, half_rows)] = tile

    each(copies, half_rows, put)


def coarse_and_up(
    along_x, along_y,
    own_ref, other_ref, u0_ref, fx_ref, wx0_ref, wy0_ref, wz0_ref, diag0_ref, inv0_ref,
    out_ref,
    f_ref, c_ref, wx_ref, wy_ref, wz_ref, diag_ref, inv_ref, v_ref,
    f2_ref, c2_ref, wx2_ref, wy2_ref, wz2_ref, diag2_ref, inv2_ref, d2_ref, e2_ref, e3_ref,
    py_ref, vw_ref, dw_ref, vx_ref, e1_ref, yy_ref, v0_ref, d0_ref, x0_ref, o_ref,
):
    gx, gy = lax.axis_index("gx"), lax.axis_index("gy")
    odd = lax.rem(gy, 2) == 1
    brick1 = own_ref.shape[0] // (along_x * (along_y // 2))
    rows1, cols1, depth1 = f_ref.shape[0] - 2 * PAD, f_ref.shape[1], f_ref.shape[2]
    across = cols1 // SUB
    registers1 = across * (depth1 // 128)
    shape1 = (cols1, depth1)
    zero1 = jnp.zeros(shape1, F32)
    inv_mid, ((keep, push),) = chebyshev(SMOOTH_LOW, SMOOTH_HIGH, SMOOTH)

    low_half = iota((SUB, depth1), 0) < SUB // 2
    c_ref[PAD - 1] = zero1
    c_ref[PAD + rows1] = zero1

    def place(k):
        x, z = k // across, k % across
        at = z * SUB if isinstance(z, int) else pl.multiple_of(z * SUB, SUB)
        half = brick1 // 2
        for i in range(brick1):
            swapped = odd if i < half else jnp.logical_not(odd)
            low, high = k * brick1 + i % half, k * brick1 + half + i % half
            low = jnp.where(swapped, other_ref[low], own_ref[low])
            high = jnp.where(swapped, other_ref[high], own_ref[high])
            row = PAD + x * brick1 + i
            f_ref[row, pl.ds(at, SUB)] = jnp.where(low_half, low, high)
            c_ref[row, pl.ds(at, SUB)] = turn(jnp.where(low_half, high, low), SUB // 2, 0)

    each(along_x * across, brick1, place)

    wx_ref[PAD] = 0.5 * c_ref[PAD]

    def weigh(c, below, above, shape, stride):
        col, lane = iota(shape, 0), iota(shape, 1)
        half = 0.5 * c
        w_above = half + 0.5 * above
        w_cols = jnp.where(col == shape[0] - 1, 0.0, half + turn(half, -1, 0))
        w_depth = jnp.where(lane >= shape[1] - stride, 0.0, half + turn(half, -stride, 1))
        edge = jnp.where((col == 0) | (col == shape[0] - 1), half, 0.0)
        edge = edge + jnp.where((lane < stride) | (lane >= shape[1] - stride), half, 0.0)
        diag = half + 0.5 * below + w_above + w_cols + turn(w_cols, 1, 0)
        diag = diag + w_depth + turn(w_depth, stride, 1) + edge
        return w_above, w_cols, w_depth, diag

    def weigh1(i):
        row = PAD + i
        w_above, w_cols, w_depth, diag = weigh(
            c_ref[row], c_ref[row - 1], c_ref[row + 1], shape1, 1
        )
        inv = 1.0 / diag
        wx_ref[row + 1] = w_above
        wy_ref[row] = w_cols
        wz_ref[row] = w_depth
        diag_ref[row] = diag
        inv_ref[row] = inv
        v_ref[row] = f_ref[row] * inv * inv_mid

    v_ref[PAD - 1] = zero1
    v_ref[PAD + rows1] = zero1
    each(rows1, registers1, weigh1)

    rows2, cols2 = rows1 // 2, cols1 // 2
    shape2 = (cols2, depth1)
    registers2 = max(registers1 // 2, 1)
    zero2 = jnp.zeros(shape2, F32)
    lane2, col2 = iota(shape2, 1), iota(shape2, 0)
    even2 = lane2 % 2 == 0

    def fold(ref, row):
        half = ref[row, pl.ds(0, cols2, stride=2), :] + ref[row, pl.ds(1, cols2, stride=2), :]
        return half + jnp.where(even2, turn(half, -1, 1), turn(half, 1, 1))

    def restrict_c(k):
        row = PAD + 2 * k
        c2_ref[k + 1] = 0.125 * (fold(c_ref, row) + fold(c_ref, row + 1))

    each(rows2, 2 * registers1, restrict_c)
    u_ref = c_ref

    def residual1(x_ref, at, row):
        x = x_ref[at]
        total = beside(
            x, x_ref[at - 1], x_ref[at + 1],
            wx_ref[row], wx_ref[row + 1], wy_ref[row], wz_ref[row],
        )
        return x, f_ref[row] - (diag_ref[row] * x - total)

    def second1(i):
        row = PAD + i
        v, r = residual1(v_ref, row, row)
        u_ref[row] = v + (keep * v + push * (r * inv_ref[row]))

    each(rows1, registers1, second1)

    def restrict(k):
        row = PAD + 2 * k
        _, first = residual1(u_ref, row, row)
        _, second = residual1(u_ref, row + 1, row + 1)
        v_ref[k] = first + second
        f2_ref[k] = 0.5 * fold(v_ref, k)

    each(rows2, 2 * registers1, restrict)
    c2_ref[0] = zero2
    c2_ref[rows2 + 1] = zero2
    wx2_ref[0] = 0.5 * c2_ref[1]
    for ref in (e2_ref, e3_ref):
        ref[0] = zero2
        ref[rows2 + 1] = zero2
    inv_mid2, pairs2 = chebyshev(COARSE_LOW, COARSE_HIGH, COARSE_STEPS)

    def weigh2(k):
        w_above, w_cols, w_depth, diag = weigh(
            c2_ref[k + 1], c2_ref[k], c2_ref[k + 2], shape2, 2
        )
        inv = 1.0 / diag
        wx2_ref[k + 1] = w_above
        wy2_ref[k] = w_cols
        wz2_ref[k] = w_depth
        diag2_ref[k] = diag
        inv2_ref[k] = inv
        d = f2_ref[k] * inv * inv_mid2
        d2_ref[k] = d
        e2_ref[k + 1] = d

    each(rows2, registers2, weigh2)

    def residual2(e_ref, k):
        e = e_ref[k + 1]
        total = beside(
            e, e_ref[k], e_ref[k + 2], wx2_ref[k], wx2_ref[k + 1], wy2_ref[k], wz2_ref[k], 2
        )
        return e, f2_ref[k] - (diag2_ref[k] * e - total)

    now_ref, next_ref = e2_ref, e3_ref
    for keep2, push2 in pairs2:

        def step2(k):
            e, r = residual2(now_ref, k)
            d = keep2 * d2_ref[k] + push2 * (r * inv2_ref[k])
            d2_ref[k] = d
            next_ref[k + 1] = e + d

        each(rows2, registers2, step2)
        now_ref, next_ref = next_ref, now_ref

    def gather_sums(k, sums):
        _, r = residual2(now_ref, k)
        total = wx2_ref[k] * (k > 0) + wx2_ref[k + 1] * (k < rows2 - 1)
        total = total + wy2_ref[k] + turn(wy2_ref[k], 1, 0)
        total = total + wz2_ref[k] + turn(wz2_ref[k], 2, 1)
        return sums[0] + r, sums[1] + (diag2_ref[k] - total)

    sums = (zero2, zero2)
    if rows2 * registers2 <= WRITTEN_OUT:
        for k in range(rows2):
            sums = gather_sums(k, sums)
    else:
        sums = lax.fori_loop(0, rows2, gather_sums, sums)
    top = jnp.sum(sums[0], axis=(0, 1), keepdims=True)
    bottom = jnp.sum(sums[1], axis=(0, 1), keepdims=True)
    mean = top / bottom

    span = brick1 + 2 * PAD
    start = gx * brick1 - PAD
    coarse_span = span // 2 + 2
    for k in range(coarse_span):
        row = lax.div(gx * brick1, 2) - PAD // 2 - 1 + k
        good = (row >= 0) & (row < rows2)
        e = now_ref[jnp.clip(row, 0, rows2 - 1) + 1] + mean
        e = jnp.where(good, e, 0.0)
        back = jnp.where(lane2 < 2, 0.0, turn(e, 2, 1))
        ahead = jnp.where(lane2 >= depth1 - 2, 0.0, turn(e, -2, 1))
        e = 0.75 * e + 0.25 * jnp.where(even2, back, ahead)
        back = jnp.where(col2 == 0, 0.0, turn(e, 1, 0))
        ahead = jnp.where(col2 == cols2 - 1, 0.0, turn(e, -1, 0))
        py_ref[k, pl.ds(0, cols2, stride=2), :] = 0.75 * e + 0.25 * back
        py_ref[k, pl.ds(1, cols2, stride=2), :] = 0.75 * e + 0.25 * ahead

    def inside1(m):
        return (start + m >= 0) & (start + m < rows1)

    for m in range(span):
        near = m // 2 + 1
        far = near - 1 if m % 2 == 0 else near + 1
        total = u_ref[PAD + start + m] + (0.75 * py_ref[near] + 0.25 * py_ref[far])
        vw_ref[m] = jnp.where(inside1(m), total, 0.0)
    for m in range(1, span - 1):
        row = PAD + start + m
        v, r = residual1(vw_ref, m, row)
        d = r * inv_ref[row] * inv_mid
        dw_ref[m] = d
        vx_ref[m] = jnp.where(inside1(m), v + d, 0.0)
    margin = SUB
    e1_ref[:, 0:margin, :] = jnp.zeros((span - 4, margin, depth1), F32)
    e1_ref[:, margin + cols1 :, :] = jnp.zeros((span - 4, margin, depth1), F32)
    for m in range(2, span - 2):
        row = PAD + start + m
        v, r = residual1(vx_ref, m, row)
        e = v + (keep * dw_ref[m] + push * (r * inv_ref[row]))
        e1_ref[m - 2, margin : margin + cols1, :] = jnp.where(inside1(m), e, 0.0)

    rows, cols, depth = out_ref.shape
    wide = (cols + 2 * DEEP_C, depth)
    half_wide = wide[0] // 2
    first_col = margin + gy * (cols // 2) - DEEP_C // 2
    for k in range(span - 4):
        e = e1_ref[k, pl.ds(first_col, half_wide), :]
        at = k * wide[0]
        yy_ref[pl.ds(at, half_wide, stride=2), :] = 0.75 * e + 0.25 * turn(e, 1, 0)
        yy_ref[pl.ds(at + 1, half_wide, stride=2), :] = 0.75 * e + 0.25 * turn(e, -1, 0)
    spread = (depth1, depth)
    from_cell, to_cell = iota(spread, 0), iota(spread, 1)
    home = to_cell // 2
    near_cell = jnp.where(to_cell % 2 == 0, home - 1, home + 1)
    weights = jnp.where(from_cell == home, 0.75, 0.0) + jnp.where(from_cell == near_cell, 0.25, 0.0)
    carried = exact_dot(yy_ref[...], weights).reshape(span - 4, wide[0], depth)
    col = iota(wide, 0)
    col_inside = ((col >= DEEP_C) | (gy > 0)) & (
        (col < DEEP_C + cols) | (gy < along_y - 1)
    )
    for s in range(1, rows + 2 * DEEP_F - 1):
        row = s - DEEP_F
        near = row // 2 + 2
        far = near - 1 if row % 2 == 0 else near + 1
        inside = col_inside
        if row < 0:
            inside = inside & (gx > 0)
        if row >= rows:
            inside = inside & (gx < along_x - 1)
        total = u0_ref[s - 1] + (0.75 * carried[near] + 0.25 * carried[far])
        v0_ref[s] = jnp.where(inside, total, 0.0)

    def residual0(x_ref, s):
        x = x_ref[s]
        total = beside(
            x, x_ref[s - 1], x_ref[s + 1],
            wx0_ref[s], wx0_ref[s + 1], wy0_ref[s], wz0_ref[s],
        )
        return x, fx_ref[s] - (diag0_ref[s] * x - total)

    for s in range(2, rows + 2 * DEEP_F - 2):
        v, r = residual0(v0_ref, s)
        d = r * inv0_ref[s] * inv_mid
        d0_ref[s] = d
        x0_ref[s] = v + d
    for i in range(rows):
        s = i + DEEP_F
        v, r = residual0(x0_ref, s)
        o_ref[i] = v + (keep * d0_ref[s] + push * (r * inv0_ref[s]))
    for i in range(rows):
        out_ref[i] = o_ref[i, DEEP_C : DEEP_C + cols, :]


def pairs_from(first, count):
    swaps = []
    for i in range(first, first + count, 2):
        a, b = i % count, (i + 1) % count
        swaps += [(a, b), (b, a)]
    return swaps


def body(right_side, coefficient):
    along_x, along_y = lax.axis_size("gx"), lax.axis_size("gy")
    rows, cols, depth = right_side.shape
    assert cols == 2 * DEEP_C and rows % 4 == 0 and depth % 256 == 0
    assert along_x % 2 == 0 and along_y % 2 == 0
    small = 16 << 20
    strip = (DEEP_F + DEEP_C, cols, depth)
    odd = lax.rem(lax.axis_index("gx"), 2) == 1
    first = jnp.concatenate([right_side[:DEEP_F], coefficient[:DEEP_C]])
    last = jnp.concatenate([right_side[rows - DEEP_F :], coefficient[rows - DEEP_C :]])
    a, b = jnp.where(odd, first, last), jnp.where(odd, last, first)
    a = lax.ppermute(a, "gx", pairs_from(0, along_x))
    b = lax.ppermute(b, "gx", pairs_from(1, along_x))

    tall = rows + 2 * DEEP_F
    z, k = call(
        functools.partial(pack_cols, along_x),
        [(tall, cols, depth)] * 2,
        [],
        (right_side, coefficient, a, b),
        small,
    )
    k = lax.ppermute(k, "gy", pairs_from(0, along_y))
    z = lax.ppermute(z, "gy", pairs_from(1, along_y))

    wide = (cols + 2 * DEEP_C, depth)
    half = (rows // 2, SUB, depth // 2)
    copies = along_x * along_y // 2
    send, *state = call(
        functools.partial(fine_down, along_x, along_y, copies),
        [(copies * half[0],) + half[1:], (tall - 2,) + wide, (tall,) + wide, (tall + 1,) + wide]
        + [(tall,) + wide] * 4,
        [(tall + 2,) + wide, (tall,) + wide, (rows,) + wide],
        (right_side, coefficient, a, b, z, k),
        small + 2 * 4 * copies * half[0] * half[1] * half[2],
    )
    own = lax.all_to_all(send, ("gx", "gy"), 0, 0, tiled=True)
    other = lax.ppermute(own, "gy", pairs_from(0, along_y))

    rows1, cols1, depth1 = along_x * half[0], along_y * (cols // 2), half[2]
    whole1 = (rows1 + 2 * PAD + 1, cols1, depth1)
    rows2, cols2 = rows1 // 2, cols1 // 2
    whole2 = (rows2 + 2, cols2, depth1)
    span = half[0] + 2 * PAD
    line = (cols1, depth1)
    scratch = [(rows1 + 2 * PAD,) + line] + [whole1] * 7 + [whole2] * 10
    scratch += [(span // 2 + 2,) + line] + [(span,) + line] * 3
    scratch += [(span - 4, cols1 + 2 * SUB, depth1), ((span - 4) * wide[0], depth1)]
    scratch += [(tall,) + wide] * 3 + [(rows,) + wide]
    size = sum(4 * s[0] * s[1] * (s[2] if len(s) == 3 else 1) for s in scratch)
    size += 2 * 4 * own.size + 4 * 8 * tall * wide[0] * wide[1]
    (out,) = call(
        functools.partial(coarse_and_up, along_x, along_y),
        [right_side.shape],
        scratch,
        (own, other, *state),
        size + (12 << 20),
    )
    return out


def solution(mesh):
    placed = (P("gx", "gy", None), P("gx", "gy", None))
    return jax.shard_map(
        body, mesh=mesh, in_specs=placed, out_specs=P("gx", "gy", None), check_vma=False
    )
```

```python
import functools

import jax
import jax.numpy as jnp
from jax import lax
from jax.experimental import pallas as pl
from jax.experimental.pallas import tpu as pltpu
from jax.sharding import PartitionSpec as P

SMOOTH = 2
COARSE_STEPS = 6
SMOOTH_LOW = 0.5
SMOOTH_HIGH = 2.0
COARSE_LOW = 0.05
COARSE_HIGH = 2.0

DEEP_F = 2 * SMOOTH - 1
DEEP_C = 2 * SMOOTH
SUB = 8
PAD = 4
WRITTEN_OUT = 512

VMEM = pl.BlockSpec(memory_space=pltpu.VMEM)
F32 = jnp.float32


def chebyshev(low_end, high_end, sweeps):
    middle = 0.5 * (high_end + low_end)
    half_span = 0.5 * (high_end - low_end)
    sig_ratio = middle / half_span
    rho_now = 1.0 / sig_ratio
    coeff_pairs = []
    for sweep_num in range(1, sweeps):
        rho_next = 1.0 / (2.0 * sig_ratio - rho_now)
        coeff_pairs.append((rho_next * rho_now, 2.0 * rho_next / half_span))
        rho_now = rho_next
    return (1.0 / middle, coeff_pairs)


def each(count, registers, step):
    if count * registers <= WRITTEN_OUT:
        for i in range(count):
            step(i)
    else:

        def one(i, carry):
            step(i)
            return carry

        lax.fori_loop(0, count, one, 0)


def turn(value, amount, axis):
    return pltpu.roll(value, amount % value.shape[axis], axis)


def iota(shape, axis):
    return lax.broadcasted_iota(jnp.int32, shape, axis)


def beside(v, below, above, w_below, w_above, w_cols, w_depth, stride=1):
    out = w_above * above + w_below * below
    out = out + w_cols * turn(v, -1, 0)
    out = out + w_depth * turn(v, -stride, 1)
    return out + turn(w_cols * v, 1, 0) + turn(w_depth * v, stride, 1)


def exact_dot(a, b):
    return jnp.dot(a, b, precision=lax.Precision.HIGHEST, preferred_element_type=F32)


def call(kernel, out_shapes, scratch, args, limit):
    return pl.pallas_call(
        kernel,
        out_shape=[jax.ShapeDtypeStruct(s, F32) for s in out_shapes],
        in_specs=[VMEM] * len(args),
        out_specs=[VMEM] * len(out_shapes),
        scratch_shapes=[pltpu.VMEM(s, F32) for s in scratch],
        compiler_params=pltpu.CompilerParams(vmem_limit_bytes=limit),
    )(*args)


def pack_rows(f_ref, c_ref, a_ref, b_ref, sems):
    rows = f_ref.shape[0]
    odd = lax.rem(lax.axis_index("gx"), 2)
    copies = []
    for ref, at_end in ((a_ref, 1 - odd), (b_ref, odd)):
        for whole_ref, first, count in ((f_ref, 0, DEEP_F), (c_ref, DEEP_F, DEEP_C)):
            copies.append(
                pltpu.make_async_copy(
                    whole_ref.at[pl.ds(at_end * (rows - count), count)],
                    ref.at[pl.ds(first, count)],
                    sems.at[len(copies)],
                )
            )
    for copy in copies:
        copy.start()
    for copy in copies:
        copy.wait()


def row_sources(along_x, rows, f_ref, c_ref, a_ref, b_ref):
    gx = lax.axis_index("gx")
    odd = lax.rem(gx, 2) == 1
    has_before = (gx > 0).astype(F32)
    has_after = (gx < along_x - 1).astype(F32)

    def before(i):
        return jnp.where(odd, a_ref[i], b_ref[i]) * has_before

    def after(i):
        return jnp.where(odd, b_ref[i], a_ref[i]) * has_after

    def f_row(i):
        if i < 0:
            return before(DEEP_F + i)
        return f_ref[i] if i < rows else after(i - rows)

    def c_row(i):
        if i < 0:
            return before(DEEP_F + DEEP_C + i)
        return c_ref[i] if i < rows else after(DEEP_F + i - rows)

    return f_row, c_row


def pack_cols(along_x, f_ref, c_ref, a_ref, b_ref, z_ref, k_ref):
    rows = f_ref.shape[0]
    f_row, c_row = row_sources(along_x, rows, f_ref, c_ref, a_ref, b_ref)
    odd = lax.rem(lax.axis_index("gy"), 2) == 1
    low_half = iota(f_ref.shape[1:], 0) < DEEP_C
    for t in range(rows + 2 * DEEP_F):
        f, c = f_row(t - DEEP_F), c_row(t - DEEP_F)
        first = jnp.where(low_half, c, turn(f, DEEP_C, 0))
        last = jnp.where(low_half, turn(c, DEEP_C, 0), f)
        z_ref[t] = jnp.where(odd, last, first)
        k_ref[t] = jnp.where(odd, first, last)


def fine_down(
    along_x, along_y, copies,
    f_ref, c_ref, a_ref, b_ref, z_ref, k_ref,
    send_ref, u_ref, fx_ref, wx_ref, wy_ref, wz_ref, diag_ref, inv_ref,
    cx_ref, v_ref, r_ref,
):
    rows, cols, depth = f_ref.shape
    f_row, c_row = row_sources(along_x, rows, f_ref, c_ref, a_ref, b_ref)
    gx, gy = lax.axis_index("gx"), lax.axis_index("gy")
    odd = lax.rem(gy, 2) == 1
    has_left = (gy > 0).astype(F32)
    has_right = (gy < along_y - 1).astype(F32)
    low_half = iota((cols, depth), 0) < DEEP_C
    wide = (cols + 2 * DEEP_C, depth)
    lane = iota(wide, 1)
    col = iota(wide, 0)
    col_inside = ((col >= DEEP_C) | (gy > 0)) & (
        (col < DEEP_C + cols) | (gy < along_y - 1)
    )
    inv_mid, ((keep, push),) = chebyshev(SMOOTH_LOW, SMOOTH_HIGH, SMOOTH)

    for t in range(rows + 2 * DEEP_C):
        row = t - DEEP_C
        c = c_row(row)
        turned = turn(c, DEEP_C, 0)
        s = row + DEEP_F
        if 0 <= s < rows + 2 * DEEP_F:
            left = jnp.where(odd, k_ref[s], z_ref[s]) * has_left
            right = jnp.where(odd, z_ref[s], k_ref[s]) * has_right
            f = f_row(row)
            fx_ref[s, 0:cols] = turn(jnp.where(low_half, f, left), DEEP_C, 0)
            fx_ref[s, cols:] = jnp.where(low_half, turn(f, DEEP_C, 0), right)
        else:
            left = right = jnp.zeros_like(c)
        cx_ref[t, 0:cols] = jnp.where(low_half, left, turned)
        cx_ref[t, cols:] = jnp.where(low_half, turned, turn(right, DEEP_C, 0))

    tall = rows + 2 * DEEP_F
    wx_ref[0] = 0.5 * (cx_ref[0] + cx_ref[1])
    for s in range(tall):
        c = cx_ref[s + 1]
        half = 0.5 * c
        above = half + 0.5 * cx_ref[s + 2]
        wx_ref[s + 1] = above
        w_cols = half + turn(half, -1, 0)
        w_depth = jnp.where(lane == depth - 1, 0.0, half + turn(half, -1, 1))
        edge = jnp.where((lane == 0) | (lane == depth - 1), half, 0.0)
        diag = wx_ref[s] + above + w_cols + turn(w_cols, 1, 0)
        diag = diag + w_depth + turn(w_depth, 1, 1) + edge
        inside = col_inside
        if s < DEEP_F:
            inside = inside & (gx > 0)
        if s >= rows + DEEP_F:
            inside = inside & (gx < along_x - 1)
        inv = jnp.where(inside, 1.0 / diag, 0.0)
        wy_ref[s] = w_cols
        wz_ref[s] = w_depth
        diag_ref[s] = diag
        inv_ref[s] = inv
        v_ref[s] = fx_ref[s] * inv * inv_mid

    def residual(x_ref, shift, s):
        x = x_ref[s - shift]
        total = beside(
            x, x_ref[s - shift - 1], x_ref[s - shift + 1],
            wx_ref[s], wx_ref[s + 1], wy_ref[s], wz_ref[s],
        )
        return x, fx_ref[s] - (diag_ref[s] * x - total)

    for s in range(1, tall - 1):
        v, r = residual(v_ref, 0, s)
        u_ref[s - 1] = v + (keep * v + push * (r * inv_ref[s]))
    for i in range(rows):
        _, r_ref[i] = residual(u_ref, 1, i + DEEP_F)

    half_rows = rows // 2
    summed = [r_ref[2 * i] + r_ref[2 * i + 1] for i in range(half_rows)]
    summed += [c_ref[2 * i] + c_ref[2 * i + 1] for i in range(half_rows)]
    summed = jnp.concatenate(summed, axis=0)
    pairs = (depth, depth // 2)
    thin = exact_dot(summed, (iota(pairs, 0) // 2 == iota(pairs, 1)).astype(F32))
    choice = (SUB * half_rows, summed.shape[0])
    line, source = iota(choice, 0), iota(choice, 1)
    block, place = line // SUB, line % SUB
    half_cols = cols // 2
    f_half = (place >= half_cols) == odd
    place = place % half_cols
    f_from = wide[0] * block + DEEP_C + 2 * place
    c_from = wide[0] * half_rows + cols * block + 2 * place
    from_f = (source == f_from) | (source == f_from + 1)
    from_c = (source == c_from) | (source == c_from + 1)
    picker = jnp.where(f_half, jnp.where(from_f, 0.5, 0.0), jnp.where(from_c, 0.125, 0.0))
    tile = exact_dot(picker, thin).reshape(half_rows, SUB, depth // 2)

    def put(i):
        send_ref[pl.ds(i * half_rows, half_rows)] = tile

    each(copies, half_rows, put)


def coarse_and_up(
    along_x, along_y,
    own_ref, other_ref, u0_ref, fx_ref, wx0_ref, wy0_ref, wz0_ref, diag0_ref, inv0_ref,
    out_ref,
    f_ref, c_ref, wx_ref, wy_ref, wz_ref, diag_ref, inv_ref, v_ref,
    f2_ref, c2_ref, wx2_ref, wy2_ref, wz2_ref, diag2_ref, inv2_ref, d2_ref, e2_ref, e3_ref,
    py_ref, vw_ref, dw_ref, vx_ref, e1_ref, yy_ref, v0_ref, d0_ref, x0_ref, o_ref,
):
    gx, gy = lax.axis_index("gx"), lax.axis_index("gy")
    odd = lax.rem(gy, 2) == 1
    brick1 = own_ref.shape[0] // (along_x * (along_y // 2))
    rows1, cols1, depth1 = f_ref.shape[0] - 2 * PAD, f_ref.shape[1], f_ref.shape[2]
    across = cols1 // SUB
    registers1 = across * (depth1 // 128)
    shape1 = (cols1, depth1)
    zero1 = jnp.zeros(shape1, F32)
    inv_mid, ((keep, push),) = chebyshev(SMOOTH_LOW, SMOOTH_HIGH, SMOOTH)

    low_half = iota((SUB, depth1), 0) < SUB // 2
    c_ref[PAD - 1] = zero1
    c_ref[PAD + rows1] = zero1

    def place(k):
        x, z = k // across, k % across
        at = z * SUB if isinstance(z, int) else pl.multiple_of(z * SUB, SUB)
        half = brick1 // 2
        for i in range(brick1):
            swapped = odd if i < half else jnp.logical_not(odd)
            low, high = k * brick1 + i % half, k * brick1 + half + i % half
            low = jnp.where(swapped, other_ref[low], own_ref[low])
            high = jnp.where(swapped, other_ref[high], own_ref[high])
            row = PAD + x * brick1 + i
            f_ref[row, pl.ds(at, SUB)] = jnp.where(low_half, low, high)
            c_ref[row, pl.ds(at, SUB)] = turn(jnp.where(low_half, high, low), SUB // 2, 0)

    each(along_x * across, brick1, place)

    wx_ref[PAD] = 0.5 * c_ref[PAD]

    def weigh(c, below, above, shape, stride):
        col, lane = iota(shape, 0), iota(shape, 1)
        half = 0.5 * c
        w_above = half + 0.5 * above
        w_cols = jnp.where(col == shape[0] - 1, 0.0, half + turn(half, -1, 0))
        w_depth = jnp.where(lane >= shape[1] - stride, 0.0, half + turn(half, -stride, 1))
        edge = jnp.where((col == 0) | (col == shape[0] - 1), half, 0.0)
        edge = edge + jnp.where((lane < stride) | (lane >= shape[1] - stride), half, 0.0)
        diag = half + 0.5 * below + w_above + w_cols + turn(w_cols, 1, 0)
        diag = diag + w_depth + turn(w_depth, stride, 1) + edge
        return w_above, w_cols, w_depth, diag

    def weigh1(i):
        row = PAD + i
        w_above, w_cols, w_depth, diag = weigh(
            c_ref[row], c_ref[row - 1], c_ref[row + 1], shape1, 1
        )
        inv = 1.0 / diag
        wx_ref[row + 1] = w_above
        wy_ref[row] = w_cols
        wz_ref[row] = w_depth
        diag_ref[row] = diag
        inv_ref[row] = inv
        v_ref[row] = f_ref[row] * inv * inv_mid

    v_ref[PAD - 1] = zero1
    v_ref[PAD + rows1] = zero1
    each(rows1, registers1, weigh1)

    rows2, cols2 = rows1 // 2, cols1 // 2
    shape2 = (cols2, depth1)
    registers2 = max(registers1 // 2, 1)
    zero2 = jnp.zeros(shape2, F32)
    lane2, col2 = iota(shape2, 1), iota(shape2, 0)
    even2 = lane2 % 2 == 0

    def fold(ref, row):
        half = ref[row, pl.ds(0, cols2, stride=2), :] + ref[row, pl.ds(1, cols2, stride=2), :]
        return half + jnp.where(even2, turn(half, -1, 1), turn(half, 1, 1))

    def restrict_c(k):
        row = PAD + 2 * k
        c2_ref[k + 1] = 0.125 * (fold(c_ref, row) + fold(c_ref, row + 1))

    each(rows2, 2 * registers1, restrict_c)
    u_ref = c_ref

    def residual1(x_ref, at, row):
        x = x_ref[at]
        total = beside(
            x, x_ref[at - 1], x_ref[at + 1],
            wx_ref[row], wx_ref[row + 1], wy_ref[row], wz_ref[row],
        )
        return x, f_ref[row] - (diag_ref[row] * x - total)

    def second1(i):
        row = PAD + i
        v, r = residual1(v_ref, row, row)
        u_ref[row] = v + (keep * v + push * (r * inv_ref[row]))

    each(rows1, registers1, second1)

    def restrict(k):
        row = PAD + 2 * k
        _, first = residual1(u_ref, row, row)
        _, second = residual1(u_ref, row + 1, row + 1)
        v_ref[k] = first + second
        f2_ref[k] = 0.5 * fold(v_ref, k)

    each(rows2, 2 * registers1, restrict)
    c2_ref[0] = zero2
    c2_ref[rows2 + 1] = zero2
    wx2_ref[0] = 0.5 * c2_ref[1]
    for ref in (e2_ref, e3_ref):
        ref[0] = zero2
        ref[rows2 + 1] = zero2
    inv_mid2, pairs2 = chebyshev(COARSE_LOW, COARSE_HIGH, COARSE_STEPS)

    def weigh2(k):
        w_above, w_cols, w_depth, diag = weigh(
            c2_ref[k + 1], c2_ref[k], c2_ref[k + 2], shape2, 2
        )
        inv = 1.0 / diag
        wx2_ref[k + 1] = w_above
        wy2_ref[k] = w_cols
        wz2_ref[k] = w_depth
        diag2_ref[k] = diag
        inv2_ref[k] = inv
        d = f2_ref[k] * inv * inv_mid2
        d2_ref[k] = d
        e2_ref[k + 1] = d

    each(rows2, registers2, weigh2)

    def residual2(e_ref, k):
        e = e_ref[k + 1]
        total = beside(
            e, e_ref[k], e_ref[k + 2], wx2_ref[k], wx2_ref[k + 1], wy2_ref[k], wz2_ref[k], 2
        )
        return e, f2_ref[k] - (diag2_ref[k] * e - total)

    now_ref, next_ref = e2_ref, e3_ref
    for keep2, push2 in pairs2:

        def step2(k):
            e, r = residual2(now_ref, k)
            d = keep2 * d2_ref[k] + push2 * (r * inv2_ref[k])
            d2_ref[k] = d
            next_ref[k + 1] = e + d

        each(rows2, registers2, step2)
        now_ref, next_ref = next_ref, now_ref

    def gather_sums(k, sums):
        _, r = residual2(now_ref, k)
        total = wx2_ref[k] * (k > 0) + wx2_ref[k + 1] * (k < rows2 - 1)
        total = total + wy2_ref[k] + turn(wy2_ref[k], 1, 0)
        total = total + wz2_ref[k] + turn(wz2_ref[k], 2, 1)
        return sums[0] + r, sums[1] + (diag2_ref[k] - total)

    sums = (zero2, zero2)
    if rows2 * registers2 <= WRITTEN_OUT:
        for k in range(rows2):
            sums = gather_sums(k, sums)
    else:
        sums = lax.fori_loop(0, rows2, gather_sums, sums)
    top = jnp.sum(sums[0], axis=(0, 1), keepdims=True)
    bottom = jnp.sum(sums[1], axis=(0, 1), keepdims=True)
    mean = top / bottom

    span = brick1 + 2 * PAD
    start = gx * brick1 - PAD
    coarse_span = span // 2 + 2
    for k in range(coarse_span):
        row = lax.div(gx * brick1, 2) - PAD // 2 - 1 + k
        good = (row >= 0) & (row < rows2)
        e = now_ref[jnp.clip(row, 0, rows2 - 1) + 1] + mean
        e = jnp.where(good, e, 0.0)
        back = jnp.where(lane2 < 2, 0.0, turn(e, 2, 1))
        ahead = jnp.where(lane2 >= depth1 - 2, 0.0, turn(e, -2, 1))
        e = 0.75 * e + 0.25 * jnp.where(even2, back, ahead)
        back = jnp.where(col2 == 0, 0.0, turn(e, 1, 0))
        ahead = jnp.where(col2 == cols2 - 1, 0.0, turn(e, -1, 0))
        py_ref[k, pl.ds(0, cols2, stride=2), :] = 0.75 * e + 0.25 * back
        py_ref[k, pl.ds(1, cols2, stride=2), :] = 0.75 * e + 0.25 * ahead

    def inside1(m):
        return (start + m >= 0) & (start + m < rows1)

    for m in range(span):
        near = m // 2 + 1
        far = near - 1 if m % 2 == 0 else near + 1
        total = u_ref[PAD + start + m] + (0.75 * py_ref[near] + 0.25 * py_ref[far])
        vw_ref[m] = jnp.where(inside1(m), total, 0.0)
    for m in range(1, span - 1):
        row = PAD + start + m
        v, r = residual1(vw_ref, m, row)
        d = r * inv_ref[row] * inv_mid
        dw_ref[m] = d
        vx_ref[m] = jnp.where(inside1(m), v + d, 0.0)
    margin = SUB
    e1_ref[:, 0:margin, :] = jnp.zeros((span - 4, margin, depth1), F32)
    e1_ref[:, margin + cols1 :, :] = jnp.zeros((span - 4, margin, depth1), F32)
    for m in range(2, span - 2):
        row = PAD + start + m
        v, r = residual1(vx_ref, m, row)
        e = v + (keep * dw_ref[m] + push * (r * inv_ref[row]))
        e1_ref[m - 2, margin : margin + cols1, :] = jnp.where(inside1(m), e, 0.0)

    rows, cols, depth = out_ref.shape
    wide = (cols + 2 * DEEP_C, depth)
    half_wide = wide[0] // 2
    first_col = margin + gy * (cols // 2) - DEEP_C // 2
    for k in range(span - 4):
        e = e1_ref[k, pl.ds(first_col, half_wide), :]
        at = k * wide[0]
        yy_ref[pl.ds(at, half_wide, stride=2), :] = 0.75 * e + 0.25 * turn(e, 1, 0)
        yy_ref[pl.ds(at + 1, half_wide, stride=2), :] = 0.75 * e + 0.25 * turn(e, -1, 0)
    spread = (depth1, depth)
    from_cell, to_cell = iota(spread, 0), iota(spread, 1)
    home = to_cell // 2
    near_cell = jnp.where(to_cell % 2 == 0, home - 1, home + 1)
    weights = jnp.where(from_cell == home, 0.75, 0.0) + jnp.where(from_cell == near_cell, 0.25, 0.0)
    carried = exact_dot(yy_ref[...], weights).reshape(span - 4, wide[0], depth)
    col = iota(wide, 0)
    col_inside = ((col >= DEEP_C) | (gy > 0)) & (
        (col < DEEP_C + cols) | (gy < along_y - 1)
    )
    for s in range(1, rows + 2 * DEEP_F - 1):
        row = s - DEEP_F
        near = row // 2 + 2
        far = near - 1 if row % 2 == 0 else near + 1
        inside = col_inside
        if row < 0:
            inside = inside & (gx > 0)
        if row >= rows:
            inside = inside & (gx < along_x - 1)
        total = u0_ref[s - 1] + (0.75 * carried[near] + 0.25 * carried[far])
        v0_ref[s] = jnp.where(inside, total, 0.0)

    def residual0(x_ref, s):
        x = x_ref[s]
        total = beside(
            x, x_ref[s - 1], x_ref[s + 1],
            wx0_ref[s], wx0_ref[s + 1], wy0_ref[s], wz0_ref[s],
        )
        return x, fx_ref[s] - (diag0_ref[s] * x - total)

    for s in range(2, rows + 2 * DEEP_F - 2):
        v, r = residual0(v0_ref, s)
        d = r * inv0_ref[s] * inv_mid
        d0_ref[s] = d
        x0_ref[s] = v + d
    for i in range(rows):
        s = i + DEEP_F
        v, r = residual0(x0_ref, s)
        o_ref[i] = v + (keep * d0_ref[s] + push * (r * inv0_ref[s]))
    for i in range(rows):
        out_ref[i] = o_ref[i, DEEP_C : DEEP_C + cols, :]


def pairs_from(first, count):
    swaps = []
    for i in range(first, first + count, 2):
        a, b = i % count, (i + 1) % count
        swaps += [(a, b), (b, a)]
    return swaps


def swaps(along_x, along_y, axis, first):
    pairs = []
    for x in range(along_x):
        for y in range(along_y):
            place, count = (x, along_x) if axis == "gx" else (y, along_y)
            other = place + 1 if (place - first) % 2 == 0 else place - 1
            if 0 <= other < count:
                to = (other, y) if axis == "gx" else (x, other)
            else:
                to = (x, y ^ 1) if axis == "gx" else (x ^ 1, y)
            pairs.append((x * along_y + y, to[0] * along_y + to[1]))
    return pairs


def body(right_side, coefficient):
    along_x, along_y = lax.axis_size("gx"), lax.axis_size("gy")
    rows, cols, depth = right_side.shape
    assert cols == 2 * DEEP_C and rows % 4 == 0 and depth % 256 == 0
    assert along_x % 2 == 0 and along_y % 2 == 0
    small = 16 << 20
    strip = (DEEP_F + DEEP_C, cols, depth)
    odd = lax.rem(lax.axis_index("gx"), 2) == 1
    first = jnp.concatenate([right_side[:DEEP_F], coefficient[:DEEP_C]])
    last = jnp.concatenate([right_side[rows - DEEP_F :], coefficient[rows - DEEP_C :]])
    a, b = jnp.where(odd, first, last), jnp.where(odd, last, first)
    a = lax.ppermute(a, "gx", pairs_from(0, along_x))
    b = lax.ppermute(b, ("gx", "gy"), swaps(along_x, along_y, "gx", 1))

    tall = rows + 2 * DEEP_F
    z, k = call(
        functools.partial(pack_cols, along_x),
        [(tall, cols, depth)] * 2,
        [],
        (right_side, coefficient, a, b),
        small,
    )
    k = lax.ppermute(k, "gy", pairs_from(0, along_y))
    z = lax.ppermute(z, ("gx", "gy"), swaps(along_x, along_y, "gy", 1))

    wide = (cols + 2 * DEEP_C, depth)
    half = (rows // 2, SUB, depth // 2)
    copies = along_x * along_y // 2
    send, *state = call(
        functools.partial(fine_down, along_x, along_y, copies),
        [(copies * half[0],) + half[1:], (tall - 2,) + wide, (tall,) + wide, (tall + 1,) + wide]
        + [(tall,) + wide] * 4,
        [(tall + 2,) + wide, (tall,) + wide, (rows,) + wide],
        (right_side, coefficient, a, b, z, k),
        small + 2 * 4 * copies * half[0] * half[1] * half[2],
    )
    own = lax.all_to_all(send, ("gx", "gy"), 0, 0, tiled=True)
    other = lax.ppermute(own, "gy", pairs_from(0, along_y))

    rows1, cols1, depth1 = along_x * half[0], along_y * (cols // 2), half[2]
    whole1 = (rows1 + 2 * PAD + 1, cols1, depth1)
    rows2, cols2 = rows1 // 2, cols1 // 2
    whole2 = (rows2 + 2, cols2, depth1)
    span = half[0] + 2 * PAD
    line = (cols1, depth1)
    scratch = [(rows1 + 2 * PAD,) + line] + [whole1] * 7 + [whole2] * 10
    scratch += [(span // 2 + 2,) + line] + [(span,) + line] * 3
    scratch += [(span - 4, cols1 + 2 * SUB, depth1), ((span - 4) * wide[0], depth1)]
    scratch += [(tall,) + wide] * 3 + [(rows,) + wide]
    size = sum(4 * s[0] * s[1] * (s[2] if len(s) == 3 else 1) for s in scratch)
    size += 2 * 4 * own.size + 4 * 8 * tall * wide[0] * wide[1]
    (out,) = call(
        functools.partial(coarse_and_up, along_x, along_y),
        [right_side.shape],
        scratch,
        (own, other, *state),
        size + (12 << 20),
    )
    return out


def solution(mesh):
    placed = (P("gx", "gy", None), P("gx", "gy", None))
    return jax.shard_map(
        body, mesh=mesh, in_specs=placed, out_specs=P("gx", "gy", None), check_vma=False
    )
```

```python
import functools
import math

import jax
import jax.numpy as jnp
from jax import lax
from jax.experimental import pallas as pl
from jax.experimental.pallas import tpu as pltpu
from jax.sharding import PartitionSpec as P

SMOOTH = 2
COARSE_STEPS = 6
SMOOTH_LOW = 0.5
SMOOTH_HIGH = 2.0
COARSE_LOW = 0.05
COARSE_HIGH = 2.0

DEEP_F = 2 * SMOOTH - 1
DEEP_C = 2 * SMOOTH
SUB = 8
PAD = 4
WRITTEN_OUT = 512

VMEM = pl.BlockSpec(memory_space=pltpu.VMEM)
F32 = jnp.float32


def chebyshev(low_end, high_end, sweeps):
    middle = 0.5 * (high_end + low_end)
    half_span = 0.5 * (high_end - low_end)
    sig_ratio = middle / half_span
    rho_now = 1.0 / sig_ratio
    coeff_pairs = []
    for sweep_num in range(1, sweeps):
        rho_next = 1.0 / (2.0 * sig_ratio - rho_now)
        coeff_pairs.append((rho_next * rho_now, 2.0 * rho_next / half_span))
        rho_now = rho_next
    return (1.0 / middle, coeff_pairs)


def each(count, registers, step):
    each_sum(count, registers, lambda i, carry: (step(i), carry)[1], 0)


def each_sum(count, registers, step, carry):
    if count * registers > WRITTEN_OUT:
        return lax.fori_loop(0, count, step, carry)
    for i in range(count):
        carry = step(i, carry)
    return carry


def turn(value, amount, axis):
    return pltpu.roll(value, amount % value.shape[axis], axis)


def iota(shape, axis):
    return lax.broadcasted_iota(jnp.int32, shape, axis)


def beside(v, below, above, w_below, w_above, w_cols, w_depth):
    span = below.shape[0]
    out = w_above * above + w_below * below
    out = out + w_cols[:span] * turn(v, -1, 0)[:span]
    out = out + turn(w_cols * v, 1, 0)[:span]
    v = v[:span]
    return out + w_depth * turn(v, -1, 1) + turn(w_depth * v, 1, 1)


def inside_cols(col, cols, along_y):
    gy = lax.axis_index("gy")
    after = (col >= cols) & (col < cols + DEEP_C) & (gy == along_y - 1)
    before = (col >= cols + DEEP_C) & (gy == 0)
    return jnp.logical_not(after | before)


def exact_dot(a, b):
    return jnp.dot(a, b, precision=lax.Precision.HIGHEST, preferred_element_type=F32)


def call(kernel, out_shapes, scratch, args, limit):
    return pl.pallas_call(
        kernel,
        out_shape=[jax.ShapeDtypeStruct(s, F32) for s in out_shapes],
        in_specs=[VMEM] * len(args),
        out_specs=[VMEM] * len(out_shapes),
        scratch_shapes=[pltpu.VMEM(s, F32) for s in scratch],
        compiler_params=pltpu.CompilerParams(vmem_limit_bytes=limit),
    )(*args)


def pack_rows(f_ref, c_ref, a_ref, b_ref, sems):
    rows = f_ref.shape[0]
    odd = lax.rem(lax.axis_index("gx"), 2)
    copies = []
    for ref, at_end in ((a_ref, 1 - odd), (b_ref, odd)):
        for whole_ref, first, count in ((f_ref, 0, DEEP_F), (c_ref, DEEP_F, DEEP_C)):
            copies.append(
                pltpu.make_async_copy(
                    whole_ref.at[pl.ds(at_end * (rows - count), count)],
                    ref.at[pl.ds(first, count)],
                    sems.at[len(copies)],
                )
            )
    for copy in copies:
        copy.start()
    for copy in copies:
        copy.wait()


def row_sources(along_x, rows, f_ref, c_ref, a_ref, b_ref):
    gx = lax.axis_index("gx")
    odd = lax.rem(gx, 2) == 1
    has_before = (gx > 0).astype(F32)
    has_after = (gx < along_x - 1).astype(F32)

    def before(i):
        return jnp.where(odd, a_ref[i], b_ref[i]) * has_before

    def after(i):
        return jnp.where(odd, b_ref[i], a_ref[i]) * has_after

    def f_row(i):
        if i < 0:
            return before(DEEP_F + i)
        return f_ref[i] if i < rows else after(i - rows)

    def c_row(i):
        if i < 0:
            return before(DEEP_F + DEEP_C + i)
        return c_ref[i] if i < rows else after(DEEP_F + i - rows)

    return f_row, c_row


def pack_cols(along_x, f_ref, c_ref, a_ref, b_ref, z_ref, k_ref):
    rows = f_ref.shape[0]
    f_row, c_row = row_sources(along_x, rows, f_ref, c_ref, a_ref, b_ref)
    odd = lax.rem(lax.axis_index("gy"), 2) == 1
    sub = iota(f_ref.shape[1:], 0)
    low_half = sub < DEEP_C

    def put(t, first, last):
        z_ref[t] = jnp.where(odd, last, first)
        k_ref[t] = jnp.where(odd, first, last)

    for t in range(rows + 2):
        f, c = turn(f_row(t - 1), DEEP_C, 0), c_row(t - 1)
        put(t, jnp.where(low_half, c, f), jnp.where(low_half, f, c))

    def corners(sub, way):
        near, near_f, far = c_row(-2), f_row(-2), c_row(-3)
        out = jnp.where(sub < 2, near, jnp.where(sub == 2, turn(near_f, 2 * way, 0), turn(far, 3 * way, 0)))
        near, near_f, far = c_row(rows + 1), f_row(rows + 1), c_row(rows + 2)
        out = jnp.where(sub < 4, out, jnp.where(sub < 6, turn(near, 4 * way, 0), turn(near_f, 6 * way, 0)))
        return jnp.where(sub < 7, out, turn(far, 7 * way, 0))

    put(rows + 2, corners(sub, 1), corners(SUB - 1 - sub, -1))


def fine_down(
    along_x, along_y, copies,
    f_ref, c_ref, a_ref, b_ref, z_ref, k_ref,
    send_ref, u_ref, fx_ref, wx_ref, wy_ref, wz_ref, inv_ref,
    cx_ref, v_ref, diag_ref,
):
    rows, cols, depth = f_ref.shape
    f_row, c_row = row_sources(along_x, rows, f_ref, c_ref, a_ref, b_ref)
    gx, gy = lax.axis_index("gx"), lax.axis_index("gy")
    odd = lax.rem(gy, 2) == 1
    has_left = (gy > 0).astype(F32)
    has_right = (gy < along_y - 1).astype(F32)
    low_half = iota((cols, depth), 0) < DEEP_C
    wide = (cols + 2 * DEEP_C, depth)
    lane = iota(wide, 1)
    col = iota(wide, 0)
    col_inside = inside_cols(col, cols, along_y)
    inv_mid, ((keep, push),) = chebyshev(SMOOTH_LOW, SMOOTH_HIGH, SMOOTH)

    def sides(t):
        left = jnp.where(odd, k_ref[t], z_ref[t]) * has_left
        return left, jnp.where(odd, z_ref[t], k_ref[t]) * has_right

    corner_tiles = sides(rows + 2)
    for t in range(rows + 2 * DEEP_C):
        row = t - DEEP_C
        cx_ref[t, 0:cols] = c_row(row)
        s = row + DEEP_F
        if -1 <= row <= rows:
            left, right = sides(row + 1)
            cx_ref[t, cols:] = jnp.where(low_half, right, left)
            f = turn(jnp.where(low_half, left, right), DEEP_C, 0)
        else:
            left, right = corner_tiles
            c_turn = {-2: 0, -3: 3, rows + 1: 4, rows + 2: 7}.get(row)
            f_turn = {-2: 2, rows + 1: 6}.get(row)
            c = f = jnp.zeros((cols, depth), F32)
            if c_turn is not None:
                c = jnp.where(low_half, turn(right, -c_turn, 0), turn(left, c_turn, 0))
            if f_turn is not None:
                f = jnp.where(low_half, turn(right, -f_turn, 0), turn(left, f_turn, 0))
            cx_ref[t, cols:] = c
        if 0 <= s < rows + 2 * DEEP_F:
            fx_ref[s, 0:cols] = f_row(row)
            fx_ref[s, cols:] = f

    tall = rows + 2 * DEEP_F
    wx_ref[0] = 0.5 * (cx_ref[0] + cx_ref[1])
    for s in range(tall):
        c = cx_ref[s + 1]
        half = 0.5 * c
        above = half + 0.5 * cx_ref[s + 2]
        wx_ref[s + 1] = above
        w_cols = half + turn(half, -1, 0)
        w_depth = jnp.where(lane == depth - 1, 0.0, half + turn(half, -1, 1))
        edge = jnp.where((lane == 0) | (lane == depth - 1), half, 0.0)
        diag = wx_ref[s] + above + w_cols + turn(w_cols, 1, 0)
        diag = diag + w_depth + turn(w_depth, 1, 1) + edge
        inside = col_inside
        if s < DEEP_F:
            inside = inside & (gx > 0)
        if s >= rows + DEEP_F:
            inside = inside & (gx < along_x - 1)
        inv = jnp.where(inside, 1.0 / diag, 0.0)
        wy_ref[s] = w_cols
        wz_ref[s] = w_depth
        if DEEP_F <= s < DEEP_F + rows:
            diag_ref[s - DEEP_F] = diag[:cols]
        inv_ref[s] = inv
        v_ref[s] = fx_ref[s] * inv * inv_mid

    def pulled(x_ref, shift, s, span):
        at = s - shift
        total = beside(
            x_ref[at], x_ref[at - 1, :span], x_ref[at + 1, :span],
            wx_ref[s, :span], wx_ref[s + 1, :span], wy_ref[s], wz_ref[s, :span],
        )
        return fx_ref[s, :span] + total

    for s in range(1, tall - 1):
        total = pulled(v_ref, 0, s, wide[0])
        u_ref[s - 1] = (1.0 + keep - push) * v_ref[s] + push * (inv_ref[s] * total)

    def residual(s):
        return pulled(u_ref, 1, s, cols) - diag_ref[s - DEEP_F] * u_ref[s - 1, :cols]

    half_rows = rows // 2
    summed = [residual(2 * i + DEEP_F) + residual(2 * i + 1 + DEEP_F) for i in range(half_rows)]
    summed += [c_ref[2 * i] + c_ref[2 * i + 1] for i in range(half_rows)]
    summed = jnp.concatenate(summed, axis=0)
    pairs = (depth, depth // 2)
    thin = exact_dot(summed, (iota(pairs, 0) // 2 == iota(pairs, 1)).astype(F32))
    choice = (SUB * half_rows, summed.shape[0])
    line, source = iota(choice, 0), iota(choice, 1)
    block, place = line // SUB, line % SUB
    half_cols = cols // 2
    f_half = (place >= half_cols) == odd
    place = place % half_cols
    f_from = cols * block + 2 * place
    c_from = f_from + cols * half_rows
    from_f = (source == f_from) | (source == f_from + 1)
    from_c = (source == c_from) | (source == c_from + 1)
    picker = jnp.where(f_half, jnp.where(from_f, 0.5, 0.0), jnp.where(from_c, 0.125, 0.0))
    tile = exact_dot(picker, thin).reshape(half_rows, SUB, depth // 2)

    def put(i):
        send_ref[pl.ds(i * half_rows, half_rows)] = tile

    each(copies, half_rows, put)


def coarse_and_up(
    along_x, along_y,
    own_ref, other_ref, u0_ref, fx_ref, wx0_ref, wy0_ref, wz0_ref, inv0_ref,
    out_ref,
    f_ref, c_ref, wx_ref, wy_ref, wz_ref, diag_ref, inv_ref, v_ref,
    f2_ref, c2_ref, diag2_ref, d2_ref, e2_ref, e3_ref, a2_ref,
    py_ref, vw_ref, dw_ref, vx_ref, e1_ref, yy_ref, v0_ref, d0_ref, x0_ref,
):
    gx, gy = lax.axis_index("gx"), lax.axis_index("gy")
    odd = lax.rem(gy, 2) == 1
    brick1 = own_ref.shape[0] // (along_x * (along_y // 2))
    rows1, cols1, depth1 = f_ref.shape[0] - 2 * PAD, f_ref.shape[1], f_ref.shape[2]
    across = cols1 // SUB
    registers1 = across * (depth1 // 128)
    shape1 = (cols1, depth1)
    zero1 = jnp.zeros(shape1, F32)
    inv_mid, ((keep, push),) = chebyshev(SMOOTH_LOW, SMOOTH_HIGH, SMOOTH)

    low_half = iota((SUB, depth1), 0) < SUB // 2
    c_ref[PAD - 1] = zero1
    c_ref[PAD + rows1] = zero1

    def place(k):
        x, z = k // across, k % across
        at = z * SUB if isinstance(z, int) else pl.multiple_of(z * SUB, SUB)
        half = brick1 // 2
        for i in range(brick1):
            swapped = odd if i < half else jnp.logical_not(odd)
            low, high = k * brick1 + i % half, k * brick1 + half + i % half
            low = jnp.where(swapped, other_ref[low], own_ref[low])
            high = jnp.where(swapped, other_ref[high], own_ref[high])
            row = PAD + x * brick1 + i
            f_ref[row, pl.ds(at, SUB)] = jnp.where(low_half, low, high)
            c_ref[row, pl.ds(at, SUB)] = turn(jnp.where(low_half, high, low), SUB // 2, 0)

    each(along_x * across, brick1, place)

    wx_ref[PAD] = 0.5 * c_ref[PAD]

    def weigh(c, below, above, shape, stride):
        col, lane = iota(shape, 0), iota(shape, 1)
        half = 0.5 * c
        w_above = half + 0.5 * above
        w_cols = jnp.where(col == shape[0] - 1, 0.0, half + turn(half, -1, 0))
        w_depth = jnp.where(lane >= shape[1] - stride, 0.0, half + turn(half, -stride, 1))
        edge = jnp.where((col == 0) | (col == shape[0] - 1), half, 0.0)
        edge = edge + jnp.where((lane < stride) | (lane >= shape[1] - stride), half, 0.0)
        w_below, w_before, w_back = half + 0.5 * below, turn(w_cols, 1, 0), turn(w_depth, stride, 1)
        diag = w_below + w_above + w_cols + w_before + w_depth + w_back + edge
        return (w_below, w_above, w_cols, w_before, w_depth, w_back), diag, edge

    def weigh1(i):
        row = PAD + i
        (_, w_above, w_cols, _, w_depth, _), diag, _ = weigh(
            c_ref[row], c_ref[row - 1], c_ref[row + 1], shape1, 1
        )
        inv = 1.0 / diag
        wx_ref[row + 1] = w_above
        wy_ref[row] = w_cols
        wz_ref[row] = w_depth
        diag_ref[row] = diag
        inv_ref[row] = inv
        v_ref[row] = f_ref[row] * inv * inv_mid

    v_ref[PAD - 1] = zero1
    v_ref[PAD + rows1] = zero1
    each(rows1, registers1, weigh1)

    rows2, cols2 = rows1 // 2, cols1 // 2
    shape2 = (cols2, depth1)
    registers2 = max(registers1 // 2, 1)
    zero2 = jnp.zeros(shape2, F32)
    lane2, col2 = iota(shape2, 1), iota(shape2, 0)
    even2 = lane2 % 2 == 0

    def fold(ref, row):
        half = ref[row, pl.ds(0, cols2, stride=2), :] + ref[row, pl.ds(1, cols2, stride=2), :]
        return half + jnp.where(even2, turn(half, -1, 1), turn(half, 1, 1))

    def restrict_c(k):
        row = PAD + 2 * k
        c2_ref[k + 1] = 0.125 * (fold(c_ref, row) + fold(c_ref, row + 1))

    each(rows2, 2 * registers1, restrict_c)
    u_ref = c_ref

    def pulled1(x_ref, at, row):
        return f_ref[row] + beside(
            x_ref[at], x_ref[at - 1], x_ref[at + 1],
            wx_ref[row], wx_ref[row + 1], wy_ref[row], wz_ref[row],
        )

    def second1(i):
        row = PAD + i
        total = pulled1(v_ref, row, row)
        u_ref[row] = (1.0 + keep - push) * v_ref[row] + push * (inv_ref[row] * total)

    each(rows1, registers1, second1)

    def residual1(row):
        return pulled1(u_ref, row, row) - diag_ref[row] * u_ref[row]

    def restrict(k):
        row = PAD + 2 * k
        v_ref[k] = residual1(row) + residual1(row + 1)
        f2_ref[k] = 0.5 * fold(v_ref, k)

    each(rows2, 2 * registers1, restrict)
    c2_ref[0] = zero2
    c2_ref[rows2 + 1] = zero2
    for ref in (e2_ref, e3_ref):
        ref[0] = zero2
        ref[rows2 + 1] = zero2
    inv_mid2, pairs2 = chebyshev(COARSE_LOW, COARSE_HIGH, COARSE_STEPS)

    def weigh2(k, edges):
        shares, diag, edge = weigh(c2_ref[k + 1], c2_ref[k], c2_ref[k + 2], shape2, 2)
        inv = 1.0 / diag
        for at, share in enumerate(shares):
            a2_ref[at, k] = share * inv
        diag2_ref[k] = diag
        scaled = f2_ref[k] * inv
        f2_ref[k] = scaled
        d = scaled * inv_mid2
        d2_ref[k] = d
        e2_ref[k + 1] = d
        half = 0.5 * c2_ref[k + 1]
        edge = edge + jnp.where(k == 0, half, 0.0) + jnp.where(k == rows2 - 1, half, 0.0)
        return edges + edge

    edges = each_sum(rows2, registers2, weigh2, zero2)

    def residual2(e_ref, k):
        e = e_ref[k + 1]
        r = f2_ref[k] - e + a2_ref[0, k] * e_ref[k] + a2_ref[1, k] * e_ref[k + 2]
        r = r + (a2_ref[2, k] * turn(e, -1, 0) + a2_ref[3, k] * turn(e, 1, 0))
        return r + (a2_ref[4, k] * turn(e, -2, 1) + a2_ref[5, k] * turn(e, 2, 1))

    now_ref, next_ref = e2_ref, e3_ref
    for keep2, push2 in pairs2:

        def step2(k):
            d = keep2 * d2_ref[k] + push2 * residual2(now_ref, k)
            d2_ref[k] = d
            next_ref[k + 1] = now_ref[k + 1] + d

        each(rows2, registers2, step2)
        now_ref, next_ref = next_ref, now_ref

    def add_residual(k, total):
        return total + diag2_ref[k] * residual2(now_ref, k)

    total = each_sum(rows2, registers2, add_residual, zero2)
    top = jnp.sum(total, axis=(0, 1), keepdims=True)
    bottom = jnp.sum(edges, axis=(0, 1), keepdims=True)
    mean = top / bottom

    span = brick1 + 2 * PAD
    start = gx * brick1 - PAD
    coarse_span = span // 2 + 2
    for k in range(coarse_span):
        row = lax.div(gx * brick1, 2) - PAD // 2 - 1 + k
        good = (row >= 0) & (row < rows2)
        e = now_ref[jnp.clip(row, 0, rows2 - 1) + 1] + mean
        e = jnp.where(good, e, 0.0)
        back = jnp.where(lane2 < 2, 0.0, turn(e, 2, 1))
        ahead = jnp.where(lane2 >= depth1 - 2, 0.0, turn(e, -2, 1))
        e = 0.75 * e + 0.25 * jnp.where(even2, back, ahead)
        back = jnp.where(col2 == 0, 0.0, turn(e, 1, 0))
        ahead = jnp.where(col2 == cols2 - 1, 0.0, turn(e, -1, 0))
        py_ref[k, pl.ds(0, cols2, stride=2), :] = 0.75 * e + 0.25 * back
        py_ref[k, pl.ds(1, cols2, stride=2), :] = 0.75 * e + 0.25 * ahead

    def inside1(m):
        return (start + m >= 0) & (start + m < rows1)

    for m in range(span):
        near = m // 2 + 1
        far = near - 1 if m % 2 == 0 else near + 1
        total = u_ref[PAD + start + m] + (0.75 * py_ref[near] + 0.25 * py_ref[far])
        vw_ref[m] = jnp.where(inside1(m), total, 0.0)
    for m in range(1, span - 1):
        row = PAD + start + m
        v = vw_ref[m]
        d = (inv_ref[row] * pulled1(vw_ref, m, row) - v) * inv_mid
        dw_ref[m] = d
        vx_ref[m] = jnp.where(inside1(m), v + d, 0.0)
    margin = SUB
    e1_ref[:, 0:margin, :] = jnp.zeros((span - 4, margin, depth1), F32)
    e1_ref[:, margin + cols1 :, :] = jnp.zeros((span - 4, margin, depth1), F32)
    for m in range(2, span - 2):
        row = PAD + start + m
        total = inv_ref[row] * pulled1(vx_ref, m, row)
        e = (1.0 - push) * vx_ref[m] + (keep * dw_ref[m] + push * total)
        e1_ref[m - 2, margin : margin + cols1, :] = jnp.where(inside1(m), e, 0.0)

    rows, cols, depth = out_ref.shape
    wide = (cols + 2 * DEEP_C, depth)
    half_wide = wide[0] // 2
    first_col = margin + gy * (cols // 2) - DEEP_C // 2
    for k in range(span - 4):
        e = turn(e1_ref[k, pl.ds(first_col, half_wide), :], -(DEEP_C // 2), 0)
        at = k * wide[0]
        yy_ref[pl.ds(at, half_wide, stride=2), :] = 0.75 * e + 0.25 * turn(e, 1, 0)
        yy_ref[pl.ds(at + 1, half_wide, stride=2), :] = 0.75 * e + 0.25 * turn(e, -1, 0)
    spread = (depth1, depth)
    from_cell, to_cell = iota(spread, 0), iota(spread, 1)
    home = to_cell // 2
    near_cell = jnp.where(to_cell % 2 == 0, home - 1, home + 1)
    weights = jnp.where(from_cell == home, 0.75, 0.0) + jnp.where(from_cell == near_cell, 0.25, 0.0)
    carried = exact_dot(yy_ref[...], weights).reshape(span - 4, wide[0], depth)
    col_inside = inside_cols(iota(wide, 0), cols, along_y)
    for s in range(1, rows + 2 * DEEP_F - 1):
        row = s - DEEP_F
        near = row // 2 + 2
        far = near - 1 if row % 2 == 0 else near + 1
        inside = col_inside
        if row < 0:
            inside = inside & (gx > 0)
        if row >= rows:
            inside = inside & (gx < along_x - 1)
        total = u0_ref[s - 1] + (0.75 * carried[near] + 0.25 * carried[far])
        v0_ref[s] = jnp.where(inside, total, 0.0)

    def pulled0(x_ref, s, span):
        return fx_ref[s, :span] + beside(
            x_ref[s], x_ref[s - 1, :span], x_ref[s + 1, :span],
            wx0_ref[s, :span], wx0_ref[s + 1, :span], wy0_ref[s], wz0_ref[s, :span],
        )

    for s in range(2, rows + 2 * DEEP_F - 2):
        v = v0_ref[s]
        d = (inv0_ref[s] * pulled0(v0_ref, s, wide[0]) - v) * inv_mid
        d0_ref[s] = d[:cols]
        x0_ref[s] = v + d
    for i in range(rows):
        s = i + DEEP_F
        total = inv0_ref[s, :cols] * pulled0(x0_ref, s, cols)
        out_ref[i] = (1.0 - push) * x0_ref[s, :cols] + (keep * d0_ref[s] + push * total)


def pairs_from(first, count):
    swaps = []
    for i in range(first, first + count, 2):
        a, b = i % count, (i + 1) % count
        swaps += [(a, b), (b, a)]
    return swaps


def swaps(along_x, along_y, axis, first):
    pairs = []
    for x in range(along_x):
        for y in range(along_y):
            place, count = (x, along_x) if axis == "gx" else (y, along_y)
            other = place + 1 if (place - first) % 2 == 0 else place - 1
            if 0 <= other < count:
                to = (other, y) if axis == "gx" else (x, other)
            else:
                to = (x, y ^ 1) if axis == "gx" else (x ^ 1, y)
            pairs.append((x * along_y + y, to[0] * along_y + to[1]))
    return pairs


def body(right_side, coefficient):
    along_x, along_y = lax.axis_size("gx"), lax.axis_size("gy")
    rows, cols, depth = right_side.shape
    assert cols == 2 * DEEP_C and rows % 4 == 0 and depth % 256 == 0
    assert along_x % 2 == 0 and along_y % 2 == 0
    small = 16 << 20
    strip = (DEEP_F + DEEP_C, cols, depth)
    odd = lax.rem(lax.axis_index("gx"), 2) == 1
    first = jnp.concatenate([right_side[:DEEP_F], coefficient[:DEEP_C]])
    last = jnp.concatenate([right_side[rows - DEEP_F :], coefficient[rows - DEEP_C :]])
    a, b = jnp.where(odd, first, last), jnp.where(odd, last, first)
    a = lax.ppermute(a, "gx", pairs_from(0, along_x))
    b = lax.ppermute(b, ("gx", "gy"), swaps(along_x, along_y, "gx", 1))

    tall = rows + 2 * DEEP_F
    z, k = call(
        functools.partial(pack_cols, along_x),
        [(rows + 3, cols, depth)] * 2,
        [],
        (right_side, coefficient, a, b),
        small,
    )
    k = lax.ppermute(k, "gy", pairs_from(0, along_y))
    z = lax.ppermute(z, ("gx", "gy"), swaps(along_x, along_y, "gy", 1))

    wide = (cols + 2 * DEEP_C, depth)
    half = (rows // 2, SUB, depth // 2)
    copies = along_x * along_y // 2
    send, *state = call(
        functools.partial(fine_down, along_x, along_y, copies),
        [(copies * half[0],) + half[1:], (tall - 2,) + wide, (tall,) + wide, (tall + 1,) + wide]
        + [(tall,) + wide] * 3,
        [(tall + 2,) + wide, (tall,) + wide, (rows, cols, depth)],
        (right_side, coefficient, a, b, z, k),
        small + 2 * 4 * copies * half[0] * half[1] * half[2],
    )
    own = lax.all_to_all(send, ("gx", "gy"), 0, 0, tiled=True)
    other = lax.ppermute(own, "gy", pairs_from(0, along_y))

    rows1, cols1, depth1 = along_x * half[0], along_y * (cols // 2), half[2]
    whole1 = (rows1 + 2 * PAD + 1, cols1, depth1)
    rows2, cols2 = rows1 // 2, cols1 // 2
    whole2 = (rows2 + 2, cols2, depth1)
    span = half[0] + 2 * PAD
    line = (cols1, depth1)
    scratch = [(rows1 + 2 * PAD,) + line] + [whole1] * 7 + [whole2] * 6 + [(6, rows2) + whole2[1:]]
    scratch += [(span // 2 + 2,) + line] + [(span,) + line] * 3
    scratch += [(span - 4, cols1 + 2 * SUB, depth1), ((span - 4) * wide[0], depth1)]
    scratch += [(tall,) + wide, (tall, cols, depth), (tall,) + wide]
    size = sum(4 * math.prod(s) for s in scratch)
    size += 2 * 4 * own.size + 4 * 8 * tall * wide[0] * wide[1]
    (out,) = call(
        functools.partial(coarse_and_up, along_x, along_y),
        [right_side.shape],
        scratch,
        (own, other, *state),
        size + (12 << 20),
    )
    return out


def solution(mesh):
    placed = (P("gx", "gy", None), P("gx", "gy", None))
    return jax.shard_map(
        body, mesh=mesh, in_specs=placed, out_specs=P("gx", "gy", None), check_vma=False
    )
```

```python
import functools
import math

import jax
import jax.numpy as jnp
from jax import lax
from jax.experimental import pallas as pl
from jax.experimental.pallas import tpu as pltpu
from jax.sharding import PartitionSpec as P

SMOOTH = 2
COARSE_STEPS = 6
SMOOTH_LOW = 0.5
SMOOTH_HIGH = 2.0
COARSE_LOW = 0.05
COARSE_HIGH = 2.0

DEEP_F = 2 * SMOOTH - 1
DEEP_C = 2 * SMOOTH
SUB = 8
PAD = 4
MARGIN = SUB
WRITTEN_OUT = 512

VMEM = pl.BlockSpec(memory_space=pltpu.VMEM)
F32 = jnp.float32


def chebyshev(low_end, high_end, sweeps):
    middle = 0.5 * (high_end + low_end)
    half_span = 0.5 * (high_end - low_end)
    sig_ratio = middle / half_span
    rho_now = 1.0 / sig_ratio
    coeff_pairs = []
    for sweep_num in range(1, sweeps):
        rho_next = 1.0 / (2.0 * sig_ratio - rho_now)
        coeff_pairs.append((rho_next * rho_now, 2.0 * rho_next / half_span))
        rho_now = rho_next
    return (1.0 / middle, coeff_pairs)


def each(count, registers, step):
    each_sum(count, registers, lambda i, carry: (step(i), carry)[1], 0)


def each_sum(count, registers, step, carry):
    if count * registers > WRITTEN_OUT:
        return lax.fori_loop(0, count, step, carry)
    for i in range(count):
        carry = step(i, carry)
    return carry


def turn(value, amount, axis):
    return pltpu.roll(value, amount % value.shape[axis], axis)


def iota(shape, axis):
    return lax.broadcasted_iota(jnp.int32, shape, axis)


def beside(v, below, above, w_below, w_above, w_cols, w_depth):
    span = below.shape[0]
    out = w_above * above + w_below * below
    out = out + w_cols[:span] * turn(v, -1, 0)[:span]
    out = out + turn(w_cols * v, 1, 0)[:span]
    v = v[:span]
    return out + w_depth * turn(v, -1, 1) + turn(w_depth * v, 1, 1)


def inside_cols(col, cols, along_y):
    gy = lax.axis_index("gy")
    after = (col >= cols) & (col < cols + DEEP_C) & (gy == along_y - 1)
    before = (col >= cols + DEEP_C) & (gy == 0)
    return jnp.logical_not(after | before)


def exact_dot(a, b):
    return jnp.dot(a, b, precision=lax.Precision.HIGHEST, preferred_element_type=F32)


def call(kernel, out_shapes, scratch, args, limit):
    return pl.pallas_call(
        kernel,
        out_shape=[jax.ShapeDtypeStruct(s, F32) for s in out_shapes],
        in_specs=[VMEM] * len(args),
        out_specs=[VMEM] * len(out_shapes),
        scratch_shapes=[pltpu.VMEM(s, F32) for s in scratch],
        compiler_params=pltpu.CompilerParams(vmem_limit_bytes=limit),
    )(*args)


def pack_rows(f_ref, c_ref, a_ref, b_ref, sems):
    rows = f_ref.shape[0]
    odd = lax.rem(lax.axis_index("gx"), 2)
    copies = []
    for ref, at_end in ((a_ref, 1 - odd), (b_ref, odd)):
        for whole_ref, first, count in ((f_ref, 0, DEEP_F), (c_ref, DEEP_F, DEEP_C)):
            copies.append(
                pltpu.make_async_copy(
                    whole_ref.at[pl.ds(at_end * (rows - count), count)],
                    ref.at[pl.ds(first, count)],
                    sems.at[len(copies)],
                )
            )
    for copy in copies:
        copy.start()
    for copy in copies:
        copy.wait()


def row_sources(along_x, rows, f_ref, c_ref, a_ref, b_ref):
    gx = lax.axis_index("gx")
    odd = lax.rem(gx, 2) == 1
    has_before = (gx > 0).astype(F32)
    has_after = (gx < along_x - 1).astype(F32)

    def before(i):
        return jnp.where(odd, a_ref[i], b_ref[i]) * has_before

    def after(i):
        return jnp.where(odd, b_ref[i], a_ref[i]) * has_after

    def f_row(i):
        if i < 0:
            return before(DEEP_F + i)
        return f_ref[i] if i < rows else after(i - rows)

    def c_row(i):
        if i < 0:
            return before(DEEP_F + DEEP_C + i)
        return c_ref[i] if i < rows else after(DEEP_F + i - rows)

    return f_row, c_row


def pack_cols(along_x, f_ref, c_ref, a_ref, b_ref, z_ref, k_ref):
    rows = f_ref.shape[0]
    f_row, c_row = row_sources(along_x, rows, f_ref, c_ref, a_ref, b_ref)
    odd = lax.rem(lax.axis_index("gy"), 2) == 1
    sub = iota(f_ref.shape[1:], 0)
    low_half = sub < DEEP_C

    def put(t, first, last):
        z_ref[t] = jnp.where(odd, last, first)
        k_ref[t] = jnp.where(odd, first, last)

    for t in range(rows + 2):
        f, c = turn(f_row(t - 1), DEEP_C, 0), c_row(t - 1)
        put(t, jnp.where(low_half, c, f), jnp.where(low_half, f, c))

    def corners(sub, way):
        near, near_f, far = c_row(-2), f_row(-2), c_row(-3)
        out = jnp.where(sub < 2, near, jnp.where(sub == 2, turn(near_f, 2 * way, 0), turn(far, 3 * way, 0)))
        near, near_f, far = c_row(rows + 1), f_row(rows + 1), c_row(rows + 2)
        out = jnp.where(sub < 4, out, jnp.where(sub < 6, turn(near, 4 * way, 0), turn(near_f, 6 * way, 0)))
        return jnp.where(sub < 7, out, turn(far, 7 * way, 0))

    put(rows + 2, corners(sub, 1), corners(SUB - 1 - sub, -1))


def fine_down(
    along_x, along_y, copies,
    f_ref, c_ref, a_ref, b_ref, z_ref, k_ref,
    send_ref, u_ref, fx_ref, wx_ref, wy_ref, wz_ref, inv_ref,
    cx_ref, v_ref, diag_ref,
):
    rows, cols, depth = f_ref.shape
    f_row, c_row = row_sources(along_x, rows, f_ref, c_ref, a_ref, b_ref)
    gx, gy = lax.axis_index("gx"), lax.axis_index("gy")
    odd = lax.rem(gy, 2) == 1
    has_left = (gy > 0).astype(F32)
    has_right = (gy < along_y - 1).astype(F32)
    low_half = iota((cols, depth), 0) < DEEP_C
    wide = (cols + 2 * DEEP_C, depth)
    lane = iota(wide, 1)
    col = iota(wide, 0)
    col_inside = inside_cols(col, cols, along_y)
    inv_mid, ((keep, push),) = chebyshev(SMOOTH_LOW, SMOOTH_HIGH, SMOOTH)

    def sides(t):
        left = jnp.where(odd, k_ref[t], z_ref[t]) * has_left
        return left, jnp.where(odd, z_ref[t], k_ref[t]) * has_right

    corner_tiles = sides(rows + 2)
    for t in range(rows + 2 * DEEP_C):
        row = t - DEEP_C
        cx_ref[t, 0:cols] = 0.5 * c_row(row)
        s = row + DEEP_F
        if -1 <= row <= rows:
            left, right = sides(row + 1)
            cx_ref[t, cols:] = 0.5 * jnp.where(low_half, right, left)
            f = turn(jnp.where(low_half, left, right), DEEP_C, 0)
        else:
            left, right = corner_tiles
            c_turn = {-2: 0, -3: 3, rows + 1: 4, rows + 2: 7}.get(row)
            f_turn = {-2: 2, rows + 1: 6}.get(row)
            c = f = jnp.zeros((cols, depth), F32)
            if c_turn is not None:
                c = jnp.where(low_half, turn(right, -c_turn, 0), turn(left, c_turn, 0))
            if f_turn is not None:
                f = jnp.where(low_half, turn(right, -f_turn, 0), turn(left, f_turn, 0))
            cx_ref[t, cols:] = 0.5 * c
        if 0 <= s < rows + 2 * DEEP_F:
            fx_ref[s, 0:cols] = f_row(row)
            fx_ref[s, cols:] = f

    tall = rows + 2 * DEEP_F
    wx_ref[0] = cx_ref[0] + cx_ref[1]
    for s in range(tall):
        half = cx_ref[s + 1]
        above = half + cx_ref[s + 2]
        after = half + turn(half, -1, 0)
        deeper = jnp.where(lane == depth - 1, 0.0, half + turn(half, -1, 1))
        wx_ref[s + 1] = above
        wy_ref[s] = after
        wz_ref[s] = deeper
        diag = wx_ref[s] + above + after + turn(after, 1, 0) + deeper + turn(deeper, 1, 1)
        diag = diag + jnp.where((lane == 0) | (lane == depth - 1), half, 0.0)
        inside = col_inside
        if s < DEEP_F:
            inside = inside & (gx > 0)
        if s >= rows + DEEP_F:
            inside = inside & (gx < along_x - 1)
        inv = jnp.where(inside, 1.0 / diag, 0.0)
        if DEEP_F <= s < DEEP_F + rows:
            diag_ref[s - DEEP_F] = diag[:cols]
        inv_ref[s] = inv
        v_ref[s] = fx_ref[s] * inv * inv_mid

    def pulled(x_ref, shift, s, span):
        at = s - shift
        total = beside(
            x_ref[at], x_ref[at - 1, :span], x_ref[at + 1, :span],
            wx_ref[s, :span], wx_ref[s + 1, :span], wy_ref[s], wz_ref[s, :span],
        )
        return fx_ref[s, :span] + total

    for s in range(1, tall - 1):
        total = pulled(v_ref, 0, s, wide[0])
        u_ref[s - 1] = (1.0 + keep - push) * v_ref[s] + push * (inv_ref[s] * total)

    def residual(s):
        return pulled(u_ref, 1, s, cols) - diag_ref[s - DEEP_F] * u_ref[s - 1, :cols]

    half_rows = rows // 2
    summed = [residual(2 * i + DEEP_F) + residual(2 * i + 1 + DEEP_F) for i in range(half_rows)]
    summed += [c_ref[2 * i] + c_ref[2 * i + 1] for i in range(half_rows)]
    summed = jnp.concatenate(summed, axis=0)
    pairs = (depth, depth // 2)
    thin = exact_dot(summed, (iota(pairs, 0) // 2 == iota(pairs, 1)).astype(F32))
    choice = (SUB * half_rows, summed.shape[0])
    line, source = iota(choice, 0), iota(choice, 1)
    block, place = line // SUB, line % SUB
    half_cols = cols // 2
    f_half = (place >= half_cols) == odd
    place = place % half_cols
    f_from = cols * block + 2 * place
    c_from = f_from + cols * half_rows
    from_f = (source == f_from) | (source == f_from + 1)
    from_c = (source == c_from) | (source == c_from + 1)
    picker = jnp.where(f_half, jnp.where(from_f, 0.5, 0.0), jnp.where(from_c, 0.0625, 0.0))
    tile = exact_dot(picker, thin).reshape(half_rows, SUB, depth // 2)

    def put(i):
        send_ref[pl.ds(i * half_rows, half_rows)] = tile

    each(copies, half_rows, put)


def coarse_and_up(
    along_x, along_y,
    own_ref, other_ref, u0_ref, fx_ref, wx0_ref, wy0_ref, wz0_ref, inv0_ref,
    out_ref,
    f_ref, h_ref, wx_ref, wy_ref, wz_ref, inv_ref, v_ref, diag_ref,
    f2_ref, h2_ref, e2_ref, e3_ref, py_ref, vw_ref, dw_ref, vx_ref, e1_ref, yy_ref, v0_ref, d0_ref, x0_ref,
):
    gx, gy = lax.axis_index("gx"), lax.axis_index("gy")
    odd = lax.rem(gy, 2) == 1
    brick1 = own_ref.shape[0] // (along_x * (along_y // 2))
    rows1, cols1, depth1 = diag_ref.shape
    across = cols1 // SUB
    registers1 = across * (depth1 // 128)
    inv_mid, ((keep, push),) = chebyshev(SMOOTH_LOW, SMOOTH_HIGH, SMOOTH)
    inner = pl.ds(MARGIN, cols1)

    low_half = iota((SUB, depth1), 0) < SUB // 2

    def place(k):
        x, z = k // across, k % across
        at = z * SUB + MARGIN
        if not isinstance(z, int):
            at = pl.multiple_of(at, SUB)
        half = brick1 // 2
        for i in range(brick1):
            swapped = odd if i < half else jnp.logical_not(odd)
            low, high = k * brick1 + i % half, k * brick1 + half + i % half
            low = jnp.where(swapped, other_ref[low], own_ref[low])
            high = jnp.where(swapped, other_ref[high], own_ref[high])
            row = PAD + x * brick1 + i
            f_ref[row, pl.ds(at, SUB)] = jnp.where(low_half, low, high)
            h_ref[row, pl.ds(at, SUB)] = turn(jnp.where(low_half, high, low), SUB // 2, 0)

    each(along_x * across, brick1, place)

    def clear_beside(ref, row):
        zero = jnp.zeros((MARGIN, depth1), F32)
        ref[row, 0:MARGIN] = zero
        ref[row, pl.ds(ref.shape[1] - MARGIN, MARGIN)] = zero

    def clear(i):
        for ref in (h_ref, v_ref):
            clear_beside(ref, PAD + i)
        wy_ref[PAD + i, 0:MARGIN] = jnp.zeros((MARGIN, depth1), F32)

    each(rows1, 1, clear)
    for ref in (h_ref, v_ref):
        for row in (PAD - 1, PAD + rows1):
            ref[row] = jnp.zeros(ref.shape[1:], F32)

    def weigh(ref, row, cols, stride):
        half = ref[row, pl.ds(MARGIN, cols)]
        lane = iota(half.shape, 1)
        first, last = lane < stride, lane >= half.shape[1] - stride
        around = [ref[row - 1, pl.ds(MARGIN, cols)], ref[row + 1, pl.ds(MARGIN, cols)]]
        around += [ref[row, pl.ds(MARGIN - 1, cols)], ref[row, pl.ds(MARGIN + 1, cols)]]
        around += [
            jnp.where(first, 0.0, turn(half, stride, 1)),
            jnp.where(last, 0.0, turn(half, -stride, 1)),
        ]
        total = (around[0] + around[1]) + (around[2] + around[3]) + (around[4] + around[5])
        return half, around, 6.0 * half + total, first, last

    wx_ref[PAD, inner] = h_ref[PAD, inner]

    def weigh1(i):
        row = PAD + i
        half, around, diag, _, last = weigh(h_ref, row, cols1, 1)
        inv = 1.0 / diag
        wx_ref[row + 1, inner] = half + around[1]
        wy_ref[row, inner] = half + around[3]
        wz_ref[row, inner] = jnp.where(last, 0.0, half + around[5])
        diag_ref[i] = diag
        inv_ref[row, inner] = inv
        v_ref[row, inner] = f_ref[row, inner] * inv * inv_mid

    each(rows1, registers1, weigh1)

    rows2, cols2 = rows1 // 2, cols1 // 2
    shape2 = (cols2, depth1)
    registers2 = max(registers1 // 2, 1)
    zero2 = jnp.zeros(shape2, F32)
    lane2, col2 = iota(shape2, 1), iota(shape2, 0)
    even2 = lane2 % 2 == 0
    inner2 = pl.ds(MARGIN, cols2)

    def fold(ref, row):
        half = ref[row, pl.ds(MARGIN, cols2, stride=2), :] + ref[row, pl.ds(MARGIN + 1, cols2, stride=2), :]
        return half + turn(half, -1, 1)

    def restrict_h(k):
        row = PAD + 2 * k
        h2_ref[k + 1, inner2] = 0.125 * (fold(h_ref, row) + fold(h_ref, row + 1))

    each(rows2, 2 * registers1, restrict_h)
    u_ref = h_ref

    def pulled1(x_ref, at, x_first, row, first, count):
        def part(ref, i, begin, shift=0):
            return ref[i, pl.ds(begin + shift, count), :]

        x, depths = part(x_ref, at, x_first), part(wz_ref, row, first)
        total = part(wx_ref, row + 1, first) * part(x_ref, at + 1, x_first)
        total = total + part(wx_ref, row, first) * part(x_ref, at - 1, x_first)
        total = total + part(wy_ref, row, first) * part(x_ref, at, x_first, 1)
        total = total + part(wy_ref, row, first, -1) * part(x_ref, at, x_first, -1)
        total = total + depths * turn(x, -1, 1) + turn(depths * x, 1, 1)
        return x, part(f_ref, row, first) + total

    def second1(i):
        row = PAD + i
        v, total = pulled1(v_ref, row, MARGIN, row, MARGIN, cols1)
        u_ref[row, inner] = (1.0 + keep - push) * v + push * (inv_ref[row, inner] * total)

    each(rows1, registers1, second1)

    def residual1(i):
        u, total = pulled1(u_ref, PAD + i, MARGIN, PAD + i, MARGIN, cols1)
        return total - diag_ref[i] * u

    def restrict(k):
        v_ref[k, inner] = residual1(2 * k) + residual1(2 * k + 1)
        f2_ref[k] = 0.5 * fold(v_ref, k)

    each(rows2, 2 * registers1, restrict)
    for ref in (h2_ref, e2_ref, e3_ref):
        for row in (0, rows2 + 1):
            ref[row] = jnp.zeros(ref.shape[1:], F32)

    def clear2(k):
        for ref in (h2_ref, e2_ref, e3_ref):
            clear_beside(ref, k + 1)

    each(rows2, 1, clear2)
    inv_mid2, pairs2 = chebyshev(COARSE_LOW, COARSE_HIGH, COARSE_STEPS)

    def kept(at, k):
        ref, at, begin = (diag_ref, at, 0) if at < 4 else (v_ref, at - 4, MARGIN)
        return ref, 2 * k + at // 2, pl.ds(begin + at % 2 * cols2, cols2)

    def keep_value(at, k, value):
        ref, row, columns = kept(at, k)
        ref[row, columns] = value

    def kept_value(at, k):
        ref, row, columns = kept(at, k)
        return ref[row, columns]

    diagonal, direction = 6, 7

    def weigh2(k, edges):
        half, around, diag, first, last = weigh(h2_ref, k + 1, cols2, 2)
        inv = 1.0 / diag
        scaled = half * inv
        for at in range(4):
            keep_value(at, k, scaled + around[at] * inv)
        keep_value(4, k, jnp.where(first, 0.0, scaled + around[4] * inv))
        keep_value(5, k, jnp.where(last, 0.0, scaled + around[5] * inv))
        keep_value(diagonal, k, diag)
        f = f2_ref[k] * inv
        f2_ref[k] = f
        d = f * inv_mid2
        keep_value(direction, k, d)
        e2_ref[k + 1, inner2] = d
        edges = edges + jnp.where((col2 == 0) | (col2 == cols2 - 1), half, 0.0)
        edges = edges + jnp.where(first | last, half, 0.0)
        return edges + jnp.where(k == 0, half, 0.0) + jnp.where(k == rows2 - 1, half, 0.0)

    edges = each_sum(rows2, registers2, weigh2, zero2)

    def residual2(e_ref, k):
        e = e_ref[k + 1, inner2]
        r = f2_ref[k] - e + kept_value(0, k) * e_ref[k, inner2] + kept_value(1, k) * e_ref[k + 2, inner2]
        r = r + kept_value(2, k) * e_ref[k + 1, pl.ds(MARGIN - 1, cols2)]
        r = r + kept_value(3, k) * e_ref[k + 1, pl.ds(MARGIN + 1, cols2)]
        return e, r + (kept_value(4, k) * turn(e, 2, 1) + kept_value(5, k) * turn(e, -2, 1))

    now_ref, next_ref = e2_ref, e3_ref
    for keep2, push2 in pairs2:

        def step2(k):
            e, r = residual2(now_ref, k)
            d = keep2 * kept_value(direction, k) + push2 * r
            keep_value(direction, k, d)
            next_ref[k + 1, inner2] = e + d

        each(rows2, registers2, step2)
        now_ref, next_ref = next_ref, now_ref

    def add_residual(k, total):
        return total + kept_value(diagonal, k) * residual2(now_ref, k)[1]

    total = each_sum(rows2, registers2, add_residual, zero2)
    top = jnp.sum(jnp.where(even2, total, 0.0), axis=(0, 1), keepdims=True)
    bottom = jnp.sum(jnp.where(even2, edges, 0.0), axis=(0, 1), keepdims=True)
    mean = top / bottom

    span, broad = brick1 + 2 * PAD, 2 * SUB
    start, first_col = gx * brick1 - PAD, gy * (cols1 // along_y) - PAD
    coarse_span = span // 2 + 2
    for k in range(coarse_span):
        row = lax.div(gx * brick1, 2) - PAD // 2 - 1 + k
        good = (row >= 0) & (row < rows2)
        e = now_ref[jnp.clip(row, 0, rows2 - 1) + 1, inner2] + mean
        e = jnp.where(good, e, 0.0)
        back = jnp.where(lane2 < 2, 0.0, turn(e, 2, 1))
        ahead = jnp.where(lane2 >= depth1 - 2, 0.0, turn(e, -1, 1))
        home = jnp.where(even2, e, turn(e, 1, 1))
        e = 0.75 * home + 0.25 * jnp.where(even2, back, ahead)
        back = jnp.where(col2 == 0, 0.0, turn(e, 1, 0))
        ahead = jnp.where(col2 == cols2 - 1, 0.0, turn(e, -1, 0))
        py_ref[k, pl.ds(MARGIN, cols2, stride=2), :] = 0.75 * e + 0.25 * back
        py_ref[k, pl.ds(MARGIN + 1, cols2, stride=2), :] = 0.75 * e + 0.25 * ahead

    window, held = pl.ds(MARGIN + first_col, broad), pl.ds(MARGIN, broad)
    col1 = first_col + iota((broad, depth1), 0)
    col_good = (col1 >= 0) & (col1 < cols1)

    def inside1(m):
        return col_good & ((start + m >= 0) & (start + m < rows1))

    for m in range(span):
        near = m // 2 + 1
        far = near - 1 if m % 2 == 0 else near + 1
        total = u_ref[PAD + start + m, window, :]
        total = total + (0.75 * py_ref[near, window, :] + 0.25 * py_ref[far, window, :])
        vw_ref[m, held] = jnp.where(inside1(m), total, 0.0)
    for m in range(1, span - 1):
        row = PAD + start + m
        v, total = pulled1(vw_ref, m, MARGIN, row, MARGIN + first_col, broad)
        d = (inv_ref[row, window, :] * total - v) * inv_mid
        dw_ref[m] = d
        vx_ref[m, held] = jnp.where(inside1(m), v + d, 0.0)
    for m in range(2, span - 2):
        row = PAD + start + m
        v, total = pulled1(vx_ref, m, MARGIN, row, MARGIN + first_col, broad)
        e = (1.0 - push) * v + (keep * dw_ref[m] + push * (inv_ref[row, window, :] * total))
        e1_ref[m - 2] = jnp.where(inside1(m), e, 0.0)

    rows, cols, depth = out_ref.shape
    wide = (cols + 2 * DEEP_C, depth)
    half_wide = wide[0] // 2
    for k in range(span - 4):
        e = turn(e1_ref[k, pl.ds(PAD - DEEP_C // 2, half_wide), :], -(DEEP_C // 2), 0)
        at = k * wide[0]
        yy_ref[pl.ds(at, half_wide, stride=2), :] = 0.75 * e + 0.25 * turn(e, 1, 0)
        yy_ref[pl.ds(at + 1, half_wide, stride=2), :] = 0.75 * e + 0.25 * turn(e, -1, 0)
    spread = (depth1, depth)
    from_cell, to_cell = iota(spread, 0), iota(spread, 1)
    home = to_cell // 2
    near_cell = jnp.where(to_cell % 2 == 0, home - 1, home + 1)
    weights = jnp.where(from_cell == home, 0.75, 0.0) + jnp.where(from_cell == near_cell, 0.25, 0.0)
    carried = exact_dot(yy_ref[...], weights).reshape(span - 4, wide[0], depth)
    col_inside = inside_cols(iota(wide, 0), cols, along_y)
    for s in range(1, rows + 2 * DEEP_F - 1):
        row = s - DEEP_F
        near = row // 2 + 2
        far = near - 1 if row % 2 == 0 else near + 1
        inside = col_inside
        if row < 0:
            inside = inside & (gx > 0)
        if row >= rows:
            inside = inside & (gx < along_x - 1)
        total = u0_ref[s - 1] + (0.75 * carried[near] + 0.25 * carried[far])
        v0_ref[s] = jnp.where(inside, total, 0.0)

    def pulled0(x_ref, s, span):
        return fx_ref[s, :span] + beside(
            x_ref[s], x_ref[s - 1, :span], x_ref[s + 1, :span],
            wx0_ref[s, :span], wx0_ref[s + 1, :span], wy0_ref[s], wz0_ref[s, :span],
        )

    for s in range(2, rows + 2 * DEEP_F - 2):
        v = v0_ref[s]
        d = (inv0_ref[s] * pulled0(v0_ref, s, wide[0]) - v) * inv_mid
        d0_ref[s] = d[:cols]
        x0_ref[s] = v + d
    for i in range(rows):
        s = i + DEEP_F
        total = inv0_ref[s, :cols] * pulled0(x0_ref, s, cols)
        out_ref[i] = (1.0 - push) * x0_ref[s, :cols] + (keep * d0_ref[s] + push * total)


def pairs_from(first, count):
    swaps = []
    for i in range(first, first + count, 2):
        a, b = i % count, (i + 1) % count
        swaps += [(a, b), (b, a)]
    return swaps


def swaps(along_x, along_y, axis, first):
    pairs = []
    for x in range(along_x):
        for y in range(along_y):
            place, count = (x, along_x) if axis == "gx" else (y, along_y)
            other = place + 1 if (place - first) % 2 == 0 else place - 1
            if 0 <= other < count:
                to = (other, y) if axis == "gx" else (x, other)
            else:
                to = (x, y ^ 1) if axis == "gx" else (x ^ 1, y)
            pairs.append((x * along_y + y, to[0] * along_y + to[1]))
    return pairs


def body(right_side, coefficient):
    along_x, along_y = lax.axis_size("gx"), lax.axis_size("gy")
    rows, cols, depth = right_side.shape
    assert cols == 2 * DEEP_C and rows % 4 == 0 and depth % 256 == 0
    assert along_x % 2 == 0 and along_y % 2 == 0
    small = 16 << 20
    strip = (DEEP_F + DEEP_C, cols, depth)
    odd = lax.rem(lax.axis_index("gx"), 2) == 1
    first = jnp.concatenate([right_side[:DEEP_F], coefficient[:DEEP_C]])
    last = jnp.concatenate([right_side[rows - DEEP_F :], coefficient[rows - DEEP_C :]])
    a, b = jnp.where(odd, first, last), jnp.where(odd, last, first)
    a = lax.ppermute(a, "gx", pairs_from(0, along_x))
    b = lax.ppermute(b, ("gx", "gy"), swaps(along_x, along_y, "gx", 1))

    tall = rows + 2 * DEEP_F
    z, k = call(
        functools.partial(pack_cols, along_x),
        [(rows + 3, cols, depth)] * 2,
        [],
        (right_side, coefficient, a, b),
        small,
    )
    k = lax.ppermute(k, "gy", pairs_from(0, along_y))
    z = lax.ppermute(z, ("gx", "gy"), swaps(along_x, along_y, "gy", 1))

    wide = (cols + 2 * DEEP_C, depth)
    half = (rows // 2, SUB, depth // 2)
    copies = along_x * along_y // 2
    send, *state = call(
        functools.partial(fine_down, along_x, along_y, copies),
        [(copies * half[0],) + half[1:], (tall - 2,) + wide, (tall,) + wide, (tall + 1,) + wide]
        + [(tall,) + wide] * 3,
        [(tall + 2,) + wide, (tall,) + wide, (rows, cols, depth)],
        (right_side, coefficient, a, b, z, k),
        small + 2 * 4 * copies * half[0] * half[1] * half[2],
    )
    own = lax.all_to_all(send, ("gx", "gy"), 0, 0, tiled=True)
    other = lax.ppermute(own, "gy", pairs_from(0, along_y))

    rows1, cols1, depth1 = along_x * half[0], along_y * (cols // 2), half[2]
    whole1 = (rows1 + 2 * PAD + 1, cols1 + 2 * MARGIN, depth1)
    rows2, cols2 = rows1 // 2, cols1 // 2
    whole2 = (rows2 + 2, cols2 + 2 * MARGIN, depth1)
    span, broad = half[0] + 2 * PAD, 2 * SUB
    window = (span, broad + 2 * MARGIN, depth1)
    scratch = [whole1] * 7 + [(rows1, cols1, depth1)]
    scratch += [(rows2, cols2, depth1)] + [whole2] * 3
    scratch += [(span // 2 + 2,) + whole1[1:], window, (span, broad, depth1), window]
    scratch += [(span - 4, broad, depth1), ((span - 4) * wide[0], depth1)]
    scratch += [(tall,) + wide, (tall, cols, depth), (tall,) + wide]
    size = sum(4 * math.prod(s) for s in scratch)
    size += 2 * 4 * own.size + 4 * 8 * tall * wide[0] * wide[1]
    (out,) = call(
        functools.partial(coarse_and_up, along_x, along_y),
        [right_side.shape],
        scratch,
        (own, other, *state),
        size + (12 << 20),
    )
    return out


def solution(mesh):
    placed = (P("gx", "gy", None), P("gx", "gy", None))
    return jax.shard_map(
        body, mesh=mesh, in_specs=placed, out_specs=P("gx", "gy", None), check_vma=False
    )
```

```python
import functools
import math

import jax
import jax.numpy as jnp
from jax import lax
from jax.experimental import pallas as pl
from jax.experimental.pallas import tpu as pltpu
from jax.sharding import PartitionSpec as P

SMOOTH = 2
COARSE_STEPS = 6
SMOOTH_LOW = 0.5
SMOOTH_HIGH = 2.0
COARSE_LOW = 0.05
COARSE_HIGH = 2.0

DEEP_F = 2 * SMOOTH - 1
DEEP_C = 2 * SMOOTH
SUB = 8
PAD = 4
MARGIN = SUB
WRITTEN_OUT = 512

VMEM = pl.BlockSpec(memory_space=pltpu.VMEM)
F32 = jnp.float32


def chebyshev(low_end, high_end, sweeps):
    middle = 0.5 * (high_end + low_end)
    half_span = 0.5 * (high_end - low_end)
    sig_ratio = middle / half_span
    rho_now = 1.0 / sig_ratio
    coeff_pairs = []
    for sweep_num in range(1, sweeps):
        rho_next = 1.0 / (2.0 * sig_ratio - rho_now)
        coeff_pairs.append((rho_next * rho_now, 2.0 * rho_next / half_span))
        rho_now = rho_next
    return (1.0 / middle, coeff_pairs)


def each(count, registers, step):
    each_sum(count, registers, lambda i, carry: (step(i), carry)[1], 0)


def each_sum(count, registers, step, carry):
    if count * registers > WRITTEN_OUT:
        return lax.fori_loop(0, count, step, carry)
    for i in range(count):
        carry = step(i, carry)
    return carry


def turn(value, amount, axis):
    return pltpu.roll(value, amount % value.shape[axis], axis)


def iota(shape, axis):
    return lax.broadcasted_iota(jnp.int32, shape, axis)


def beside(v, below, above, w_below, w_above, w_cols, w_depth):
    span = below.shape[0]
    out = w_above * above + w_below * below
    out = out + w_cols[:span] * turn(v, -1, 0)[:span]
    out = out + turn(w_cols * v, 1, 0)[:span]
    v = v[:span]
    return out + w_depth * turn(v, -1, 1) + turn(w_depth * v, 1, 1)


def inside_cols(col, cols, along_y):
    gy = lax.axis_index("gy")
    after = (col >= cols) & (col < cols + DEEP_C) & (gy == along_y - 1)
    before = (col >= cols + DEEP_C) & (gy == 0)
    return jnp.logical_not(after | before)


def exact_dot(a, b):
    return jnp.dot(a, b, precision=lax.Precision.HIGHEST, preferred_element_type=F32)


def call(kernel, out_shapes, scratch, args, limit):
    return pl.pallas_call(
        kernel,
        out_shape=[jax.ShapeDtypeStruct(s, F32) for s in out_shapes],
        in_specs=[VMEM] * len(args),
        out_specs=[VMEM] * len(out_shapes),
        scratch_shapes=[pltpu.VMEM(s, F32) for s in scratch],
        compiler_params=pltpu.CompilerParams(vmem_limit_bytes=limit),
    )(*args)


def pack_rows(f_ref, c_ref, a_ref, b_ref, sems):
    rows = f_ref.shape[0]
    odd = lax.rem(lax.axis_index("gx"), 2)
    copies = []
    for ref, at_end in ((a_ref, 1 - odd), (b_ref, odd)):
        for whole_ref, first, count in ((f_ref, 0, DEEP_F), (c_ref, DEEP_F, DEEP_C)):
            copies.append(
                pltpu.make_async_copy(
                    whole_ref.at[pl.ds(at_end * (rows - count), count)],
                    ref.at[pl.ds(first, count)],
                    sems.at[len(copies)],
                )
            )
    for copy in copies:
        copy.start()
    for copy in copies:
        copy.wait()


def row_sources(along_x, rows, f_ref, c_ref, a_ref, b_ref):
    gx = lax.axis_index("gx")
    odd = lax.rem(gx, 2) == 1
    has_before = (gx > 0).astype(F32)
    has_after = (gx < along_x - 1).astype(F32)

    def before(i):
        return jnp.where(odd, a_ref[i], b_ref[i]) * has_before

    def after(i):
        return jnp.where(odd, b_ref[i], a_ref[i]) * has_after

    def f_row(i):
        if i < 0:
            return before(DEEP_F + i)
        return f_ref[i] if i < rows else after(i - rows)

    def c_row(i):
        if i < 0:
            return before(DEEP_F + DEEP_C + i)
        return c_ref[i] if i < rows else after(DEEP_F + i - rows)

    return f_row, c_row


def pack_cols(along_x, f_ref, c_ref, a_ref, b_ref, z_ref, k_ref):
    rows = f_ref.shape[0]
    f_row, c_row = row_sources(along_x, rows, f_ref, c_ref, a_ref, b_ref)
    odd = lax.rem(lax.axis_index("gy"), 2) == 1
    sub = iota(f_ref.shape[1:], 0)
    low_half = sub < DEEP_C

    def put(t, first, last):
        z_ref[t] = jnp.where(odd, last, first)
        k_ref[t] = jnp.where(odd, first, last)

    for t in range(rows + 2):
        f, c = turn(f_row(t - 1), DEEP_C, 0), c_row(t - 1)
        put(t, jnp.where(low_half, c, f), jnp.where(low_half, f, c))

    def corners(sub, way):
        near, near_f, far = c_row(-2), f_row(-2), c_row(-3)
        out = jnp.where(sub < 2, near, jnp.where(sub == 2, turn(near_f, 2 * way, 0), turn(far, 3 * way, 0)))
        near, near_f, far = c_row(rows + 1), f_row(rows + 1), c_row(rows + 2)
        out = jnp.where(sub < 4, out, jnp.where(sub < 6, turn(near, 4 * way, 0), turn(near_f, 6 * way, 0)))
        return jnp.where(sub < 7, out, turn(far, 7 * way, 0))

    put(rows + 2, corners(sub, 1), corners(SUB - 1 - sub, -1))


def line_up(axis, *refs):
    *block_refs, out_ref = refs
    here = lax.axis_index("gx") if axis == "gx" else lax.div(lax.axis_index("gy"), 2)
    size = block_refs[0].shape[0]
    for distance, ref in enumerate(block_refs):
        out_ref[pl.ds((here ^ distance) * size, size)] = ref[...]


def fine_down(
    along_x, along_y,
    f_ref, c_ref, a_ref, b_ref, z_ref, k_ref,
    send_ref, u_ref, fx_ref, wx_ref, wy_ref, wz_ref, inv_ref,
    cx_ref, v_ref, diag_ref,
):
    rows, cols, depth = f_ref.shape
    f_row, c_row = row_sources(along_x, rows, f_ref, c_ref, a_ref, b_ref)
    gx, gy = lax.axis_index("gx"), lax.axis_index("gy")
    odd = lax.rem(gy, 2) == 1
    has_left = (gy > 0).astype(F32)
    has_right = (gy < along_y - 1).astype(F32)
    low_half = iota((cols, depth), 0) < DEEP_C
    wide = (cols + 2 * DEEP_C, depth)
    lane = iota(wide, 1)
    col = iota(wide, 0)
    col_inside = inside_cols(col, cols, along_y)
    inv_mid, ((keep, push),) = chebyshev(SMOOTH_LOW, SMOOTH_HIGH, SMOOTH)

    def sides(t):
        left = jnp.where(odd, k_ref[t], z_ref[t]) * has_left
        return left, jnp.where(odd, z_ref[t], k_ref[t]) * has_right

    corner_tiles = sides(rows + 2)
    for t in range(rows + 2 * DEEP_C):
        row = t - DEEP_C
        cx_ref[t, 0:cols] = 0.5 * c_row(row)
        s = row + DEEP_F
        if -1 <= row <= rows:
            left, right = sides(row + 1)
            cx_ref[t, cols:] = 0.5 * jnp.where(low_half, right, left)
            f = turn(jnp.where(low_half, left, right), DEEP_C, 0)
        else:
            left, right = corner_tiles
            c_turn = {-2: 0, -3: 3, rows + 1: 4, rows + 2: 7}.get(row)
            f_turn = {-2: 2, rows + 1: 6}.get(row)
            c = f = jnp.zeros((cols, depth), F32)
            if c_turn is not None:
                c = jnp.where(low_half, turn(right, -c_turn, 0), turn(left, c_turn, 0))
            if f_turn is not None:
                f = jnp.where(low_half, turn(right, -f_turn, 0), turn(left, f_turn, 0))
            cx_ref[t, cols:] = 0.5 * c
        if 0 <= s < rows + 2 * DEEP_F:
            fx_ref[s, 0:cols] = f_row(row)
            fx_ref[s, cols:] = f

    tall = rows + 2 * DEEP_F
    wx_ref[0] = cx_ref[0] + cx_ref[1]
    for s in range(tall):
        half = cx_ref[s + 1]
        above = half + cx_ref[s + 2]
        after = half + turn(half, -1, 0)
        deeper = jnp.where(lane == depth - 1, 0.0, half + turn(half, -1, 1))
        wx_ref[s + 1] = above
        wy_ref[s] = after
        wz_ref[s] = deeper
        diag = wx_ref[s] + above + after + turn(after, 1, 0) + deeper + turn(deeper, 1, 1)
        diag = diag + jnp.where((lane == 0) | (lane == depth - 1), half, 0.0)
        inside = col_inside
        if s < DEEP_F:
            inside = inside & (gx > 0)
        if s >= rows + DEEP_F:
            inside = inside & (gx < along_x - 1)
        inv = jnp.where(inside, 1.0 / diag, 0.0)
        if DEEP_F <= s < DEEP_F + rows:
            diag_ref[s - DEEP_F] = diag[:cols]
        inv_ref[s] = inv
        v_ref[s] = fx_ref[s] * inv * inv_mid

    def pulled(x_ref, shift, s, span):
        at = s - shift
        total = beside(
            x_ref[at], x_ref[at - 1, :span], x_ref[at + 1, :span],
            wx_ref[s, :span], wx_ref[s + 1, :span], wy_ref[s], wz_ref[s, :span],
        )
        return fx_ref[s, :span] + total

    for s in range(1, tall - 1):
        total = pulled(v_ref, 0, s, wide[0])
        u_ref[s - 1] = (1.0 + keep - push) * v_ref[s] + push * (inv_ref[s] * total)

    def residual(s):
        return pulled(u_ref, 1, s, cols) - diag_ref[s - DEEP_F] * u_ref[s - 1, :cols]

    half_rows = rows // 2
    summed = [residual(2 * i + DEEP_F) + residual(2 * i + 1 + DEEP_F) for i in range(half_rows)]
    summed += [c_ref[2 * i] + c_ref[2 * i + 1] for i in range(half_rows)]
    summed = jnp.concatenate(summed, axis=0)
    pairs = (depth, depth // 2)
    thin = exact_dot(summed, (iota(pairs, 0) // 2 == iota(pairs, 1)).astype(F32))
    choice = (SUB * half_rows, summed.shape[0])
    line, source = iota(choice, 0), iota(choice, 1)
    block, place = line // SUB, line % SUB
    half_cols = cols // 2
    f_half = (place >= half_cols) == odd
    place = place % half_cols
    f_from = cols * block + 2 * place
    c_from = f_from + cols * half_rows
    from_f = (source == f_from) | (source == f_from + 1)
    from_c = (source == c_from) | (source == c_from + 1)
    picker = jnp.where(f_half, jnp.where(from_f, 0.5, 0.0), jnp.where(from_c, 0.0625, 0.0))
    tile = exact_dot(picker, thin).reshape(half_rows, SUB, depth // 2)

    send_ref[...] = tile


def coarse_and_up(
    along_x, along_y,
    own_ref, other_ref, u0_ref, fx_ref, wx0_ref, wy0_ref, wz0_ref, inv0_ref,
    out_ref,
    f_ref, h_ref, wx_ref, wy_ref, wz_ref, inv_ref, v_ref, diag_ref,
    f2_ref, h2_ref, e2_ref, e3_ref, py_ref, vw_ref, dw_ref, vx_ref, e1_ref, yy_ref, v0_ref, d0_ref, x0_ref,
):
    gx, gy = lax.axis_index("gx"), lax.axis_index("gy")
    odd = lax.rem(gy, 2) == 1
    brick1 = own_ref.shape[0] // (along_x * (along_y // 2))
    rows1, cols1, depth1 = diag_ref.shape
    across = cols1 // SUB
    registers1 = across * (depth1 // 128)
    inv_mid, ((keep, push),) = chebyshev(SMOOTH_LOW, SMOOTH_HIGH, SMOOTH)
    inner = pl.ds(MARGIN, cols1)

    low_half = iota((SUB, depth1), 0) < SUB // 2

    chip = lax.div(gy, 2)

    def place(k):
        x, z = k // across, k % across
        at = z * SUB + MARGIN
        if not isinstance(z, int):
            at = pl.multiple_of(at, SUB)
        swapped = odd == (z == chip)
        for i in range(brick1):
            own, other = own_ref[k * brick1 + i], other_ref[k * brick1 + i]
            low, high = jnp.where(swapped, other, own), jnp.where(swapped, own, other)
            row = PAD + x * brick1 + i
            f_ref[row, pl.ds(at, SUB)] = jnp.where(low_half, low, high)
            h_ref[row, pl.ds(at, SUB)] = turn(jnp.where(low_half, high, low), SUB // 2, 0)

    each(along_x * across, brick1, place)

    def clear_beside(ref, row):
        zero = jnp.zeros((MARGIN, depth1), F32)
        ref[row, 0:MARGIN] = zero
        ref[row, pl.ds(ref.shape[1] - MARGIN, MARGIN)] = zero

    def clear(i):
        for ref in (h_ref, v_ref):
            clear_beside(ref, PAD + i)
        wy_ref[PAD + i, 0:MARGIN] = jnp.zeros((MARGIN, depth1), F32)

    each(rows1, 1, clear)
    for ref in (h_ref, v_ref):
        for row in (PAD - 1, PAD + rows1):
            ref[row] = jnp.zeros(ref.shape[1:], F32)

    def weigh(ref, row, cols, stride):
        half = ref[row, pl.ds(MARGIN, cols)]
        lane = iota(half.shape, 1)
        first, last = lane < stride, lane >= half.shape[1] - stride
        around = [ref[row - 1, pl.ds(MARGIN, cols)], ref[row + 1, pl.ds(MARGIN, cols)]]
        around += [ref[row, pl.ds(MARGIN - 1, cols)], ref[row, pl.ds(MARGIN + 1, cols)]]
        around += [
            jnp.where(first, 0.0, turn(half, stride, 1)),
            jnp.where(last, 0.0, turn(half, -stride, 1)),
        ]
        total = (around[0] + around[1]) + (around[2] + around[3]) + (around[4] + around[5])
        return half, around, 6.0 * half + total, first, last

    wx_ref[PAD, inner] = h_ref[PAD, inner]

    def weigh1(i):
        row = PAD + i
        half, around, diag, _, last = weigh(h_ref, row, cols1, 1)
        inv = 1.0 / diag
        wx_ref[row + 1, inner] = half + around[1]
        wy_ref[row, inner] = half + around[3]
        wz_ref[row, inner] = jnp.where(last, 0.0, half + around[5])
        diag_ref[i] = diag
        inv_ref[row, inner] = inv
        v_ref[row, inner] = f_ref[row, inner] * inv * inv_mid

    each(rows1, registers1, weigh1)

    rows2, cols2 = rows1 // 2, cols1 // 2
    shape2 = (cols2, depth1)
    registers2 = max(registers1 // 2, 1)
    zero2 = jnp.zeros(shape2, F32)
    lane2, col2 = iota(shape2, 1), iota(shape2, 0)
    even2 = lane2 % 2 == 0
    inner2 = pl.ds(MARGIN, cols2)

    def fold(ref, row):
        half = ref[row, pl.ds(MARGIN, cols2, stride=2), :] + ref[row, pl.ds(MARGIN + 1, cols2, stride=2), :]
        return half + turn(half, -1, 1)

    def restrict_h(k):
        row = PAD + 2 * k
        h2_ref[k + 1, inner2] = 0.125 * (fold(h_ref, row) + fold(h_ref, row + 1))

    each(rows2, 2 * registers1, restrict_h)
    u_ref = h_ref

    def pulled1(x_ref, at, x_first, row, first, count):
        def part(ref, i, begin, shift=0):
            return ref[i, pl.ds(begin + shift, count), :]

        x, depths = part(x_ref, at, x_first), part(wz_ref, row, first)
        total = part(wx_ref, row + 1, first) * part(x_ref, at + 1, x_first)
        total = total + part(wx_ref, row, first) * part(x_ref, at - 1, x_first)
        total = total + part(wy_ref, row, first) * part(x_ref, at, x_first, 1)
        total = total + part(wy_ref, row, first, -1) * part(x_ref, at, x_first, -1)
        total = total + depths * turn(x, -1, 1) + turn(depths * x, 1, 1)
        return x, part(f_ref, row, first) + total

    def second1(i):
        row = PAD + i
        v, total = pulled1(v_ref, row, MARGIN, row, MARGIN, cols1)
        u_ref[row, inner] = (1.0 + keep - push) * v + push * (inv_ref[row, inner] * total)

    each(rows1, registers1, second1)

    def residual1(i):
        u, total = pulled1(u_ref, PAD + i, MARGIN, PAD + i, MARGIN, cols1)
        return total - diag_ref[i] * u

    def restrict(k):
        v_ref[k, inner] = residual1(2 * k) + residual1(2 * k + 1)
        f2_ref[k] = 0.5 * fold(v_ref, k)

    each(rows2, 2 * registers1, restrict)
    for ref in (h2_ref, e2_ref, e3_ref):
        for row in (0, rows2 + 1):
            ref[row] = jnp.zeros(ref.shape[1:], F32)

    def clear2(k):
        for ref in (h2_ref, e2_ref, e3_ref):
            clear_beside(ref, k + 1)

    each(rows2, 1, clear2)
    inv_mid2, pairs2 = chebyshev(COARSE_LOW, COARSE_HIGH, COARSE_STEPS)

    def kept(at, k):
        ref, at, begin = (diag_ref, at, 0) if at < 4 else (v_ref, at - 4, MARGIN)
        return ref, 2 * k + at // 2, pl.ds(begin + at % 2 * cols2, cols2)

    def keep_value(at, k, value):
        ref, row, columns = kept(at, k)
        ref[row, columns] = value

    def kept_value(at, k):
        ref, row, columns = kept(at, k)
        return ref[row, columns]

    diagonal, direction = 6, 7

    def weigh2(k, edges):
        half, around, diag, first, last = weigh(h2_ref, k + 1, cols2, 2)
        inv = 1.0 / diag
        scaled = half * inv
        for at in range(4):
            keep_value(at, k, scaled + around[at] * inv)
        keep_value(4, k, jnp.where(first, 0.0, scaled + around[4] * inv))
        keep_value(5, k, jnp.where(last, 0.0, scaled + around[5] * inv))
        keep_value(diagonal, k, diag)
        f = f2_ref[k] * inv
        f2_ref[k] = f
        d = f * inv_mid2
        keep_value(direction, k, d)
        e2_ref[k + 1, inner2] = d
        edges = edges + jnp.where((col2 == 0) | (col2 == cols2 - 1), half, 0.0)
        edges = edges + jnp.where(first | last, half, 0.0)
        return edges + jnp.where(k == 0, half, 0.0) + jnp.where(k == rows2 - 1, half, 0.0)

    edges = each_sum(rows2, registers2, weigh2, zero2)

    def residual2(e_ref, k):
        e = e_ref[k + 1, inner2]
        r = f2_ref[k] - e + kept_value(0, k) * e_ref[k, inner2] + kept_value(1, k) * e_ref[k + 2, inner2]
        r = r + kept_value(2, k) * e_ref[k + 1, pl.ds(MARGIN - 1, cols2)]
        r = r + kept_value(3, k) * e_ref[k + 1, pl.ds(MARGIN + 1, cols2)]
        return e, r + (kept_value(4, k) * turn(e, 2, 1) + kept_value(5, k) * turn(e, -2, 1))

    now_ref, next_ref = e2_ref, e3_ref
    for keep2, push2 in pairs2:

        def step2(k):
            e, r = residual2(now_ref, k)
            d = keep2 * kept_value(direction, k) + push2 * r
            keep_value(direction, k, d)
            next_ref[k + 1, inner2] = e + d

        each(rows2, registers2, step2)
        now_ref, next_ref = next_ref, now_ref

    def add_residual(k, total):
        return total + kept_value(diagonal, k) * residual2(now_ref, k)[1]

    total = each_sum(rows2, registers2, add_residual, zero2)
    top = jnp.sum(jnp.where(even2, total, 0.0), axis=(0, 1), keepdims=True)
    bottom = jnp.sum(jnp.where(even2, edges, 0.0), axis=(0, 1), keepdims=True)
    mean = top / bottom

    span, broad = brick1 + 2 * PAD, 2 * SUB
    start, first_col = gx * brick1 - PAD, gy * (cols1 // along_y) - PAD
    coarse_span = span // 2 + 2
    for k in range(coarse_span):
        row = lax.div(gx * brick1, 2) - PAD // 2 - 1 + k
        good = (row >= 0) & (row < rows2)
        e = now_ref[jnp.clip(row, 0, rows2 - 1) + 1, inner2] + mean
        e = jnp.where(good, e, 0.0)
        back = jnp.where(lane2 < 2, 0.0, turn(e, 2, 1))
        ahead = jnp.where(lane2 >= depth1 - 2, 0.0, turn(e, -1, 1))
        home = jnp.where(even2, e, turn(e, 1, 1))
        e = 0.75 * home + 0.25 * jnp.where(even2, back, ahead)
        back = jnp.where(col2 == 0, 0.0, turn(e, 1, 0))
        ahead = jnp.where(col2 == cols2 - 1, 0.0, turn(e, -1, 0))
        py_ref[k, pl.ds(MARGIN, cols2, stride=2), :] = 0.75 * e + 0.25 * back
        py_ref[k, pl.ds(MARGIN + 1, cols2, stride=2), :] = 0.75 * e + 0.25 * ahead

    window, held = pl.ds(MARGIN + first_col, broad), pl.ds(MARGIN, broad)
    col1 = first_col + iota((broad, depth1), 0)
    col_good = (col1 >= 0) & (col1 < cols1)

    def inside1(m):
        return col_good & ((start + m >= 0) & (start + m < rows1))

    for m in range(span):
        near = m // 2 + 1
        far = near - 1 if m % 2 == 0 else near + 1
        total = u_ref[PAD + start + m, window, :]
        total = total + (0.75 * py_ref[near, window, :] + 0.25 * py_ref[far, window, :])
        vw_ref[m, held] = jnp.where(inside1(m), total, 0.0)
    for m in range(1, span - 1):
        row = PAD + start + m
        v, total = pulled1(vw_ref, m, MARGIN, row, MARGIN + first_col, broad)
        d = (inv_ref[row, window, :] * total - v) * inv_mid
        dw_ref[m] = d
        vx_ref[m, held] = jnp.where(inside1(m), v + d, 0.0)
    for m in range(2, span - 2):
        row = PAD + start + m
        v, total = pulled1(vx_ref, m, MARGIN, row, MARGIN + first_col, broad)
        e = (1.0 - push) * v + (keep * dw_ref[m] + push * (inv_ref[row, window, :] * total))
        e1_ref[m - 2] = jnp.where(inside1(m), e, 0.0)

    rows, cols, depth = out_ref.shape
    wide = (cols + 2 * DEEP_C, depth)
    half_wide = wide[0] // 2
    for k in range(span - 4):
        e = turn(e1_ref[k, pl.ds(PAD - DEEP_C // 2, half_wide), :], -(DEEP_C // 2), 0)
        at = k * wide[0]
        yy_ref[pl.ds(at, half_wide, stride=2), :] = 0.75 * e + 0.25 * turn(e, 1, 0)
        yy_ref[pl.ds(at + 1, half_wide, stride=2), :] = 0.75 * e + 0.25 * turn(e, -1, 0)
    spread = (depth1, depth)
    from_cell, to_cell = iota(spread, 0), iota(spread, 1)
    home = to_cell // 2
    near_cell = jnp.where(to_cell % 2 == 0, home - 1, home + 1)
    weights = jnp.where(from_cell == home, 0.75, 0.0) + jnp.where(from_cell == near_cell, 0.25, 0.0)
    carried = exact_dot(yy_ref[...], weights).reshape(span - 4, wide[0], depth)
    col_inside = inside_cols(iota(wide, 0), cols, along_y)
    for s in range(1, rows + 2 * DEEP_F - 1):
        row = s - DEEP_F
        near = row // 2 + 2
        far = near - 1 if row % 2 == 0 else near + 1
        inside = col_inside
        if row < 0:
            inside = inside & (gx > 0)
        if row >= rows:
            inside = inside & (gx < along_x - 1)
        total = u0_ref[s - 1] + (0.75 * carried[near] + 0.25 * carried[far])
        v0_ref[s] = jnp.where(inside, total, 0.0)

    def pulled0(x_ref, s, span):
        return fx_ref[s, :span] + beside(
            x_ref[s], x_ref[s - 1, :span], x_ref[s + 1, :span],
            wx0_ref[s, :span], wx0_ref[s + 1, :span], wy0_ref[s], wz0_ref[s, :span],
        )

    for s in range(2, rows + 2 * DEEP_F - 2):
        v = v0_ref[s]
        d = (inv0_ref[s] * pulled0(v0_ref, s, wide[0]) - v) * inv_mid
        d0_ref[s] = d[:cols]
        x0_ref[s] = v + d
    for i in range(rows):
        s = i + DEEP_F
        total = inv0_ref[s, :cols] * pulled0(x0_ref, s, cols)
        out_ref[i] = (1.0 - push) * x0_ref[s, :cols] + (keep * d0_ref[s] + push * total)


def pairs_from(first, count):
    swaps = []
    for i in range(first, first + count, 2):
        a, b = i % count, (i + 1) % count
        swaps += [(a, b), (b, a)]
    return swaps


def swaps(along_x, along_y, axis, first):
    pairs = []
    for x in range(along_x):
        for y in range(along_y):
            place, count = (x, along_x) if axis == "gx" else (y, along_y)
            other = place + 1 if (place - first) % 2 == 0 else place - 1
            if 0 <= other < count:
                to = (other, y) if axis == "gx" else (x, other)
            else:
                to = (x, y ^ 1) if axis == "gx" else (x ^ 1, y)
            pairs.append((x * along_y + y, to[0] * along_y + to[1]))
    return pairs


def at_distance(along_x, along_y, axis, distance):
    pairs = []
    for x in range(along_x):
        for y in range(along_y):
            to = (x ^ distance, y) if axis == "gx" else (x, y ^ (2 * distance + 1))
            pairs.append((x * along_y + y, to[0] * along_y + to[1]))
    return pairs


def body(right_side, coefficient):
    along_x, along_y = lax.axis_size("gx"), lax.axis_size("gy")
    rows, cols, depth = right_side.shape
    assert cols == 2 * DEEP_C and rows % 4 == 0 and depth % 256 == 0
    assert along_x & (along_x - 1) == 0 and along_y & (along_y - 1) == 0 and along_x * along_y > 3
    small = 16 << 20
    strip = (DEEP_F + DEEP_C, cols, depth)
    odd = lax.rem(lax.axis_index("gx"), 2) == 1
    first = jnp.concatenate([right_side[:DEEP_F], coefficient[:DEEP_C]])
    last = jnp.concatenate([right_side[rows - DEEP_F :], coefficient[rows - DEEP_C :]])
    a, b = jnp.where(odd, first, last), jnp.where(odd, last, first)
    a = lax.ppermute(a, "gx", pairs_from(0, along_x))
    b = lax.ppermute(b, ("gx", "gy"), swaps(along_x, along_y, "gx", 1))

    tall = rows + 2 * DEEP_F
    z, k = call(
        functools.partial(pack_cols, along_x),
        [(rows + 3, cols, depth)] * 2,
        [],
        (right_side, coefficient, a, b),
        small,
    )
    k = lax.ppermute(k, "gy", pairs_from(0, along_y))
    z = lax.ppermute(z, ("gx", "gy"), swaps(along_x, along_y, "gy", 1))

    wide = (cols + 2 * DEEP_C, depth)
    half = (rows // 2, SUB, depth // 2)
    send, *state = call(
        functools.partial(fine_down, along_x, along_y),
        [half, (tall - 2,) + wide, (tall,) + wide, (tall + 1,) + wide]
        + [(tall,) + wide] * 3,
        [(tall + 2,) + wide, (tall,) + wide, (rows, cols, depth)],
        (right_side, coefficient, a, b, z, k),
        small,
    )
    own = send
    for axis, count in [("gy", along_y // 2), ("gx", along_x)]:
        parts = [own] + [
            lax.ppermute(own, ("gx", "gy"), at_distance(along_x, along_y, axis, distance))
            for distance in range(1, count)
        ]
        shape = (count * own.shape[0],) + own.shape[1:]
        (own,) = call(functools.partial(line_up, axis), [shape], [], parts, small + 8 * math.prod(shape))
    other = lax.ppermute(own, "gy", pairs_from(0, along_y))

    rows1, cols1, depth1 = along_x * half[0], along_y * (cols // 2), half[2]
    whole1 = (rows1 + 2 * PAD + 1, cols1 + 2 * MARGIN, depth1)
    rows2, cols2 = rows1 // 2, cols1 // 2
    whole2 = (rows2 + 2, cols2 + 2 * MARGIN, depth1)
    span, broad = half[0] + 2 * PAD, 2 * SUB
    window = (span, broad + 2 * MARGIN, depth1)
    scratch = [whole1] * 7 + [(rows1, cols1, depth1)]
    scratch += [(rows2, cols2, depth1)] + [whole2] * 3
    scratch += [(span // 2 + 2,) + whole1[1:], window, (span, broad, depth1), window]
    scratch += [(span - 4, broad, depth1), ((span - 4) * wide[0], depth1)]
    scratch += [(tall,) + wide, (tall, cols, depth), (tall,) + wide]
    size = sum(4 * math.prod(s) for s in scratch)
    size += 2 * 4 * own.size + 4 * 8 * tall * wide[0] * wide[1]
    (out,) = call(
        functools.partial(coarse_and_up, along_x, along_y),
        [right_side.shape],
        scratch,
        (own, other, *state),
        size + (12 << 20),
    )
    return out


def solution(mesh):
    placed = (P("gx", "gy", None), P("gx", "gy", None))
    return jax.shard_map(
        body, mesh=mesh, in_specs=placed, out_specs=P("gx", "gy", None), check_vma=False
    )
```

```python
import functools
import math

import jax
import jax.numpy as jnp
from jax import lax
from jax.experimental import pallas as pl
from jax.experimental.pallas import tpu as pltpu
from jax.sharding import PartitionSpec as P

SMOOTH = 2
COARSE_STEPS = 6
SMOOTH_LOW = 0.5
SMOOTH_HIGH = 2.0
COARSE_LOW = 0.05
COARSE_HIGH = 2.0

DEEP_F = 2 * SMOOTH - 1
DEEP_C = 2 * SMOOTH
SUB = 8
PAD = 4
MARGIN = SUB
WRITTEN_OUT = 512

VMEM = pl.BlockSpec(memory_space=pltpu.VMEM)
F32 = jnp.float32


def chebyshev(low_end, high_end, sweeps):
    middle = 0.5 * (high_end + low_end)
    half_span = 0.5 * (high_end - low_end)
    sig_ratio = middle / half_span
    rho_now = 1.0 / sig_ratio
    coeff_pairs = []
    for sweep_num in range(1, sweeps):
        rho_next = 1.0 / (2.0 * sig_ratio - rho_now)
        coeff_pairs.append((rho_next * rho_now, 2.0 * rho_next / half_span))
        rho_now = rho_next
    return (1.0 / middle, coeff_pairs)


def each(count, registers, step):
    each_sum(count, registers, lambda i, carry: (step(i), carry)[1], 0)


def each_sum(count, registers, step, carry):
    if count * registers > WRITTEN_OUT:
        return lax.fori_loop(0, count, step, carry)
    for i in range(count):
        carry = step(i, carry)
    return carry


def turn(value, amount, axis):
    return pltpu.roll(value, amount % value.shape[axis], axis)


def iota(shape, axis):
    return lax.broadcasted_iota(jnp.int32, shape, axis)


def beside(v, below, above, w_below, w_above, w_cols, w_depth):
    span = below.shape[0]
    out = w_above * above + w_below * below
    out = out + w_cols[:span] * turn(v, -1, 0)[:span]
    out = out + turn(w_cols * v, 1, 0)[:span]
    v = v[:span]
    return out + w_depth * turn(v, -1, 1) + turn(w_depth * v, 1, 1)


def inside_cols(col, cols, along_y):
    gy = lax.axis_index("gy")
    after = (col >= cols) & (col < cols + DEEP_C) & (gy == along_y - 1)
    before = (col >= cols + DEEP_C) & (gy == 0)
    return jnp.logical_not(after | before)


def exact_dot(a, b):
    return jnp.dot(a, b, precision=lax.Precision.HIGHEST, preferred_element_type=F32)


def call(kernel, out_shapes, scratch, args, limit):
    return pl.pallas_call(
        kernel,
        out_shape=[jax.ShapeDtypeStruct(s, F32) for s in out_shapes],
        in_specs=[VMEM] * len(args),
        out_specs=[VMEM] * len(out_shapes),
        scratch_shapes=[pltpu.VMEM(s, F32) for s in scratch],
        compiler_params=pltpu.CompilerParams(vmem_limit_bytes=limit),
    )(*args)


def pack_rows(f_ref, c_ref, a_ref, b_ref, sems):
    rows = f_ref.shape[0]
    odd = lax.rem(lax.axis_index("gx"), 2)
    copies = []
    for ref, at_end in ((a_ref, 1 - odd), (b_ref, odd)):
        for whole_ref, first, count in ((f_ref, 0, DEEP_F), (c_ref, DEEP_F, DEEP_C)):
            copies.append(
                pltpu.make_async_copy(
                    whole_ref.at[pl.ds(at_end * (rows - count), count)],
                    ref.at[pl.ds(first, count)],
                    sems.at[len(copies)],
                )
            )
    for copy in copies:
        copy.start()
    for copy in copies:
        copy.wait()


def row_sources(along_x, rows, f_ref, c_ref, a_ref, b_ref):
    gx = lax.axis_index("gx")
    odd = lax.rem(gx, 2) == 1
    has_before = (gx > 0).astype(F32)
    has_after = (gx < along_x - 1).astype(F32)

    def before(i):
        return jnp.where(odd, a_ref[i], b_ref[i]) * has_before

    def after(i):
        return jnp.where(odd, b_ref[i], a_ref[i]) * has_after

    def f_row(i):
        if i < 0:
            return before(DEEP_F + i)
        return f_ref[i] if i < rows else after(i - rows)

    def c_row(i):
        if i < 0:
            return before(DEEP_F + DEEP_C + i)
        return c_ref[i] if i < rows else after(DEEP_F + i - rows)

    return f_row, c_row


def pack_cols(along_x, f_ref, c_ref, a_ref, b_ref, z_ref, k_ref):
    rows = f_ref.shape[0]
    f_row, c_row = row_sources(along_x, rows, f_ref, c_ref, a_ref, b_ref)
    odd = lax.rem(lax.axis_index("gy"), 2) == 1
    sub = iota(f_ref.shape[1:], 0)
    low_half = sub < DEEP_C

    def put(t, first, last):
        z_ref[t] = jnp.where(odd, last, first)
        k_ref[t] = jnp.where(odd, first, last)

    for t in range(rows + 2):
        f, c = turn(f_row(t - 1), DEEP_C, 0), c_row(t - 1)
        put(t, jnp.where(low_half, c, f), jnp.where(low_half, f, c))

    def corners(sub, way):
        near, near_f, far = c_row(-2), f_row(-2), c_row(-3)
        out = jnp.where(sub < 2, near, jnp.where(sub == 2, turn(near_f, 2 * way, 0), turn(far, 3 * way, 0)))
        near, near_f, far = c_row(rows + 1), f_row(rows + 1), c_row(rows + 2)
        out = jnp.where(sub < 4, out, jnp.where(sub < 6, turn(near, 4 * way, 0), turn(near_f, 6 * way, 0)))
        return jnp.where(sub < 7, out, turn(far, 7 * way, 0))

    put(rows + 2, corners(sub, 1), corners(SUB - 1 - sub, -1))


def line_up(*refs):
    *block_refs, out_ref = refs
    here = lax.div(lax.axis_index("gy"), 2)
    size = block_refs[0].shape[0]
    for distance, ref in enumerate(block_refs):
        out_ref[pl.ds((here ^ distance) * size, size)] = ref[...]


def fine_down(
    along_x, along_y,
    f_ref, c_ref, a_ref, b_ref, z_ref, k_ref,
    send_ref, u_ref, fx_ref, wx_ref, wy_ref, wz_ref, inv_ref,
    cx_ref, v_ref, diag_ref,
):
    rows, cols, depth = f_ref.shape
    f_row, c_row = row_sources(along_x, rows, f_ref, c_ref, a_ref, b_ref)
    gx, gy = lax.axis_index("gx"), lax.axis_index("gy")
    odd = lax.rem(gy, 2) == 1
    has_left = (gy > 0).astype(F32)
    has_right = (gy < along_y - 1).astype(F32)
    low_half = iota((cols, depth), 0) < DEEP_C
    wide = (cols + 2 * DEEP_C, depth)
    lane = iota(wide, 1)
    col = iota(wide, 0)
    col_inside = inside_cols(col, cols, along_y)
    inv_mid, ((keep, push),) = chebyshev(SMOOTH_LOW, SMOOTH_HIGH, SMOOTH)

    def sides(t):
        left = jnp.where(odd, k_ref[t], z_ref[t]) * has_left
        return left, jnp.where(odd, z_ref[t], k_ref[t]) * has_right

    corner_tiles = sides(rows + 2)
    for t in range(rows + 2 * DEEP_C):
        row = t - DEEP_C
        cx_ref[t, 0:cols] = 0.5 * c_row(row)
        s = row + DEEP_F
        if -1 <= row <= rows:
            left, right = sides(row + 1)
            cx_ref[t, cols:] = 0.5 * jnp.where(low_half, right, left)
            f = turn(jnp.where(low_half, left, right), DEEP_C, 0)
        else:
            left, right = corner_tiles
            c_turn = {-2: 0, -3: 3, rows + 1: 4, rows + 2: 7}.get(row)
            f_turn = {-2: 2, rows + 1: 6}.get(row)
            c = f = jnp.zeros((cols, depth), F32)
            if c_turn is not None:
                c = jnp.where(low_half, turn(right, -c_turn, 0), turn(left, c_turn, 0))
            if f_turn is not None:
                f = jnp.where(low_half, turn(right, -f_turn, 0), turn(left, f_turn, 0))
            cx_ref[t, cols:] = 0.5 * c
        if 0 <= s < rows + 2 * DEEP_F:
            fx_ref[s, 0:cols] = f_row(row)
            fx_ref[s, cols:] = f

    tall = rows + 2 * DEEP_F
    wx_ref[0] = cx_ref[0] + cx_ref[1]
    for s in range(tall):
        half = cx_ref[s + 1]
        above = half + cx_ref[s + 2]
        after = half + turn(half, -1, 0)
        deeper = jnp.where(lane == depth - 1, 0.0, half + turn(half, -1, 1))
        wx_ref[s + 1] = above
        wy_ref[s] = after
        wz_ref[s] = deeper
        diag = wx_ref[s] + above + after + turn(after, 1, 0) + deeper + turn(deeper, 1, 1)
        diag = diag + jnp.where((lane == 0) | (lane == depth - 1), half, 0.0)
        inside = col_inside
        if s < DEEP_F:
            inside = inside & (gx > 0)
        if s >= rows + DEEP_F:
            inside = inside & (gx < along_x - 1)
        inv = jnp.where(inside, 1.0 / diag, 0.0)
        if DEEP_F <= s < DEEP_F + rows:
            diag_ref[s - DEEP_F] = diag[:cols]
        inv_ref[s] = inv
        v_ref[s] = fx_ref[s] * inv * inv_mid

    def pulled(x_ref, shift, s, span):
        at = s - shift
        total = beside(
            x_ref[at], x_ref[at - 1, :span], x_ref[at + 1, :span],
            wx_ref[s, :span], wx_ref[s + 1, :span], wy_ref[s], wz_ref[s, :span],
        )
        return fx_ref[s, :span] + total

    for s in range(1, tall - 1):
        total = pulled(v_ref, 0, s, wide[0])
        u_ref[s - 1] = (1.0 + keep - push) * v_ref[s] + push * (inv_ref[s] * total)

    def residual(s):
        return pulled(u_ref, 1, s, cols) - diag_ref[s - DEEP_F] * u_ref[s - 1, :cols]

    half_rows = rows // 2
    summed = [residual(2 * i + DEEP_F) + residual(2 * i + 1 + DEEP_F) for i in range(half_rows)]
    summed += [c_ref[2 * i] + c_ref[2 * i + 1] for i in range(half_rows)]
    summed = jnp.concatenate(summed, axis=0)
    pairs = (depth, depth // 2)
    thin = exact_dot(summed, (iota(pairs, 0) // 2 == iota(pairs, 1)).astype(F32))
    choice = (SUB * half_rows, summed.shape[0])
    line, source = iota(choice, 0), iota(choice, 1)
    block, place = line // SUB, line % SUB
    half_cols = cols // 2
    f_half = (place >= half_cols) == odd
    place = place % half_cols
    f_from = cols * block + 2 * place
    c_from = f_from + cols * half_rows
    from_f = (source == f_from) | (source == f_from + 1)
    from_c = (source == c_from) | (source == c_from + 1)
    picker = jnp.where(f_half, jnp.where(from_f, 0.5, 0.0), jnp.where(from_c, 0.0625, 0.0))
    tile = exact_dot(picker, thin).reshape(half_rows, SUB, depth // 2)

    send_ref[...] = tile


def coarse_and_up(along_x, along_y, *refs):
    own_refs, other_refs, refs = refs[:along_x], refs[along_x : 2 * along_x], refs[2 * along_x :]
    u0_ref, fx_ref, wx0_ref, wy0_ref, wz0_ref, inv0_ref, out_ref, *refs = refs
    f_ref, h_ref, wx_ref, wy_ref, wz_ref, inv_ref, v_ref, diag_ref, f2_ref, h2_ref, e2_ref, e3_ref, *refs = refs
    py_ref, vw_ref, dw_ref, vx_ref, e1_ref, yy_ref, v0_ref, d0_ref, x0_ref = refs
    gx, gy = lax.axis_index("gx"), lax.axis_index("gy")
    odd = lax.rem(gy, 2) == 1
    brick1 = own_refs[0].shape[0] // (along_y // 2)
    rows1, cols1, depth1 = diag_ref.shape
    across = cols1 // SUB
    registers1 = across * (depth1 // 128)
    inv_mid, ((keep, push),) = chebyshev(SMOOTH_LOW, SMOOTH_HIGH, SMOOTH)
    inner = pl.ds(MARGIN, cols1)

    low_half = iota((SUB, depth1), 0) < SUB // 2

    chip = lax.div(gy, 2)

    def place(distance, z):
        own_ref, other_ref, x = own_refs[distance], other_refs[distance], gx ^ distance
        at = z * SUB + MARGIN
        if not isinstance(z, int):
            at = pl.multiple_of(at, SUB)
        swapped = odd == (z == chip)
        for i in range(brick1):
            own, other = own_ref[z * brick1 + i], other_ref[z * brick1 + i]
            low, high = jnp.where(swapped, other, own), jnp.where(swapped, own, other)
            row = PAD + x * brick1 + i
            f_ref[row, pl.ds(at, SUB)] = jnp.where(low_half, low, high)
            h_ref[row, pl.ds(at, SUB)] = turn(jnp.where(low_half, high, low), SUB // 2, 0)

    for distance in range(along_x):
        each(across, brick1, functools.partial(place, distance))

    def clear_beside(ref, row):
        zero = jnp.zeros((MARGIN, depth1), F32)
        ref[row, 0:MARGIN] = zero
        ref[row, pl.ds(ref.shape[1] - MARGIN, MARGIN)] = zero

    def clear(i):
        for ref in (h_ref, v_ref):
            clear_beside(ref, PAD + i)
        wy_ref[PAD + i, 0:MARGIN] = jnp.zeros((MARGIN, depth1), F32)

    each(rows1, 1, clear)
    for ref in (h_ref, v_ref):
        for row in (PAD - 1, PAD + rows1):
            ref[row] = jnp.zeros(ref.shape[1:], F32)

    def weigh(ref, row, cols, stride):
        half = ref[row, pl.ds(MARGIN, cols)]
        lane = iota(half.shape, 1)
        first, last = lane < stride, lane >= half.shape[1] - stride
        around = [ref[row - 1, pl.ds(MARGIN, cols)], ref[row + 1, pl.ds(MARGIN, cols)]]
        around += [ref[row, pl.ds(MARGIN - 1, cols)], ref[row, pl.ds(MARGIN + 1, cols)]]
        around += [
            jnp.where(first, 0.0, turn(half, stride, 1)),
            jnp.where(last, 0.0, turn(half, -stride, 1)),
        ]
        total = (around[0] + around[1]) + (around[2] + around[3]) + (around[4] + around[5])
        return half, around, 6.0 * half + total, first, last

    wx_ref[PAD, inner] = h_ref[PAD, inner]

    def weigh1(i):
        row = PAD + i
        half, around, diag, _, last = weigh(h_ref, row, cols1, 1)
        inv = 1.0 / diag
        wx_ref[row + 1, inner] = half + around[1]
        wy_ref[row, inner] = half + around[3]
        wz_ref[row, inner] = jnp.where(last, 0.0, half + around[5])
        diag_ref[i] = diag
        inv_ref[row, inner] = inv
        v_ref[row, inner] = f_ref[row, inner] * inv * inv_mid

    each(rows1, registers1, weigh1)

    rows2, cols2 = rows1 // 2, cols1 // 2
    shape2 = (cols2, depth1)
    registers2 = max(registers1 // 2, 1)
    zero2 = jnp.zeros(shape2, F32)
    lane2, col2 = iota(shape2, 1), iota(shape2, 0)
    even2 = lane2 % 2 == 0
    inner2 = pl.ds(MARGIN, cols2)

    def fold(ref, row):
        half = ref[row, pl.ds(MARGIN, cols2, stride=2), :] + ref[row, pl.ds(MARGIN + 1, cols2, stride=2), :]
        return half + turn(half, -1, 1)

    def restrict_h(k):
        row = PAD + 2 * k
        h2_ref[k + 1, inner2] = 0.125 * (fold(h_ref, row) + fold(h_ref, row + 1))

    each(rows2, 2 * registers1, restrict_h)
    u_ref = h_ref

    def pulled1(x_ref, at, x_first, row, first, count):
        def part(ref, i, begin, shift=0):
            return ref[i, pl.ds(begin + shift, count), :]

        x, depths = part(x_ref, at, x_first), part(wz_ref, row, first)
        total = part(wx_ref, row + 1, first) * part(x_ref, at + 1, x_first)
        total = total + part(wx_ref, row, first) * part(x_ref, at - 1, x_first)
        total = total + part(wy_ref, row, first) * part(x_ref, at, x_first, 1)
        total = total + part(wy_ref, row, first, -1) * part(x_ref, at, x_first, -1)
        total = total + depths * turn(x, -1, 1) + turn(depths * x, 1, 1)
        return x, part(f_ref, row, first) + total

    def second1(i):
        row = PAD + i
        v, total = pulled1(v_ref, row, MARGIN, row, MARGIN, cols1)
        u_ref[row, inner] = (1.0 + keep - push) * v + push * (inv_ref[row, inner] * total)

    each(rows1, registers1, second1)

    def residual1(i):
        u, total = pulled1(u_ref, PAD + i, MARGIN, PAD + i, MARGIN, cols1)
        return total - diag_ref[i] * u

    def restrict(k):
        v_ref[k, inner] = residual1(2 * k) + residual1(2 * k + 1)
        f2_ref[k] = 0.5 * fold(v_ref, k)

    each(rows2, 2 * registers1, restrict)
    for ref in (h2_ref, e2_ref, e3_ref):
        for row in (0, rows2 + 1):
            ref[row] = jnp.zeros(ref.shape[1:], F32)

    def clear2(k):
        for ref in (h2_ref, e2_ref, e3_ref):
            clear_beside(ref, k + 1)

    each(rows2, 1, clear2)
    inv_mid2, pairs2 = chebyshev(COARSE_LOW, COARSE_HIGH, COARSE_STEPS)

    def kept(at, k):
        ref, at, begin = (diag_ref, at, 0) if at < 4 else (v_ref, at - 4, MARGIN)
        return ref, 2 * k + at // 2, pl.ds(begin + at % 2 * cols2, cols2)

    def keep_value(at, k, value):
        ref, row, columns = kept(at, k)
        ref[row, columns] = value

    def kept_value(at, k):
        ref, row, columns = kept(at, k)
        return ref[row, columns]

    diagonal, direction = 6, 7

    def weigh2(k, edges):
        half, around, diag, first, last = weigh(h2_ref, k + 1, cols2, 2)
        inv = 1.0 / diag
        scaled = half * inv
        for at in range(4):
            keep_value(at, k, scaled + around[at] * inv)
        keep_value(4, k, jnp.where(first, 0.0, scaled + around[4] * inv))
        keep_value(5, k, jnp.where(last, 0.0, scaled + around[5] * inv))
        keep_value(diagonal, k, diag)
        f = f2_ref[k] * inv
        f2_ref[k] = f
        d = f * inv_mid2
        keep_value(direction, k, d)
        e2_ref[k + 1, inner2] = d
        edges = edges + jnp.where((col2 == 0) | (col2 == cols2 - 1), half, 0.0)
        edges = edges + jnp.where(first | last, half, 0.0)
        return edges + jnp.where(k == 0, half, 0.0) + jnp.where(k == rows2 - 1, half, 0.0)

    edges = each_sum(rows2, registers2, weigh2, zero2)

    def residual2(e_ref, k):
        e = e_ref[k + 1, inner2]
        r = f2_ref[k] - e + kept_value(0, k) * e_ref[k, inner2] + kept_value(1, k) * e_ref[k + 2, inner2]
        r = r + kept_value(2, k) * e_ref[k + 1, pl.ds(MARGIN - 1, cols2)]
        r = r + kept_value(3, k) * e_ref[k + 1, pl.ds(MARGIN + 1, cols2)]
        return e, r + (kept_value(4, k) * turn(e, 2, 1) + kept_value(5, k) * turn(e, -2, 1))

    now_ref, next_ref = e2_ref, e3_ref
    for keep2, push2 in pairs2:

        def step2(k):
            e, r = residual2(now_ref, k)
            d = keep2 * kept_value(direction, k) + push2 * r
            keep_value(direction, k, d)
            next_ref[k + 1, inner2] = e + d

        each(rows2, registers2, step2)
        now_ref, next_ref = next_ref, now_ref

    def add_residual(k, total):
        return total + kept_value(diagonal, k) * residual2(now_ref, k)[1]

    total = each_sum(rows2, registers2, add_residual, zero2)
    top = jnp.sum(jnp.where(even2, total, 0.0), axis=(0, 1), keepdims=True)
    bottom = jnp.sum(jnp.where(even2, edges, 0.0), axis=(0, 1), keepdims=True)
    mean = top / bottom

    span, broad = brick1 + 2 * PAD, 2 * SUB
    start, first_col = gx * brick1 - PAD, gy * (cols1 // along_y) - PAD
    coarse_span = span // 2 + 2
    for k in range(coarse_span):
        row = lax.div(gx * brick1, 2) - PAD // 2 - 1 + k
        good = (row >= 0) & (row < rows2)
        e = now_ref[jnp.clip(row, 0, rows2 - 1) + 1, inner2] + mean
        e = jnp.where(good, e, 0.0)
        back = jnp.where(lane2 < 2, 0.0, turn(e, 2, 1))
        ahead = jnp.where(lane2 >= depth1 - 2, 0.0, turn(e, -1, 1))
        home = jnp.where(even2, e, turn(e, 1, 1))
        e = 0.75 * home + 0.25 * jnp.where(even2, back, ahead)
        back = jnp.where(col2 == 0, 0.0, turn(e, 1, 0))
        ahead = jnp.where(col2 == cols2 - 1, 0.0, turn(e, -1, 0))
        py_ref[k, pl.ds(MARGIN, cols2, stride=2), :] = 0.75 * e + 0.25 * back
        py_ref[k, pl.ds(MARGIN + 1, cols2, stride=2), :] = 0.75 * e + 0.25 * ahead

    window, held = pl.ds(MARGIN + first_col, broad), pl.ds(MARGIN, broad)
    col1 = first_col + iota((broad, depth1), 0)
    col_good = (col1 >= 0) & (col1 < cols1)

    def inside1(m):
        return col_good & ((start + m >= 0) & (start + m < rows1))

    for m in range(span):
        near = m // 2 + 1
        far = near - 1 if m % 2 == 0 else near + 1
        total = u_ref[PAD + start + m, window, :]
        total = total + (0.75 * py_ref[near, window, :] + 0.25 * py_ref[far, window, :])
        vw_ref[m, held] = jnp.where(inside1(m), total, 0.0)
    for m in range(1, span - 1):
        row = PAD + start + m
        v, total = pulled1(vw_ref, m, MARGIN, row, MARGIN + first_col, broad)
        d = (inv_ref[row, window, :] * total - v) * inv_mid
        dw_ref[m] = d
        vx_ref[m, held] = jnp.where(inside1(m), v + d, 0.0)
    for m in range(2, span - 2):
        row = PAD + start + m
        v, total = pulled1(vx_ref, m, MARGIN, row, MARGIN + first_col, broad)
        e = (1.0 - push) * v + (keep * dw_ref[m] + push * (inv_ref[row, window, :] * total))
        e1_ref[m - 2] = jnp.where(inside1(m), e, 0.0)

    rows, cols, depth = out_ref.shape
    wide = (cols + 2 * DEEP_C, depth)
    half_wide = wide[0] // 2
    for k in range(span - 4):
        e = turn(e1_ref[k, pl.ds(PAD - DEEP_C // 2, half_wide), :], -(DEEP_C // 2), 0)
        at = k * wide[0]
        yy_ref[pl.ds(at, half_wide, stride=2), :] = 0.75 * e + 0.25 * turn(e, 1, 0)
        yy_ref[pl.ds(at + 1, half_wide, stride=2), :] = 0.75 * e + 0.25 * turn(e, -1, 0)
    spread = (depth1, depth)
    from_cell, to_cell = iota(spread, 0), iota(spread, 1)
    home = to_cell // 2
    near_cell = jnp.where(to_cell % 2 == 0, home - 1, home + 1)
    weights = jnp.where(from_cell == home, 0.75, 0.0) + jnp.where(from_cell == near_cell, 0.25, 0.0)
    carried = exact_dot(yy_ref[...], weights).reshape(span - 4, wide[0], depth)
    col_inside = inside_cols(iota(wide, 0), cols, along_y)
    for s in range(1, rows + 2 * DEEP_F - 1):
        row = s - DEEP_F
        near = row // 2 + 2
        far = near - 1 if row % 2 == 0 else near + 1
        inside = col_inside
        if row < 0:
            inside = inside & (gx > 0)
        if row >= rows:
            inside = inside & (gx < along_x - 1)
        total = u0_ref[s - 1] + (0.75 * carried[near] + 0.25 * carried[far])
        v0_ref[s] = jnp.where(inside, total, 0.0)

    def pulled0(x_ref, s, span):
        return fx_ref[s, :span] + beside(
            x_ref[s], x_ref[s - 1, :span], x_ref[s + 1, :span],
            wx0_ref[s, :span], wx0_ref[s + 1, :span], wy0_ref[s], wz0_ref[s, :span],
        )

    for s in range(2, rows + 2 * DEEP_F - 2):
        v = v0_ref[s]
        d = (inv0_ref[s] * pulled0(v0_ref, s, wide[0]) - v) * inv_mid
        d0_ref[s] = d[:cols]
        x0_ref[s] = v + d
    for i in range(rows):
        s = i + DEEP_F
        total = inv0_ref[s, :cols] * pulled0(x0_ref, s, cols)
        out_ref[i] = (1.0 - push) * x0_ref[s, :cols] + (keep * d0_ref[s] + push * total)


def pairs_from(first, count):
    swaps = []
    for i in range(first, first + count, 2):
        a, b = i % count, (i + 1) % count
        swaps += [(a, b), (b, a)]
    return swaps


def swaps(along_x, along_y, axis, first):
    pairs = []
    for x in range(along_x):
        for y in range(along_y):
            place, count = (x, along_x) if axis == "gx" else (y, along_y)
            other = place + 1 if (place - first) % 2 == 0 else place - 1
            if 0 <= other < count:
                to = (other, y) if axis == "gx" else (x, other)
            else:
                to = (x, y ^ 1) if axis == "gx" else (x ^ 1, y)
            pairs.append((x * along_y + y, to[0] * along_y + to[1]))
    return pairs


def at_distance(along_x, along_y, axis, distance):
    pairs = []
    for x in range(along_x):
        for y in range(along_y):
            to = (x ^ distance, y) if axis == "gx" else (x, y ^ (2 * distance + 1))
            pairs.append((x * along_y + y, to[0] * along_y + to[1]))
    return pairs


def body(right_side, coefficient):
    along_x, along_y = lax.axis_size("gx"), lax.axis_size("gy")
    rows, cols, depth = right_side.shape
    assert cols == 2 * DEEP_C and rows % 4 == 0 and depth % 256 == 0
    assert along_x & (along_x - 1) == 0 and along_y & (along_y - 1) == 0 and along_x * along_y > 3
    small = 16 << 20
    strip = (DEEP_F + DEEP_C, cols, depth)
    odd = lax.rem(lax.axis_index("gx"), 2) == 1
    first = jnp.concatenate([right_side[:DEEP_F], coefficient[:DEEP_C]])
    last = jnp.concatenate([right_side[rows - DEEP_F :], coefficient[rows - DEEP_C :]])
    a, b = jnp.where(odd, first, last), jnp.where(odd, last, first)
    a = lax.ppermute(a, "gx", pairs_from(0, along_x))
    b = lax.ppermute(b, ("gx", "gy"), swaps(along_x, along_y, "gx", 1))

    tall = rows + 2 * DEEP_F
    z, k = call(
        functools.partial(pack_cols, along_x),
        [(rows + 3, cols, depth)] * 2,
        [],
        (right_side, coefficient, a, b),
        small,
    )
    k = lax.ppermute(k, "gy", pairs_from(0, along_y))
    z = lax.ppermute(z, ("gx", "gy"), swaps(along_x, along_y, "gy", 1))

    wide = (cols + 2 * DEEP_C, depth)
    half = (rows // 2, SUB, depth // 2)
    send, *state = call(
        functools.partial(fine_down, along_x, along_y),
        [half, (tall - 2,) + wide, (tall,) + wide, (tall + 1,) + wide]
        + [(tall,) + wide] * 3,
        [(tall + 2,) + wide, (tall,) + wide, (rows, cols, depth)],
        (right_side, coefficient, a, b, z, k),
        small,
    )
    chips = along_y // 2
    parts = [send] + [
        lax.ppermute(send, ("gx", "gy"), at_distance(along_x, along_y, "gy", distance))
        for distance in range(1, chips)
    ]
    shape = (chips * half[0],) + half[1:]
    (line,) = call(line_up, [shape], [], parts, small + 8 * math.prod(shape))
    own = [line] + [
        lax.ppermute(line, ("gx", "gy"), at_distance(along_x, along_y, "gx", distance))
        for distance in range(1, along_x)
    ]
    other = [lax.ppermute(line, "gy", pairs_from(0, along_y)) for line in own]

    rows1, cols1, depth1 = along_x * half[0], along_y * (cols // 2), half[2]
    whole1 = (rows1 + 2 * PAD + 1, cols1 + 2 * MARGIN, depth1)
    rows2, cols2 = rows1 // 2, cols1 // 2
    whole2 = (rows2 + 2, cols2 + 2 * MARGIN, depth1)
    span, broad = half[0] + 2 * PAD, 2 * SUB
    window = (span, broad + 2 * MARGIN, depth1)
    scratch = [whole1] * 7 + [(rows1, cols1, depth1)]
    scratch += [(rows2, cols2, depth1)] + [whole2] * 3
    scratch += [(span // 2 + 2,) + whole1[1:], window, (span, broad, depth1), window]
    scratch += [(span - 4, broad, depth1), ((span - 4) * wide[0], depth1)]
    scratch += [(tall,) + wide, (tall, cols, depth), (tall,) + wide]
    size = sum(4 * math.prod(s) for s in scratch)
    size += 2 * 4 * along_x * line.size + 4 * 8 * tall * wide[0] * wide[1]
    (out,) = call(
        functools.partial(coarse_and_up, along_x, along_y),
        [right_side.shape],
        scratch,
        (*own, *other, *state),
        size + (12 << 20),
    )
    return out


def solution(mesh):
    placed = (P("gx", "gy", None), P("gx", "gy", None))
    return jax.shard_map(
        body, mesh=mesh, in_specs=placed, out_specs=P("gx", "gy", None), check_vma=False
    )
```

```python
import functools
import math

import jax
import jax.numpy as jnp
from jax import lax
from jax.experimental import pallas as pl
from jax.experimental.pallas import tpu as pltpu
from jax.sharding import PartitionSpec as P

SMOOTH = 2
COARSE_STEPS = 6
SMOOTH_LOW = 0.5
SMOOTH_HIGH = 2.0
COARSE_LOW = 0.05
COARSE_HIGH = 2.0

DEEP_F = 2 * SMOOTH - 1
DEEP_C = 2 * SMOOTH
SUB = 8
PAD = 4
MARGIN = SUB
WRITTEN_OUT = 512

VMEM = pl.BlockSpec(memory_space=pltpu.VMEM)
F32 = jnp.float32


def chebyshev(low_end, high_end, sweeps):
    middle = 0.5 * (high_end + low_end)
    half_span = 0.5 * (high_end - low_end)
    sig_ratio = middle / half_span
    rho_now = 1.0 / sig_ratio
    coeff_pairs = []
    for sweep_num in range(1, sweeps):
        rho_next = 1.0 / (2.0 * sig_ratio - rho_now)
        coeff_pairs.append((rho_next * rho_now, 2.0 * rho_next / half_span))
        rho_now = rho_next
    return (1.0 / middle, coeff_pairs)


def each(count, registers, step):
    each_sum(count, registers, lambda i, carry: (step(i), carry)[1], 0)


def each_sum(count, registers, step, carry):
    if count * registers > WRITTEN_OUT:
        return lax.fori_loop(0, count, step, carry)
    for i in range(count):
        carry = step(i, carry)
    return carry


def turn(value, amount, axis):
    return pltpu.roll(value, amount % value.shape[axis], axis)


def iota(shape, axis):
    return lax.broadcasted_iota(jnp.int32, shape, axis)


def beside(v, below, above, w_below, w_above, w_cols, w_depth):
    span = below.shape[0]
    out = w_above * above + w_below * below
    out = out + w_cols[:span] * turn(v, -1, 0)[:span]
    out = out + turn(w_cols * v, 1, 0)[:span]
    v = v[:span]
    return out + w_depth * turn(v, -1, 1) + turn(w_depth * v, 1, 1)


def inside_cols(col, cols, along_y):
    gy = lax.axis_index("gy")
    after = (col >= cols) & (col < cols + DEEP_C) & (gy == along_y - 1)
    before = (col >= cols + DEEP_C) & (gy == 0)
    return jnp.logical_not(after | before)


def thirds(value):
    parts = []
    for _ in range(3):
        parts.append(value.astype(jnp.bfloat16))
        value = value - parts[-1].astype(F32)
    return parts


def exact_dot(a, b):
    if a.dtype == F32:
        terms = [jnp.dot(part, b, preferred_element_type=F32) for part in thirds(a)]
    else:
        terms = [jnp.dot(a, part, preferred_element_type=F32) for part in thirds(b)]
    return (terms[2] + terms[1]) + terms[0]


def call(kernel, out_shapes, scratch, args, limit):
    return pl.pallas_call(
        kernel,
        out_shape=[jax.ShapeDtypeStruct(s, F32) for s in out_shapes],
        in_specs=[VMEM] * len(args),
        out_specs=[VMEM] * len(out_shapes),
        scratch_shapes=[pltpu.VMEM(s, F32) for s in scratch],
        compiler_params=pltpu.CompilerParams(vmem_limit_bytes=limit),
    )(*args)


def pack_rows(f_ref, c_ref, a_ref, b_ref, sems):
    rows = f_ref.shape[0]
    odd = lax.rem(lax.axis_index("gx"), 2)
    copies = []
    for ref, at_end in ((a_ref, 1 - odd), (b_ref, odd)):
        for whole_ref, first, count in ((f_ref, 0, DEEP_F), (c_ref, DEEP_F, DEEP_C)):
            copies.append(
                pltpu.make_async_copy(
                    whole_ref.at[pl.ds(at_end * (rows - count), count)],
                    ref.at[pl.ds(first, count)],
                    sems.at[len(copies)],
                )
            )
    for copy in copies:
        copy.start()
    for copy in copies:
        copy.wait()


def row_sources(rows, f_ref, c_ref, a_ref, b_ref):
    odd = lax.rem(lax.axis_index("gx"), 2) == 1

    def before(i):
        return jnp.where(odd, a_ref[i], b_ref[i])

    def after(i):
        return jnp.where(odd, b_ref[i], a_ref[i])

    def f_row(i):
        if i < 0:
            return before(DEEP_F + i)
        return f_ref[i] if i < rows else after(i - rows)

    def c_row(i):
        if i < 0:
            return before(DEEP_F + DEEP_C + i)
        return c_ref[i] if i < rows else after(DEEP_F + i - rows)

    return f_row, c_row


def pack_cols(f_ref, c_ref, a_ref, b_ref, z_ref, k_ref):
    rows = f_ref.shape[0]
    f_row, c_row = row_sources(rows, f_ref, c_ref, a_ref, b_ref)
    odd = lax.rem(lax.axis_index("gy"), 2) == 1
    sub = iota(f_ref.shape[1:], 0)
    low_half = sub < DEEP_C
    two_beyond, three_beyond = {-1: -2, rows: rows + 1}, {0: -3, rows - 1: rows + 2}
    for t in range(rows + 2):
        row = t - 1
        f, c = turn(f_row(row), DEEP_C, 0), c_row(row)
        first, last = jnp.where(low_half, c, f), jnp.where(low_half, f, c)
        if row in two_beyond:
            f, c = f_row(two_beyond[row]), c_row(two_beyond[row])
            first = jnp.where(sub >= 6, turn(c, 6, 0), jnp.where(sub == 3, turn(f, 3, 0), first))
            last = jnp.where(sub <= 1, turn(c, -6, 0), jnp.where(sub == 4, turn(f, -3, 0), last))
        if row in three_beyond:
            c = c_row(three_beyond[row])
            first = jnp.where(sub == 7, turn(c, 7, 0), first)
            last = jnp.where(sub == 0, turn(c, -7, 0), last)
        z_ref[t] = jnp.where(odd, last, first)
        k_ref[t] = jnp.where(odd, first, last)


def line_up(*refs):
    *block_refs, out_ref = refs
    here = lax.div(lax.axis_index("gy"), 2)
    size = block_refs[0].shape[0]
    for distance, ref in enumerate(block_refs):
        out_ref[pl.ds((here ^ distance) * size, size)] = ref[...]


def fine_down(
    along_x, along_y,
    f_ref, c_ref, a_ref, b_ref, z_ref, k_ref,
    send_ref, u_ref, fx_ref, wx_ref, wy_ref, wz_ref, inv_ref,
    cx_ref, v_ref, diag_ref,
):
    rows, cols, depth = f_ref.shape
    f_row, c_row = row_sources(rows, f_ref, c_ref, a_ref, b_ref)
    gx, gy = lax.axis_index("gx"), lax.axis_index("gy")
    odd = lax.rem(gy, 2) == 1
    low_half = iota((cols, depth), 0) < DEEP_C
    half_before = 0.5 * (gx > 0).astype(F32)
    half_after = 0.5 * (gx < along_x - 1).astype(F32)
    half_beside = jnp.where(low_half, 0.5 * (gy < along_y - 1).astype(F32), 0.5 * (gy > 0).astype(F32))
    wide = (cols + 2 * DEEP_C, depth)
    lane = iota(wide, 1)
    col = iota(wide, 0)
    col_inside = inside_cols(col, cols, along_y)
    inv_mid, ((keep, push),) = chebyshev(SMOOTH_LOW, SMOOTH_HIGH, SMOOTH)

    def sides(t):
        return jnp.where(odd, k_ref[t], z_ref[t]), jnp.where(odd, z_ref[t], k_ref[t])

    c_places = {-2: (0, 6), rows + 1: (rows + 1, 6), -3: (1, 7), rows + 2: (rows, 7)}
    f_places = {-2: (0, 3), rows + 1: (rows + 1, 3)}
    for t in range(rows + 2 * DEEP_C):
        row = t - DEEP_C
        half = half_before if row < 0 else 0.5 if row < rows else half_after
        beside_row = half_beside if 0 <= row < rows else half_beside * (2.0 * half)
        cx_ref[t, 0:cols] = half * c_row(row)
        s = row + DEEP_F
        if -1 <= row <= rows:
            left, right = sides(row + 1)
            cx_ref[t, cols:] = beside_row * jnp.where(low_half, right, left)
            f = turn(jnp.where(low_half, left, right), DEEP_C, 0)
        else:
            c = f = jnp.zeros((cols, depth), F32)
            if row in c_places:
                left, right = sides(c_places[row][0])
                c = jnp.where(low_half, turn(right, -c_places[row][1], 0), turn(left, c_places[row][1], 0))
            if row in f_places:
                f = jnp.where(low_half, turn(right, -f_places[row][1], 0), turn(left, f_places[row][1], 0))
            cx_ref[t, cols:] = beside_row * c
        if 0 <= s < rows + 2 * DEEP_F:
            fx_ref[s, 0:cols] = f_row(row)
            fx_ref[s, cols:] = f

    tall = rows + 2 * DEEP_F
    wx_ref[0] = cx_ref[0] + cx_ref[1]
    for s in range(tall):
        half = cx_ref[s + 1]
        above = half + cx_ref[s + 2]
        after = half + turn(half, -1, 0)
        deeper = jnp.where(lane == depth - 1, 0.0, half + turn(half, -1, 1))
        wx_ref[s + 1] = above
        wy_ref[s] = after
        wz_ref[s] = deeper
        diag = wx_ref[s] + above + after + turn(after, 1, 0) + deeper + turn(deeper, 1, 1)
        diag = diag + jnp.where((lane == 0) | (lane == depth - 1), half, 0.0)
        inside = col_inside
        if s < DEEP_F:
            inside = inside & (gx > 0)
        if s >= rows + DEEP_F:
            inside = inside & (gx < along_x - 1)
        inv = jnp.where(inside, 1.0 / diag, 0.0)
        if DEEP_F <= s < DEEP_F + rows:
            diag_ref[s - DEEP_F] = diag[:cols]
        inv_ref[s] = inv
        v_ref[s] = fx_ref[s] * inv * inv_mid

    def pulled(x_ref, shift, s, span):
        at = s - shift
        total = beside(
            x_ref[at], x_ref[at - 1, :span], x_ref[at + 1, :span],
            wx_ref[s, :span], wx_ref[s + 1, :span], wy_ref[s], wz_ref[s, :span],
        )
        return fx_ref[s, :span] + total

    for s in range(1, tall - 1):
        total = pulled(v_ref, 0, s, wide[0])
        u_ref[s - 1] = (1.0 + keep - push) * v_ref[s] + push * (inv_ref[s] * total)

    def residual(s):
        return pulled(u_ref, 1, s, cols) - diag_ref[s - DEEP_F] * u_ref[s - 1, :cols]

    half_rows = rows // 2
    summed = [residual(2 * i + DEEP_F) + residual(2 * i + 1 + DEEP_F) for i in range(half_rows)]
    summed += [c_ref[2 * i] + c_ref[2 * i + 1] for i in range(half_rows)]
    summed = jnp.concatenate(summed, axis=0)
    pairs = (depth, depth // 2)
    thin = exact_dot(summed, (iota(pairs, 0) // 2 == iota(pairs, 1)).astype(F32).astype(jnp.bfloat16))
    choice = (SUB * half_rows, summed.shape[0])
    line, source = iota(choice, 0), iota(choice, 1)
    block, place = line // SUB, line % SUB
    half_cols = cols // 2
    f_half = (place >= half_cols) == odd
    place = place % half_cols
    f_from = cols * block + 2 * place
    c_from = f_from + cols * half_rows
    from_f = (source == f_from) | (source == f_from + 1)
    from_c = (source == c_from) | (source == c_from + 1)
    picker = jnp.where(f_half, jnp.where(from_f, 0.5, 0.0), jnp.where(from_c, 0.0625, 0.0))
    tile = exact_dot(picker.astype(jnp.bfloat16), thin).reshape(half_rows, SUB, depth // 2)

    send_ref[...] = tile


def coarse_and_up(along_x, along_y, *refs):
    own_refs, other_refs, refs = refs[:along_x], refs[along_x : 2 * along_x], refs[2 * along_x :]
    u0_ref, fx_ref, wx0_ref, wy0_ref, wz0_ref, inv0_ref, out_ref, *refs = refs
    f_ref, h_ref, wx_ref, wy_ref, wz_ref, inv_ref, v_ref, diag_ref, f2_ref, h2_ref, e2_ref, e3_ref, *refs = refs
    py_ref, vw_ref, dw_ref, vx_ref, e1_ref, yy_ref, v0_ref, d0_ref, x0_ref = refs
    gx, gy = lax.axis_index("gx"), lax.axis_index("gy")
    odd = lax.rem(gy, 2) == 1
    brick1 = own_refs[0].shape[0] // (along_y // 2)
    rows1, cols1, depth1 = diag_ref.shape
    across = cols1 // SUB
    registers1 = across * (depth1 // 128)
    inv_mid, ((keep, push),) = chebyshev(SMOOTH_LOW, SMOOTH_HIGH, SMOOTH)
    inner = pl.ds(MARGIN, cols1)

    low_half = iota((SUB, depth1), 0) < SUB // 2

    chip = lax.div(gy, 2)

    def place(distance, z):
        own_ref, other_ref, x = own_refs[distance], other_refs[distance], gx ^ distance
        at = z * SUB + MARGIN
        if not isinstance(z, int):
            at = pl.multiple_of(at, SUB)
        swapped = odd == (z == chip)
        for i in range(brick1):
            own, other = own_ref[z * brick1 + i], other_ref[z * brick1 + i]
            low, high = jnp.where(swapped, other, own), jnp.where(swapped, own, other)
            row = PAD + x * brick1 + i
            f_ref[row, pl.ds(at, SUB)] = jnp.where(low_half, low, high)
            h_ref[row, pl.ds(at, SUB)] = turn(jnp.where(low_half, high, low), SUB // 2, 0)

    for distance in range(along_x):
        each(across, brick1, functools.partial(place, distance))

    def clear_beside(ref, row):
        zero = jnp.zeros((MARGIN, depth1), F32)
        ref[row, 0:MARGIN] = zero
        ref[row, pl.ds(ref.shape[1] - MARGIN, MARGIN)] = zero

    def clear(i):
        for ref in (h_ref, v_ref):
            clear_beside(ref, PAD + i)
        wy_ref[PAD + i, 0:MARGIN] = jnp.zeros((MARGIN, depth1), F32)

    each(rows1, 1, clear)
    for ref in (h_ref, v_ref):
        for row in (PAD - 1, PAD + rows1):
            ref[row] = jnp.zeros(ref.shape[1:], F32)

    def weigh(ref, row, cols, stride):
        half = ref[row, pl.ds(MARGIN, cols)]
        lane = iota(half.shape, 1)
        first, last = lane < stride, lane >= half.shape[1] - stride
        around = [ref[row - 1, pl.ds(MARGIN, cols)], ref[row + 1, pl.ds(MARGIN, cols)]]
        around += [ref[row, pl.ds(MARGIN - 1, cols)], ref[row, pl.ds(MARGIN + 1, cols)]]
        around += [
            jnp.where(first, 0.0, turn(half, stride, 1)),
            jnp.where(last, 0.0, turn(half, -stride, 1)),
        ]
        total = (around[0] + around[1]) + (around[2] + around[3]) + (around[4] + around[5])
        return half, around, 6.0 * half + total, first, last

    wx_ref[PAD, inner] = h_ref[PAD, inner]

    def weigh1(i):
        row = PAD + i
        half, around, diag, _, last = weigh(h_ref, row, cols1, 1)
        inv = 1.0 / diag
        wx_ref[row + 1, inner] = half + around[1]
        wy_ref[row, inner] = half + around[3]
        wz_ref[row, inner] = jnp.where(last, 0.0, half + around[5])
        diag_ref[i] = diag
        inv_ref[row, inner] = inv
        v_ref[row, inner] = f_ref[row, inner] * inv * inv_mid

    each(rows1, registers1, weigh1)

    rows2, cols2 = rows1 // 2, cols1 // 2
    shape2 = (cols2, depth1)
    registers2 = max(registers1 // 2, 1)
    zero2 = jnp.zeros(shape2, F32)
    lane2, col2 = iota(shape2, 1), iota(shape2, 0)
    even2 = lane2 % 2 == 0
    inner2 = pl.ds(MARGIN, cols2)

    def fold(ref, row):
        half = ref[row, pl.ds(MARGIN, cols2, stride=2), :] + ref[row, pl.ds(MARGIN + 1, cols2, stride=2), :]
        return half + turn(half, -1, 1)

    def restrict_h(k):
        row = PAD + 2 * k
        h2_ref[k + 1, inner2] = 0.125 * (fold(h_ref, row) + fold(h_ref, row + 1))

    each(rows2, 2 * registers1, restrict_h)
    u_ref = h_ref

    def pulled1(x_ref, at, x_first, row, first, count):
        def part(ref, i, begin, shift=0):
            return ref[i, pl.ds(begin + shift, count), :]

        x, depths = part(x_ref, at, x_first), part(wz_ref, row, first)
        total = part(wx_ref, row + 1, first) * part(x_ref, at + 1, x_first)
        total = total + part(wx_ref, row, first) * part(x_ref, at - 1, x_first)
        total = total + part(wy_ref, row, first) * part(x_ref, at, x_first, 1)
        total = total + part(wy_ref, row, first, -1) * part(x_ref, at, x_first, -1)
        total = total + depths * turn(x, -1, 1) + turn(depths * x, 1, 1)
        return x, part(f_ref, row, first) + total

    def second1(i):
        row = PAD + i
        v, total = pulled1(v_ref, row, MARGIN, row, MARGIN, cols1)
        u_ref[row, inner] = (1.0 + keep - push) * v + push * (inv_ref[row, inner] * total)

    each(rows1, registers1, second1)

    def residual1(i):
        u, total = pulled1(u_ref, PAD + i, MARGIN, PAD + i, MARGIN, cols1)
        return total - diag_ref[i] * u

    def restrict(k):
        v_ref[k, inner] = residual1(2 * k) + residual1(2 * k + 1)
        f2_ref[k] = 0.5 * fold(v_ref, k)

    each(rows2, 2 * registers1, restrict)
    for ref in (h2_ref, e2_ref, e3_ref):
        for row in (0, rows2 + 1):
            ref[row] = jnp.zeros(ref.shape[1:], F32)

    def clear2(k):
        for ref in (h2_ref, e2_ref, e3_ref):
            clear_beside(ref, k + 1)

    each(rows2, 1, clear2)
    inv_mid2, pairs2 = chebyshev(COARSE_LOW, COARSE_HIGH, COARSE_STEPS)

    def kept(at, k):
        ref, at, begin = (diag_ref, at, 0) if at < 4 else (v_ref, at - 4, MARGIN)
        return ref, 2 * k + at // 2, pl.ds(begin + at % 2 * cols2, cols2)

    def keep_value(at, k, value):
        ref, row, columns = kept(at, k)
        ref[row, columns] = value

    def kept_value(at, k):
        ref, row, columns = kept(at, k)
        return ref[row, columns]

    diagonal, direction = 6, 7

    def weigh2(k, edges):
        half, around, diag, first, last = weigh(h2_ref, k + 1, cols2, 2)
        inv = 1.0 / diag
        scaled = half * inv
        for at in range(4):
            keep_value(at, k, scaled + around[at] * inv)
        keep_value(4, k, jnp.where(first, 0.0, scaled + around[4] * inv))
        keep_value(5, k, jnp.where(last, 0.0, scaled + around[5] * inv))
        keep_value(diagonal, k, diag)
        f = f2_ref[k] * inv
        f2_ref[k] = f
        d = f * inv_mid2
        keep_value(direction, k, d)
        e2_ref[k + 1, inner2] = d
        edges = edges + jnp.where((col2 == 0) | (col2 == cols2 - 1), half, 0.0)
        edges = edges + jnp.where(first | last, half, 0.0)
        return edges + jnp.where(k == 0, half, 0.0) + jnp.where(k == rows2 - 1, half, 0.0)

    edges = each_sum(rows2, registers2, weigh2, zero2)

    def residual2(e_ref, k):
        e = e_ref[k + 1, inner2]
        r = f2_ref[k] - e + kept_value(0, k) * e_ref[k, inner2] + kept_value(1, k) * e_ref[k + 2, inner2]
        r = r + kept_value(2, k) * e_ref[k + 1, pl.ds(MARGIN - 1, cols2)]
        r = r + kept_value(3, k) * e_ref[k + 1, pl.ds(MARGIN + 1, cols2)]
        return e, r + (kept_value(4, k) * turn(e, 2, 1) + kept_value(5, k) * turn(e, -2, 1))

    now_ref, next_ref = e2_ref, e3_ref
    for keep2, push2 in pairs2:

        def step2(k):
            e, r = residual2(now_ref, k)
            d = keep2 * kept_value(direction, k) + push2 * r
            keep_value(direction, k, d)
            next_ref[k + 1, inner2] = e + d

        each(rows2, registers2, step2)
        now_ref, next_ref = next_ref, now_ref

    def add_residual(k, total):
        return total + kept_value(diagonal, k) * residual2(now_ref, k)[1]

    total = each_sum(rows2, registers2, add_residual, zero2)
    top = jnp.sum(jnp.where(even2, total, 0.0), axis=(0, 1), keepdims=True)
    bottom = jnp.sum(jnp.where(even2, edges, 0.0), axis=(0, 1), keepdims=True)
    mean = top / bottom

    span, broad = brick1 + 2 * PAD, 2 * SUB
    start, first_col = gx * brick1 - PAD, gy * (cols1 // along_y) - PAD
    coarse_span = span // 2 + 2
    for k in range(coarse_span):
        row = lax.div(gx * brick1, 2) - PAD // 2 - 1 + k
        good = (row >= 0) & (row < rows2)
        e = now_ref[jnp.clip(row, 0, rows2 - 1) + 1, inner2] + mean
        e = jnp.where(good, e, 0.0)
        back = jnp.where(lane2 < 2, 0.0, turn(e, 2, 1))
        ahead = jnp.where(lane2 >= depth1 - 2, 0.0, turn(e, -1, 1))
        home = jnp.where(even2, e, turn(e, 1, 1))
        e = 0.75 * home + 0.25 * jnp.where(even2, back, ahead)
        back = jnp.where(col2 == 0, 0.0, turn(e, 1, 0))
        ahead = jnp.where(col2 == cols2 - 1, 0.0, turn(e, -1, 0))
        py_ref[k, pl.ds(MARGIN, cols2, stride=2), :] = 0.75 * e + 0.25 * back
        py_ref[k, pl.ds(MARGIN + 1, cols2, stride=2), :] = 0.75 * e + 0.25 * ahead

    window, held = pl.ds(MARGIN + first_col, broad), pl.ds(MARGIN, broad)
    col1 = first_col + iota((broad, depth1), 0)
    col_good = (col1 >= 0) & (col1 < cols1)

    def inside1(m):
        return col_good & ((start + m >= 0) & (start + m < rows1))

    for m in range(span):
        near = m // 2 + 1
        far = near - 1 if m % 2 == 0 else near + 1
        total = u_ref[PAD + start + m, window, :]
        total = total + (0.75 * py_ref[near, window, :] + 0.25 * py_ref[far, window, :])
        vw_ref[m, held] = jnp.where(inside1(m), total, 0.0)
    for m in range(1, span - 1):
        row = PAD + start + m
        v, total = pulled1(vw_ref, m, MARGIN, row, MARGIN + first_col, broad)
        d = (inv_ref[row, window, :] * total - v) * inv_mid
        dw_ref[m] = d
        vx_ref[m, held] = jnp.where(inside1(m), v + d, 0.0)
    for m in range(2, span - 2):
        row = PAD + start + m
        v, total = pulled1(vx_ref, m, MARGIN, row, MARGIN + first_col, broad)
        e = (1.0 - push) * v + (keep * dw_ref[m] + push * (inv_ref[row, window, :] * total))
        e1_ref[m - 2] = jnp.where(inside1(m), e, 0.0)

    rows, cols, depth = out_ref.shape
    wide = (cols + 2 * DEEP_C, depth)
    half_wide = wide[0] // 2
    for k in range(span - 4):
        e = turn(e1_ref[k, pl.ds(PAD - DEEP_C // 2, half_wide), :], -(DEEP_C // 2), 0)
        at = k * wide[0]
        yy_ref[pl.ds(at, half_wide, stride=2), :] = 0.75 * e + 0.25 * turn(e, 1, 0)
        yy_ref[pl.ds(at + 1, half_wide, stride=2), :] = 0.75 * e + 0.25 * turn(e, -1, 0)
    spread = (depth1, depth)
    from_cell, to_cell = iota(spread, 0), iota(spread, 1)
    home = to_cell // 2
    near_cell = jnp.where(to_cell % 2 == 0, home - 1, home + 1)
    weights = jnp.where(from_cell == home, 0.75, 0.0) + jnp.where(from_cell == near_cell, 0.25, 0.0)
    carried = exact_dot(yy_ref[...], weights.astype(jnp.bfloat16)).reshape(span - 4, wide[0], depth)
    col_inside = inside_cols(iota(wide, 0), cols, along_y)
    for s in range(1, rows + 2 * DEEP_F - 1):
        row = s - DEEP_F
        near = row // 2 + 2
        far = near - 1 if row % 2 == 0 else near + 1
        inside = col_inside
        if row < 0:
            inside = inside & (gx > 0)
        if row >= rows:
            inside = inside & (gx < along_x - 1)
        total = u0_ref[s - 1] + (0.75 * carried[near] + 0.25 * carried[far])
        v0_ref[s] = jnp.where(inside, total, 0.0)

    def pulled0(x_ref, s, span):
        return fx_ref[s, :span] + beside(
            x_ref[s], x_ref[s - 1, :span], x_ref[s + 1, :span],
            wx0_ref[s, :span], wx0_ref[s + 1, :span], wy0_ref[s], wz0_ref[s, :span],
        )

    for s in range(2, rows + 2 * DEEP_F - 2):
        v = v0_ref[s]
        d = (inv0_ref[s] * pulled0(v0_ref, s, wide[0]) - v) * inv_mid
        d0_ref[s] = d[:cols]
        x0_ref[s] = v + d
    for i in range(rows):
        s = i + DEEP_F
        total = inv0_ref[s, :cols] * pulled0(x0_ref, s, cols)
        out_ref[i] = (1.0 - push) * x0_ref[s, :cols] + (keep * d0_ref[s] + push * total)


def pairs_from(first, count):
    swaps = []
    for i in range(first, first + count, 2):
        a, b = i % count, (i + 1) % count
        swaps += [(a, b), (b, a)]
    return swaps


def swaps(along_x, along_y, axis, first):
    pairs = []
    for x in range(along_x):
        for y in range(along_y):
            place, count = (x, along_x) if axis == "gx" else (y, along_y)
            other = place + 1 if (place - first) % 2 == 0 else place - 1
            if 0 <= other < count:
                to = (other, y) if axis == "gx" else (x, other)
            else:
                to = (x, y ^ 1) if axis == "gx" else (x ^ 1, y)
            pairs.append((x * along_y + y, to[0] * along_y + to[1]))
    return pairs


def at_distance(along_x, along_y, axis, distance):
    pairs = []
    for x in range(along_x):
        for y in range(along_y):
            to = (x ^ distance, y) if axis == "gx" else (x, y ^ (2 * distance + 1))
            pairs.append((x * along_y + y, to[0] * along_y + to[1]))
    return pairs


def body(right_side, coefficient):
    along_x, along_y = lax.axis_size("gx"), lax.axis_size("gy")
    rows, cols, depth = right_side.shape
    assert cols == 2 * DEEP_C and rows % 4 == 0 and depth % 256 == 0
    assert along_x & (along_x - 1) == 0 and along_y & (along_y - 1) == 0 and along_x * along_y > 3
    small = 16 << 20
    strip = (DEEP_F + DEEP_C, cols, depth)
    odd = lax.rem(lax.axis_index("gx"), 2) == 1
    first = jnp.concatenate([right_side[:DEEP_F], coefficient[:DEEP_C]])
    last = jnp.concatenate([right_side[rows - DEEP_F :], coefficient[rows - DEEP_C :]])
    a, b = jnp.where(odd, first, last), jnp.where(odd, last, first)
    a = lax.ppermute(a, "gx", pairs_from(0, along_x))
    b = lax.ppermute(b, ("gx", "gy"), swaps(along_x, along_y, "gx", 1))

    tall = rows + 2 * DEEP_F
    z, k = call(
        pack_cols,
        [(rows + 2, cols, depth)] * 2,
        [],
        (right_side, coefficient, a, b),
        small,
    )
    k = lax.ppermute(k, "gy", pairs_from(0, along_y))
    z = lax.ppermute(z, ("gx", "gy"), swaps(along_x, along_y, "gy", 1))

    wide = (cols + 2 * DEEP_C, depth)
    half = (rows // 2, SUB, depth // 2)
    send, *state = call(
        functools.partial(fine_down, along_x, along_y),
        [half, (tall - 2,) + wide, (tall,) + wide, (tall + 1,) + wide]
        + [(tall,) + wide] * 3,
        [(tall + 2,) + wide, (tall,) + wide, (rows, cols, depth)],
        (right_side, coefficient, a, b, z, k),
        small,
    )
    chips = along_y // 2
    parts = [send] + [
        lax.ppermute(send, ("gx", "gy"), at_distance(along_x, along_y, "gy", distance))
        for distance in range(1, chips)
    ]
    shape = (chips * half[0],) + half[1:]
    (line,) = call(line_up, [shape], [], parts, small + 8 * math.prod(shape))
    own = [line] + [
        lax.ppermute(line, ("gx", "gy"), at_distance(along_x, along_y, "gx", distance))
        for distance in range(1, along_x)
    ]
    other = [lax.ppermute(line, "gy", pairs_from(0, along_y)) for line in own]

    rows1, cols1, depth1 = along_x * half[0], along_y * (cols // 2), half[2]
    whole1 = (rows1 + 2 * PAD + 1, cols1 + 2 * MARGIN, depth1)
    rows2, cols2 = rows1 // 2, cols1 // 2
    whole2 = (rows2 + 2, cols2 + 2 * MARGIN, depth1)
    span, broad = half[0] + 2 * PAD, 2 * SUB
    window = (span, broad + 2 * MARGIN, depth1)
    scratch = [whole1] * 7 + [(rows1, cols1, depth1)]
    scratch += [(rows2, cols2, depth1)] + [whole2] * 3
    scratch += [(span // 2 + 2,) + whole1[1:], window, (span, broad, depth1), window]
    scratch += [(span - 4, broad, depth1), ((span - 4) * wide[0], depth1)]
    scratch += [(tall,) + wide, (tall, cols, depth), (tall,) + wide]
    size = sum(4 * math.prod(s) for s in scratch)
    size += 2 * 4 * along_x * line.size + 4 * 8 * tall * wide[0] * wide[1]
    (out,) = call(
        functools.partial(coarse_and_up, along_x, along_y),
        [right_side.shape],
        scratch,
        (*own, *other, *state),
        size + (12 << 20),
    )
    return out


def solution(mesh):
    placed = (P("gx", "gy", None), P("gx", "gy", None))
    return jax.shard_map(
        body, mesh=mesh, in_specs=placed, out_specs=P("gx", "gy", None), check_vma=False
    )
```

```python
import functools
import math

import jax
import jax.numpy as jnp
from jax import lax
from jax.experimental import pallas as pl
from jax.experimental.pallas import tpu as pltpu
from jax.sharding import PartitionSpec as P

SMOOTH = 2
COARSE_STEPS = 6
SMOOTH_LOW = 0.5
SMOOTH_HIGH = 2.0
COARSE_LOW = 0.05
COARSE_HIGH = 2.0

DEEP_F = 2 * SMOOTH - 1
DEEP_C = 2 * SMOOTH
SUB = 8
PAD = 4
MARGIN = SUB
WRITTEN_OUT = 512

VMEM = pl.BlockSpec(memory_space=pltpu.VMEM)
F32 = jnp.float32


def chebyshev(low_end, high_end, sweeps):
    middle = 0.5 * (high_end + low_end)
    half_span = 0.5 * (high_end - low_end)
    sig_ratio = middle / half_span
    rho_now = 1.0 / sig_ratio
    coeff_pairs = []
    for sweep_num in range(1, sweeps):
        rho_next = 1.0 / (2.0 * sig_ratio - rho_now)
        coeff_pairs.append((rho_next * rho_now, 2.0 * rho_next / half_span))
        rho_now = rho_next
    return (1.0 / middle, coeff_pairs)


def each(count, registers, step):
    each_sum(count, registers, lambda i, carry: (step(i), carry)[1], 0)


def each_sum(count, registers, step, carry):
    if count * registers > WRITTEN_OUT:
        return lax.fori_loop(0, count, step, carry)
    for i in range(count):
        carry = step(i, carry)
    return carry


def turn(value, amount, axis):
    return pltpu.roll(value, amount % value.shape[axis], axis)


def iota(shape, axis):
    return lax.broadcasted_iota(jnp.int32, shape, axis)


def beside(v, below, above, w_below, w_above, w_cols, w_depth):
    span = below.shape[0]
    out = w_above * above + w_below * below
    out = out + w_cols[:span] * turn(v, -1, 0)[:span]
    out = out + turn(w_cols * v, 1, 0)[:span]
    v = v[:span]
    return out + w_depth * turn(v, -1, 1) + turn(w_depth * v, 1, 1)


def inside_cols(col, cols, along_y):
    gy = lax.axis_index("gy")
    after = (col >= cols) & (col < cols + DEEP_C) & (gy == along_y - 1)
    before = (col >= cols + DEEP_C) & (gy == 0)
    return jnp.logical_not(after | before)


def thirds(value):
    parts = []
    for _ in range(3):
        parts.append(value.astype(jnp.bfloat16))
        value = value - parts[-1].astype(F32)
    return parts


def exact_dot(a, b):
    if a.dtype == F32:
        terms = [jnp.dot(part, b, preferred_element_type=F32) for part in thirds(a)]
    else:
        terms = [jnp.dot(a, part, preferred_element_type=F32) for part in thirds(b)]
    return (terms[2] + terms[1]) + terms[0]


def call(kernel, out_shapes, scratch, args, limit):
    return pl.pallas_call(
        kernel,
        out_shape=[jax.ShapeDtypeStruct(s, F32) for s in out_shapes],
        in_specs=[VMEM] * len(args),
        out_specs=[VMEM] * len(out_shapes),
        scratch_shapes=[pltpu.VMEM(s, F32) for s in scratch],
        compiler_params=pltpu.CompilerParams(vmem_limit_bytes=limit),
    )(*args)


def pack_rows(f_ref, c_ref, a_ref, b_ref, sems):
    rows = f_ref.shape[0]
    odd = lax.rem(lax.axis_index("gx"), 2)
    copies = []
    for ref, at_end in ((a_ref, 1 - odd), (b_ref, odd)):
        for whole_ref, first, count in ((f_ref, 0, DEEP_F), (c_ref, DEEP_F, DEEP_C)):
            copies.append(
                pltpu.make_async_copy(
                    whole_ref.at[pl.ds(at_end * (rows - count), count)],
                    ref.at[pl.ds(first, count)],
                    sems.at[len(copies)],
                )
            )
    for copy in copies:
        copy.start()
    for copy in copies:
        copy.wait()


def row_sources(rows, f_ref, c_ref, a_ref, b_ref):
    odd = lax.rem(lax.axis_index("gx"), 2) == 1

    def before(i):
        return jnp.where(odd, a_ref[i], b_ref[i])

    def after(i):
        return jnp.where(odd, b_ref[i], a_ref[i])

    def f_row(i):
        if i < 0:
            return before(DEEP_F + i)
        return f_ref[i] if i < rows else after(i - rows)

    def c_row(i):
        if i < 0:
            return before(DEEP_F + DEEP_C + i)
        return c_ref[i] if i < rows else after(DEEP_F + i - rows)

    return f_row, c_row


def pack_cols(f_ref, c_ref, a_ref, b_ref, z_ref, k_ref):
    rows = f_ref.shape[0]
    f_row, c_row = row_sources(rows, f_ref, c_ref, a_ref, b_ref)
    odd = lax.rem(lax.axis_index("gy"), 2) == 1
    sub = iota(f_ref.shape[1:], 0)
    low_half = sub < DEEP_C
    two_beyond, three_beyond = {-1: -2, rows: rows + 1}, {0: -3, rows - 1: rows + 2}
    for t in range(rows + 2):
        row = t - 1
        f, c = turn(f_row(row), DEEP_C, 0), c_row(row)
        first, last = jnp.where(low_half, c, f), jnp.where(low_half, f, c)
        if row in two_beyond:
            f, c = f_row(two_beyond[row]), c_row(two_beyond[row])
            first = jnp.where(sub >= 6, turn(c, 6, 0), jnp.where(sub == 3, turn(f, 3, 0), first))
            last = jnp.where(sub <= 1, turn(c, -6, 0), jnp.where(sub == 4, turn(f, -3, 0), last))
        if row in three_beyond:
            c = c_row(three_beyond[row])
            first = jnp.where(sub == 7, turn(c, 7, 0), first)
            last = jnp.where(sub == 0, turn(c, -7, 0), last)
        z_ref[t] = jnp.where(odd, last, first)
        k_ref[t] = jnp.where(odd, first, last)


def line_up(*refs):
    *block_refs, out_ref = refs
    here = lax.div(lax.axis_index("gy"), 2)
    size = block_refs[0].shape[0]
    for distance, ref in enumerate(block_refs):
        out_ref[pl.ds((here ^ distance) * size, size)] = ref[...]


def fine_down(
    along_x, along_y,
    f_ref, c_ref, a_ref, b_ref, z_ref, k_ref,
    send_ref, u_ref, fx_ref, wx_ref, wy_ref, wz_ref, inv_ref,
    cx_ref, v_ref, diag_ref,
):
    rows, cols, depth = f_ref.shape
    f_row, c_row = row_sources(rows, f_ref, c_ref, a_ref, b_ref)
    gx, gy = lax.axis_index("gx"), lax.axis_index("gy")
    odd = lax.rem(gy, 2) == 1
    low_half = iota((cols, depth), 0) < DEEP_C
    half_before = 0.5 * (gx > 0).astype(F32)
    half_after = 0.5 * (gx < along_x - 1).astype(F32)
    half_beside = jnp.where(low_half, 0.5 * (gy < along_y - 1).astype(F32), 0.5 * (gy > 0).astype(F32))
    wide = (cols + 2 * DEEP_C, depth)
    lane = iota(wide, 1)
    col = iota(wide, 0)
    col_inside = inside_cols(col, cols, along_y)
    inv_mid, ((keep, push),) = chebyshev(SMOOTH_LOW, SMOOTH_HIGH, SMOOTH)

    def sides(t):
        return jnp.where(odd, k_ref[t], z_ref[t]), jnp.where(odd, z_ref[t], k_ref[t])

    c_places = {-2: (0, 6), rows + 1: (rows + 1, 6), -3: (1, 7), rows + 2: (rows, 7)}
    f_places = {-2: (0, 3), rows + 1: (rows + 1, 3)}
    for t in range(rows + 2 * DEEP_C):
        row = t - DEEP_C
        half = half_before if row < 0 else 0.5 if row < rows else half_after
        beside_row = half_beside if 0 <= row < rows else half_beside * (2.0 * half)
        cx_ref[t, 0:cols] = half * c_row(row)
        s = row + DEEP_F
        if -1 <= row <= rows:
            left, right = sides(row + 1)
            cx_ref[t, cols:] = beside_row * jnp.where(low_half, right, left)
            f = turn(jnp.where(low_half, left, right), DEEP_C, 0)
        else:
            c = f = jnp.zeros((cols, depth), F32)
            if row in c_places:
                left, right = sides(c_places[row][0])
                c = jnp.where(low_half, turn(right, -c_places[row][1], 0), turn(left, c_places[row][1], 0))
            if row in f_places:
                f = jnp.where(low_half, turn(right, -f_places[row][1], 0), turn(left, f_places[row][1], 0))
            cx_ref[t, cols:] = beside_row * c
        if 0 <= s < rows + 2 * DEEP_F:
            fx_ref[s, 0:cols] = f_row(row)
            fx_ref[s, cols:] = f

    tall = rows + 2 * DEEP_F
    wx_ref[0] = cx_ref[0] + cx_ref[1]
    for s in range(tall):
        half = cx_ref[s + 1]
        above = half + cx_ref[s + 2]
        after = half + turn(half, -1, 0)
        deeper = jnp.where(lane == depth - 1, 0.0, half + turn(half, -1, 1))
        wx_ref[s + 1] = above
        inner = 0 < s < tall - 1
        if inner:
            wy_ref[s] = after
            wz_ref[s] = deeper
        diag = wx_ref[s] + above + after + turn(after, 1, 0) + deeper + turn(deeper, 1, 1)
        diag = diag + jnp.where((lane == 0) | (lane == depth - 1), half, 0.0)
        inside = col_inside
        if s < DEEP_F:
            inside = inside & (gx > 0)
        if s >= rows + DEEP_F:
            inside = inside & (gx < along_x - 1)
        inv = jnp.where(inside, 1.0 / diag, 0.0)
        if DEEP_F <= s < DEEP_F + rows:
            diag_ref[s - DEEP_F] = diag[:cols]
        if inner:
            inv_ref[s] = inv
        span = wide[0] if inner else cols
        v_ref[s, :span] = fx_ref[s, :span] * inv[:span] * inv_mid

    def pulled(x_ref, shift, s, span):
        at = s - shift
        total = beside(
            x_ref[at], x_ref[at - 1, :span], x_ref[at + 1, :span],
            wx_ref[s, :span], wx_ref[s + 1, :span], wy_ref[s], wz_ref[s, :span],
        )
        return fx_ref[s, :span] + total

    for s in range(1, tall - 1):
        span = wide[0] if 1 < s < tall - 2 else cols
        total = pulled(v_ref, 0, s, span)
        u_ref[s - 1, :span] = (1.0 + keep - push) * v_ref[s, :span] + push * (inv_ref[s, :span] * total)

    def residual(s):
        return pulled(u_ref, 1, s, cols) - diag_ref[s - DEEP_F] * u_ref[s - 1, :cols]

    half_rows = rows // 2
    summed = [residual(2 * i + DEEP_F) + residual(2 * i + 1 + DEEP_F) for i in range(half_rows)]
    summed += [c_ref[2 * i] + c_ref[2 * i + 1] for i in range(half_rows)]
    summed = jnp.concatenate(summed, axis=0)
    pairs = (depth, depth // 2)
    thin = exact_dot(summed, (iota(pairs, 0) // 2 == iota(pairs, 1)).astype(F32).astype(jnp.bfloat16))
    choice = (SUB * half_rows, summed.shape[0])
    line, source = iota(choice, 0), iota(choice, 1)
    block, place = line // SUB, line % SUB
    half_cols = cols // 2
    f_half = (place >= half_cols) == odd
    place = place % half_cols
    f_from = cols * block + 2 * place
    c_from = f_from + cols * half_rows
    from_f = (source == f_from) | (source == f_from + 1)
    from_c = (source == c_from) | (source == c_from + 1)
    picker = jnp.where(f_half, jnp.where(from_f, 0.5, 0.0), jnp.where(from_c, 0.0625, 0.0))
    tile = exact_dot(picker.astype(jnp.bfloat16), thin).reshape(half_rows, SUB, depth // 2)

    send_ref[...] = tile


def coarse_and_up(along_x, along_y, *refs):
    own_refs, other_refs, refs = refs[:along_x], refs[along_x : 2 * along_x], refs[2 * along_x :]
    u0_ref, fx_ref, wx0_ref, wy0_ref, wz0_ref, inv0_ref, out_ref, *refs = refs
    f_ref, h_ref, wx_ref, wy_ref, wz_ref, inv_ref, v_ref, diag_ref, f2_ref, h2_ref, e2_ref, e3_ref, *refs = refs
    py_ref, vw_ref, dw_ref, vx_ref, e1_ref, yy_ref, v0_ref, d0_ref, x0_ref = refs
    gx, gy = lax.axis_index("gx"), lax.axis_index("gy")
    odd = lax.rem(gy, 2) == 1
    brick1 = own_refs[0].shape[0] // (along_y // 2)
    rows1, cols1, depth1 = diag_ref.shape
    across = cols1 // SUB
    registers1 = across * (depth1 // 128)
    inv_mid, ((keep, push),) = chebyshev(SMOOTH_LOW, SMOOTH_HIGH, SMOOTH)
    inner = pl.ds(MARGIN, cols1)

    low_half = iota((SUB, depth1), 0) < SUB // 2

    chip = lax.div(gy, 2)

    def place(distance, z):
        own_ref, other_ref, x = own_refs[distance], other_refs[distance], gx ^ distance
        at = z * SUB + MARGIN
        if not isinstance(z, int):
            at = pl.multiple_of(at, SUB)
        swapped = odd == (z == chip)
        for i in range(brick1):
            own, other = own_ref[z * brick1 + i], other_ref[z * brick1 + i]
            low, high = jnp.where(swapped, other, own), jnp.where(swapped, own, other)
            row = PAD + x * brick1 + i
            f_ref[row, pl.ds(at, SUB)] = jnp.where(low_half, low, high)
            h_ref[row, pl.ds(at, SUB)] = turn(jnp.where(low_half, high, low), SUB // 2, 0)

    for distance in range(along_x):
        each(across, brick1, functools.partial(place, distance))

    def clear_beside(ref, row):
        zero = jnp.zeros((MARGIN, depth1), F32)
        ref[row, 0:MARGIN] = zero
        ref[row, pl.ds(ref.shape[1] - MARGIN, MARGIN)] = zero

    def clear(i):
        for ref in (h_ref, v_ref):
            clear_beside(ref, PAD + i)
        wy_ref[PAD + i, 0:MARGIN] = jnp.zeros((MARGIN, depth1), F32)

    each(rows1, 1, clear)
    for ref in (h_ref, v_ref):
        for row in (PAD - 1, PAD + rows1):
            ref[row] = jnp.zeros(ref.shape[1:], F32)

    def weigh(ref, row, cols, stride):
        half = ref[row, pl.ds(MARGIN, cols)]
        lane = iota(half.shape, 1)
        first, last = lane < stride, lane >= half.shape[1] - stride
        around = [ref[row - 1, pl.ds(MARGIN, cols)], ref[row + 1, pl.ds(MARGIN, cols)]]
        around += [ref[row, pl.ds(MARGIN - 1, cols)], ref[row, pl.ds(MARGIN + 1, cols)]]
        around += [
            jnp.where(first, 0.0, turn(half, stride, 1)),
            jnp.where(last, 0.0, turn(half, -stride, 1)),
        ]
        total = (around[0] + around[1]) + (around[2] + around[3]) + (around[4] + around[5])
        return half, around, 6.0 * half + total, first, last

    wx_ref[PAD, inner] = h_ref[PAD, inner]

    def weigh1(i):
        row = PAD + i
        half, around, diag, _, last = weigh(h_ref, row, cols1, 1)
        inv = 1.0 / diag
        wx_ref[row + 1, inner] = half + around[1]
        wy_ref[row, inner] = half + around[3]
        wz_ref[row, inner] = jnp.where(last, 0.0, half + around[5])
        diag_ref[i] = diag
        inv_ref[row, inner] = inv
        v_ref[row, inner] = f_ref[row, inner] * inv * inv_mid

    each(rows1, registers1, weigh1)

    rows2, cols2 = rows1 // 2, cols1 // 2
    shape2 = (cols2, depth1)
    registers2 = max(registers1 // 2, 1)
    zero2 = jnp.zeros(shape2, F32)
    lane2, col2 = iota(shape2, 1), iota(shape2, 0)
    even2 = lane2 % 2 == 0
    inner2 = pl.ds(MARGIN, cols2)

    def fold(ref, row):
        half = ref[row, pl.ds(MARGIN, cols2, stride=2), :] + ref[row, pl.ds(MARGIN + 1, cols2, stride=2), :]
        return half + turn(half, -1, 1)

    def restrict_h(k):
        row = PAD + 2 * k
        h2_ref[k + 1, inner2] = 0.125 * (fold(h_ref, row) + fold(h_ref, row + 1))

    each(rows2, 2 * registers1, restrict_h)
    u_ref = h_ref

    def pulled1(x_ref, at, x_first, row, first, count):
        def part(ref, i, begin, shift=0):
            return ref[i, pl.ds(begin + shift, count), :]

        x, depths = part(x_ref, at, x_first), part(wz_ref, row, first)
        total = part(wx_ref, row + 1, first) * part(x_ref, at + 1, x_first)
        total = total + part(wx_ref, row, first) * part(x_ref, at - 1, x_first)
        total = total + part(wy_ref, row, first) * part(x_ref, at, x_first, 1)
        total = total + part(wy_ref, row, first, -1) * part(x_ref, at, x_first, -1)
        total = total + depths * turn(x, -1, 1) + turn(depths * x, 1, 1)
        return x, part(f_ref, row, first) + total

    def second1(i):
        row = PAD + i
        v, total = pulled1(v_ref, row, MARGIN, row, MARGIN, cols1)
        u_ref[row, inner] = (1.0 + keep - push) * v + push * (inv_ref[row, inner] * total)

    each(rows1, registers1, second1)

    def residual1(i):
        u, total = pulled1(u_ref, PAD + i, MARGIN, PAD + i, MARGIN, cols1)
        return total - diag_ref[i] * u

    def restrict(k):
        v_ref[k, inner] = residual1(2 * k) + residual1(2 * k + 1)
        f2_ref[k] = 0.5 * fold(v_ref, k)

    each(rows2, 2 * registers1, restrict)
    for ref in (h2_ref, e2_ref, e3_ref):
        for row in (0, rows2 + 1):
            ref[row] = jnp.zeros(ref.shape[1:], F32)

    def clear2(k):
        for ref in (h2_ref, e2_ref, e3_ref):
            clear_beside(ref, k + 1)

    each(rows2, 1, clear2)
    inv_mid2, pairs2 = chebyshev(COARSE_LOW, COARSE_HIGH, COARSE_STEPS)

    def kept(at, k):
        ref, at, begin = (diag_ref, at, 0) if at < 4 else (v_ref, at - 4, MARGIN)
        return ref, 2 * k + at // 2, pl.ds(begin + at % 2 * cols2, cols2)

    def keep_value(at, k, value):
        ref, row, columns = kept(at, k)
        ref[row, columns] = value

    def kept_value(at, k):
        ref, row, columns = kept(at, k)
        return ref[row, columns]

    diagonal, direction = 6, 7

    def weigh2(k, edges):
        half, around, diag, first, last = weigh(h2_ref, k + 1, cols2, 2)
        inv = 1.0 / diag
        scaled = half * inv
        for at in range(4):
            keep_value(at, k, scaled + around[at] * inv)
        keep_value(4, k, jnp.where(first, 0.0, scaled + around[4] * inv))
        keep_value(5, k, jnp.where(last, 0.0, scaled + around[5] * inv))
        keep_value(diagonal, k, diag)
        f = f2_ref[k] * inv
        f2_ref[k] = f
        d = f * inv_mid2
        keep_value(direction, k, d)
        e2_ref[k + 1, inner2] = d
        edges = edges + jnp.where((col2 == 0) | (col2 == cols2 - 1), half, 0.0)
        edges = edges + jnp.where(first | last, half, 0.0)
        return edges + jnp.where(k == 0, half, 0.0) + jnp.where(k == rows2 - 1, half, 0.0)

    edges = each_sum(rows2, registers2, weigh2, zero2)

    def residual2(e_ref, k):
        e = e_ref[k + 1, inner2]
        r = f2_ref[k] - e + kept_value(0, k) * e_ref[k, inner2] + kept_value(1, k) * e_ref[k + 2, inner2]
        r = r + kept_value(2, k) * e_ref[k + 1, pl.ds(MARGIN - 1, cols2)]
        r = r + kept_value(3, k) * e_ref[k + 1, pl.ds(MARGIN + 1, cols2)]
        return e, r + (kept_value(4, k) * turn(e, 2, 1) + kept_value(5, k) * turn(e, -2, 1))

    now_ref, next_ref = e2_ref, e3_ref
    for keep2, push2 in pairs2:

        def step2(k):
            e, r = residual2(now_ref, k)
            d = keep2 * kept_value(direction, k) + push2 * r
            keep_value(direction, k, d)
            next_ref[k + 1, inner2] = e + d

        each(rows2, registers2, step2)
        now_ref, next_ref = next_ref, now_ref

    def add_residual(k, total):
        return total + kept_value(diagonal, k) * residual2(now_ref, k)[1]

    total = each_sum(rows2, registers2, add_residual, zero2)
    top = jnp.sum(jnp.where(even2, total, 0.0), axis=(0, 1), keepdims=True)
    bottom = jnp.sum(jnp.where(even2, edges, 0.0), axis=(0, 1), keepdims=True)
    mean = top / bottom

    span, broad = brick1 + 2 * PAD, 2 * SUB
    start, first_col = gx * brick1 - PAD, gy * (cols1 // along_y) - PAD
    coarse_span = span // 2 + 2
    for k in range(coarse_span):
        row = lax.div(gx * brick1, 2) - PAD // 2 - 1 + k
        good = (row >= 0) & (row < rows2)
        e = now_ref[jnp.clip(row, 0, rows2 - 1) + 1, inner2] + mean
        e = jnp.where(good, e, 0.0)
        back = jnp.where(lane2 < 2, 0.0, turn(e, 2, 1))
        ahead = jnp.where(lane2 >= depth1 - 2, 0.0, turn(e, -1, 1))
        home = jnp.where(even2, e, turn(e, 1, 1))
        e = 0.75 * home + 0.25 * jnp.where(even2, back, ahead)
        back = jnp.where(col2 == 0, 0.0, turn(e, 1, 0))
        ahead = jnp.where(col2 == cols2 - 1, 0.0, turn(e, -1, 0))
        py_ref[k, pl.ds(MARGIN, cols2, stride=2), :] = 0.75 * e + 0.25 * back
        py_ref[k, pl.ds(MARGIN + 1, cols2, stride=2), :] = 0.75 * e + 0.25 * ahead

    window, held = pl.ds(MARGIN + first_col, broad), pl.ds(MARGIN, broad)
    col1 = first_col + iota((broad, depth1), 0)
    col_good = (col1 >= 0) & (col1 < cols1)

    def inside1(m):
        return col_good & ((start + m >= 0) & (start + m < rows1))

    for m in range(span):
        near = m // 2 + 1
        far = near - 1 if m % 2 == 0 else near + 1
        total = u_ref[PAD + start + m, window, :]
        total = total + (0.75 * py_ref[near, window, :] + 0.25 * py_ref[far, window, :])
        vw_ref[m, held] = jnp.where(inside1(m), total, 0.0)
    for m in range(1, span - 1):
        row = PAD + start + m
        v, total = pulled1(vw_ref, m, MARGIN, row, MARGIN + first_col, broad)
        d = (inv_ref[row, window, :] * total - v) * inv_mid
        dw_ref[m] = d
        vx_ref[m, held] = jnp.where(inside1(m), v + d, 0.0)
    for m in range(2, span - 2):
        row = PAD + start + m
        v, total = pulled1(vx_ref, m, MARGIN, row, MARGIN + first_col, broad)
        e = (1.0 - push) * v + (keep * dw_ref[m] + push * (inv_ref[row, window, :] * total))
        e1_ref[m - 2] = jnp.where(inside1(m), e, 0.0)

    rows, cols, depth = out_ref.shape
    wide = (cols + 2 * DEEP_C, depth)
    half_wide = wide[0] // 2
    for k in range(span - 4):
        e = turn(e1_ref[k, pl.ds(PAD - DEEP_C // 2, half_wide), :], -(DEEP_C // 2), 0)
        at = k * wide[0]
        yy_ref[pl.ds(at, half_wide, stride=2), :] = 0.75 * e + 0.25 * turn(e, 1, 0)
        yy_ref[pl.ds(at + 1, half_wide, stride=2), :] = 0.75 * e + 0.25 * turn(e, -1, 0)
    spread = (depth1, depth)
    from_cell, to_cell = iota(spread, 0), iota(spread, 1)
    home = to_cell // 2
    near_cell = jnp.where(to_cell % 2 == 0, home - 1, home + 1)
    weights = jnp.where(from_cell == home, 0.75, 0.0) + jnp.where(from_cell == near_cell, 0.25, 0.0)
    carried = exact_dot(yy_ref[...], weights.astype(jnp.bfloat16)).reshape(span - 4, wide[0], depth)
    col_inside = inside_cols(iota(wide, 0), cols, along_y)
    for s in range(1, rows + 2 * DEEP_F - 1):
        row = s - DEEP_F
        near = row // 2 + 2
        far = near - 1 if row % 2 == 0 else near + 1
        inside = col_inside
        if row < 0:
            inside = inside & (gx > 0)
        if row >= rows:
            inside = inside & (gx < along_x - 1)
        span = wide[0] if 1 < s < rows + 2 * DEEP_F - 2 else cols
        total = u0_ref[s - 1, :span] + (0.75 * carried[near][:span] + 0.25 * carried[far][:span])
        v0_ref[s, :span] = jnp.where(inside[:span], total, 0.0)

    def pulled0(x_ref, s, span):
        return fx_ref[s, :span] + beside(
            x_ref[s], x_ref[s - 1, :span], x_ref[s + 1, :span],
            wx0_ref[s, :span], wx0_ref[s + 1, :span], wy0_ref[s], wz0_ref[s, :span],
        )

    for s in range(2, rows + 2 * DEEP_F - 2):
        span = wide[0] if 2 < s < rows + 2 * DEEP_F - 3 else cols
        v = v0_ref[s, :span]
        d = (inv0_ref[s, :span] * pulled0(v0_ref, s, span) - v) * inv_mid
        d0_ref[s] = d[:cols]
        x0_ref[s, :span] = v + d
    for i in range(rows):
        s = i + DEEP_F
        total = inv0_ref[s, :cols] * pulled0(x0_ref, s, cols)
        out_ref[i] = (1.0 - push) * x0_ref[s, :cols] + (keep * d0_ref[s] + push * total)


def pairs_from(first, count):
    swaps = []
    for i in range(first, first + count, 2):
        a, b = i % count, (i + 1) % count
        swaps += [(a, b), (b, a)]
    return swaps


def swaps(along_x, along_y, axis, first):
    pairs = []
    for x in range(along_x):
        for y in range(along_y):
            place, count = (x, along_x) if axis == "gx" else (y, along_y)
            other = place + 1 if (place - first) % 2 == 0 else place - 1
            if 0 <= other < count:
                to = (other, y) if axis == "gx" else (x, other)
            else:
                to = (x, y ^ 1) if axis == "gx" else (x ^ 1, y)
            pairs.append((x * along_y + y, to[0] * along_y + to[1]))
    return pairs


def at_distance(along_x, along_y, axis, distance):
    pairs = []
    for x in range(along_x):
        for y in range(along_y):
            to = (x ^ distance, y) if axis == "gx" else (x, y ^ (2 * distance + 1))
            pairs.append((x * along_y + y, to[0] * along_y + to[1]))
    return pairs


def body(right_side, coefficient):
    along_x, along_y = lax.axis_size("gx"), lax.axis_size("gy")
    rows, cols, depth = right_side.shape
    assert cols == 2 * DEEP_C and rows % 4 == 0 and depth % 256 == 0
    assert along_x & (along_x - 1) == 0 and along_y & (along_y - 1) == 0 and along_x * along_y > 3
    small = 16 << 20
    strip = (DEEP_F + DEEP_C, cols, depth)
    odd = lax.rem(lax.axis_index("gx"), 2) == 1
    first = jnp.concatenate([right_side[:DEEP_F], coefficient[:DEEP_C]])
    last = jnp.concatenate([right_side[rows - DEEP_F :], coefficient[rows - DEEP_C :]])
    a, b = jnp.where(odd, first, last), jnp.where(odd, last, first)
    a = lax.ppermute(a, "gx", pairs_from(0, along_x))
    b = lax.ppermute(b, ("gx", "gy"), swaps(along_x, along_y, "gx", 1))

    tall = rows + 2 * DEEP_F
    z, k = call(
        pack_cols,
        [(rows + 2, cols, depth)] * 2,
        [],
        (right_side, coefficient, a, b),
        small,
    )
    k = lax.ppermute(k, "gy", pairs_from(0, along_y))
    z = lax.ppermute(z, ("gx", "gy"), swaps(along_x, along_y, "gy", 1))

    wide = (cols + 2 * DEEP_C, depth)
    half = (rows // 2, SUB, depth // 2)
    send, *state = call(
        functools.partial(fine_down, along_x, along_y),
        [half, (tall - 2,) + wide, (tall,) + wide, (tall + 1,) + wide]
        + [(tall,) + wide] * 3,
        [(tall + 2,) + wide, (tall,) + wide, (rows, cols, depth)],
        (right_side, coefficient, a, b, z, k),
        small,
    )
    chips = along_y // 2
    parts = [send] + [
        lax.ppermute(send, ("gx", "gy"), at_distance(along_x, along_y, "gy", distance))
        for distance in range(1, chips)
    ]
    shape = (chips * half[0],) + half[1:]
    (line,) = call(line_up, [shape], [], parts, small + 8 * math.prod(shape))
    own = [line] + [
        lax.ppermute(line, ("gx", "gy"), at_distance(along_x, along_y, "gx", distance))
        for distance in range(1, along_x)
    ]
    other = [lax.ppermute(line, "gy", pairs_from(0, along_y)) for line in own]

    rows1, cols1, depth1 = along_x * half[0], along_y * (cols // 2), half[2]
    whole1 = (rows1 + 2 * PAD + 1, cols1 + 2 * MARGIN, depth1)
    rows2, cols2 = rows1 // 2, cols1 // 2
    whole2 = (rows2 + 2, cols2 + 2 * MARGIN, depth1)
    span, broad = half[0] + 2 * PAD, 2 * SUB
    window = (span, broad + 2 * MARGIN, depth1)
    scratch = [whole1] * 7 + [(rows1, cols1, depth1)]
    scratch += [(rows2, cols2, depth1)] + [whole2] * 3
    scratch += [(span // 2 + 2,) + whole1[1:], window, (span, broad, depth1), window]
    scratch += [(span - 4, broad, depth1), ((span - 4) * wide[0], depth1)]
    scratch += [(tall,) + wide, (tall, cols, depth), (tall,) + wide]
    size = sum(4 * math.prod(s) for s in scratch)
    size += 2 * 4 * along_x * line.size + 4 * 8 * tall * wide[0] * wide[1]
    (out,) = call(
        functools.partial(coarse_and_up, along_x, along_y),
        [right_side.shape],
        scratch,
        (*own, *other, *state),
        size + (12 << 20),
    )
    return out


def solution(mesh):
    placed = (P("gx", "gy", None), P("gx", "gy", None))
    return jax.shard_map(
        body, mesh=mesh, in_specs=placed, out_specs=P("gx", "gy", None), check_vma=False
    )
```
